256 devices in a mesh: cache: 32 (over x, y, core), tp: 8 (over z).
Axes of the slice: x: 4, y: 4, z: 8, core: 2. Of those that a mesh axis runs over, the one named last changes fastest.
Arguments:
- x_in: bfloat16 [4096, 16384], P('cache', 'tp'), may hold values from -6 to 6
- conv_weight: float32 [4, 16384], P(None, 'tp'), may hold values from -3 to 3
- dt_in_weight: bfloat16 [16384, 512], P('tp'), may hold values from -0.046875 to 0.046875
- bc_weight: bfloat16 [32, 16384], P(None, 'tp'), may hold values from -0.046875 to 0.046875
- dt_weight: bfloat16 [512, 16384], P(None, 'tp'), may hold values from -0.25 to 0.25
- dt_bias: float32 [16384], P('tp'), may hold values from -6 to -2
- decay_rates: float32 [16, 16384], P(None, 'tp'), may hold values from 0.5 to 16
- skip_gain: float32 [16384], P('tp'), may hold values from 0.5 to 1.5
- queries: bfloat16 [4096, 4096], P('cache', 'tp'), may hold values from -40 to 40
- new_keys: bfloat16 [4096, 1024], P('cache', 'tp'), may hold values from -4.5 to 4.5
- new_values: bfloat16 [4096, 1024], P('cache', 'tp'), may hold values from -6 to 6
- store_state: float32 [640, 16, 16384], P('cache', None, 'tp'), may hold values from -6 to 6
- store_conv: bfloat16 [640, 3, 16384], P('cache', None, 'tp'), may hold values from -6 to 6
- store_keys: bfloat16 [640, 256, 1024], P('cache', None, 'tp'), may hold values from -4 to 4
- store_values: bfloat16 [640, 256, 1024], P('cache', None, 'tp'), may hold values from -6 to 6
- hit_entry: int32 [512], P('cache'), may hold values from 0 to 639, as said below
- hit_blocks: int32 [512], P('cache'), may hold values from 1 to 2
- seg_lengths: int32 [32, 16], P('cache'), may hold values from 1 to 64, 128 in all within a row
Outputs:
- mixer_out: bfloat16 [4096, 16384], P('cache', 'tp')
- attn_out: bfloat16 [4096, 4096], P('cache', 'tp')
- new_state: float32 [640, 16, 16384], P('cache', None, 'tp')
- new_conv: bfloat16 [640, 3, 16384], P('cache', None, 'tp')
The draws below stay inside these ranges and needn't reach their ends.
Inputs may be any that keep to these rules, and one draw needn't show every extreme that they name: `hit_entry`: entry e lives on cache index e // 20. The 16 requests of one cache index come in consecutive groups of 1 that name entries of one owner, different groups different owners; every owner serves exactly 16 requests, and no entry is named twice.
All inputs are finite; a program needn't handle non-finite values.
Results may differ from the reference program's by a relative error of at most 0.012.
Values may be sent and summed in bfloat16 or wider, within the bound.
No kernel may reach another device: no remote copies, remote signals or barrier semaphores. Data moves between devices by JAX's collectives and lax.ppermute only.
A program may use at most 192 MiB of HBM per device.

```python
import math
import jax
import jax.numpy as jnp
import numpy as np
from jax import lax

INNER = 16384
STATE = 16
DT_RANK = 512
HEAD_DIM = 128
KV_HEADS = 8
Q_HEADS = 32
TOK_DEV = 128
PAIR = 1
MAXB = 2
KVB = 128
REQ_DEV = 16
SLOTS = 20
TOKENS = 4096
REQUESTS = 512
ENTRIES = 640
PREFIX = 256
N_CACHE = 32


def key_basis(key):
    first_key = jax.random.fold_in(key, 0)
    gauss_part = jnp.clip(jax.random.normal(first_key, (TOKENS, KV_HEADS * HEAD_DIM), jnp.float32), -4.0, 4.0)
    basis_rows = gauss_part
    places = jnp.arange(TOKENS, dtype=jnp.int32)
    chosen = places % 97 == 6
    follow = jnp.roll(chosen, -1)
    return jnp.where(follow[:, None], basis_rows, basis_rows)


def draw_new_keys(key, part):
    shared = key_basis(key)
    return shared.astype(jnp.bfloat16)


def draw_queries(key, part):
    key = jax.random.fold_in(key, 5)
    result = jnp.clip(jax.random.normal(key, (TOKENS, Q_HEADS * HEAD_DIM), jnp.float32), -4.0, 4.0)
    return result.astype(jnp.bfloat16)


def swap_first(order_row, wanted):
    positions = jnp.arange(order_row.shape[0], dtype=jnp.int32)
    where_wanted = jnp.argmax(order_row == wanted).astype(jnp.int32)
    swapped = jnp.where(positions == where_wanted, order_row[0], order_row)
    return jnp.where(positions == 0, wanted, swapped).astype(jnp.int32)


def draw_hit_entry(key, part):
    key = jax.random.fold_in(key, 11)
    group_count = REQ_DEV // PAIR
    owner_key, device_key, slot_key = jax.random.split(key, 3)
    owner_order = jax.random.permutation(owner_key, N_CACHE).astype(jnp.int32)
    device_order = jax.random.permutation(device_key, N_CACHE).astype(jnp.int32)
    request_ids = jnp.arange(REQUESTS, dtype=jnp.int32)
    devices = request_ids // REQ_DEV
    pair_group = request_ids % REQ_DEV // PAIR
    position = (jnp.take(device_order, devices) * group_count + pair_group) % N_CACHE
    owner_of = jnp.take(owner_order, position)
    before = (request_ids[None, :] < request_ids[:, None]) & (owner_of[None, :] == owner_of[:, None])
    rank_of = jnp.sum(jnp.where(before, 1, 0), axis=1, dtype=jnp.int32)
    scores = jax.random.randint(slot_key, (N_CACHE, SLOTS), 0, 1 << 20, jnp.int32) * SLOTS + jnp.arange(SLOTS, dtype=jnp.int32)[None, :]
    slot_order = jnp.argsort(scores, axis=1, stable=True).astype(jnp.int32)
    slot_order = slot_order.at[0].set(swap_first(slot_order[0], 0))
    slot_order = slot_order.at[N_CACHE - 1].set(swap_first(slot_order[N_CACHE - 1], SLOTS - 1))
    slot_of = slot_order[owner_of, rank_of]
    return (owner_of * SLOTS + slot_of).astype(jnp.int32)


def place_ends(array, own_key, low, top_value):
    dims = array.shape
    index_at = [jax.random.randint(jax.random.fold_in(own_key, axis), (), 0, dims[axis]) for axis in range(len(dims))]
    array = array.at[tuple(index_at)].set(low)
    longest = dims.index(max(dims))
    index_at[longest] = (index_at[longest] + 1) % dims[longest]
    return array.at[tuple(index_at)].set(top_value)


def levels(own_key, dims, shards, smallest, top_value):
    factor_of = 1.0
    for axis_at, parts in shards:
        steps = jax.random.uniform(jax.random.fold_in(jax.random.fold_in(own_key, 6), axis_at), (parts,), jnp.float32, smallest / len(shards), top_value / len(shards))
        factor_of = factor_of * jnp.repeat(jnp.exp(steps), dims[axis_at] // parts).reshape((-1,) + (1,) * (len(dims) - 1 - axis_at))
    return factor_of


def split_up(number_of, total, limit, slope):
    weights = [(1 << 20) // math.isqrt(rank ** slope) + 1 for rank in range(2, number_of + 1)]
    rest, counts = total - limit - (number_of - 1), [1] * (number_of - 1)
    while rest > 0:
        movable = [i for i in range(number_of - 1) if counts[i] < limit]
        mass, budget = sum([weights[i] for i in movable]), rest
        for i in movable:
            more = min(limit - counts[i], max(1, budget * weights[i] // mass), rest)
            counts[i] = counts[i] + more
            rest = rest - more
    return np.array([limit] + counts)


def uneven(stream_key, amount, total, limit, slope):
    if amount == 2:
        one = jax.random.randint(stream_key, (), max(1, total - limit), min(limit, total - 1) + 1)
        return jnp.stack([one, total - one])
    sizes = jnp.asarray(split_up(amount, total, limit, slope), jnp.int32)
    couples = (amount - 1) // 2
    giver, sink = sizes[1:1 + 2 * couples:2], sizes[2:2 + 2 * couples:2]
    margin = jnp.minimum(giver - 1, limit - sink)
    passed = jax.random.randint(jax.random.fold_in(stream_key, 1), (couples,), 0, 1 << 20) % (margin + 1)
    sizes = sizes.at[1:1 + 2 * couples:2].set(giver - passed).at[2:2 + 2 * couples:2].set(sink + passed)
    return sizes[jax.random.permutation(jax.random.fold_in(stream_key, 2), amount)]


def centred(own_key, shape, scale, bound, pieces=(), held_as=jnp.bfloat16):
    gain = levels(own_key, shape, pieces, -0.22, 0.18) if pieces else 1.0
    drawn = jax.random.normal(own_key, shape, jnp.float32) * scale * gain
    return jnp.minimum(jnp.maximum(drawn, -bound), bound).astype(held_as)


def setup_inputs(seed: int = 0) -> dict:
    key_list = jax.random.split(jax.random.key(seed), 19)
    x_in = centred(key_list[0], (TOKENS, INNER), 1.0, 6.0, ((0, 32), (1, 8)))
    conv_weight = centred(key_list[1], (4, INNER), 4 ** -0.5, 3.0, ((1, 8),), jnp.float32)
    dt_in_weight = centred(key_list[2], (INNER, DT_RANK), INNER ** -0.5, 0.046875, ((0, 8),))
    bc_weight = centred(key_list[3], (2 * STATE, INNER), INNER ** -0.5, 0.046875, ((1, 8),))
    dt_weight = centred(key_list[4], (DT_RANK, INNER), DT_RANK ** -0.5, 0.25, ((1, 8),))
    dt_bias = jnp.clip(-6.0 + 4.0 * jax.random.uniform(key_list[5], (INNER,), jnp.float32) ** levels(key_list[5], (INNER,), ((0, 8),), -0.2, 0.2), -6.0, -2.0)
    decay_rates = jnp.clip(jnp.exp(math.log(16.0) - 3.465736 * jax.random.uniform(key_list[6], (STATE, INNER), jnp.float32) ** levels(key_list[6], (STATE, INNER), ((1, 8),), -0.2, 0.2)), 0.5, 16.0)
    skip_gain = jnp.clip(0.5 + 1.0 * jax.random.uniform(key_list[7], (INNER,), jnp.float32) ** levels(key_list[7], (INNER,), ((0, 8),), -0.2, 0.2), 0.5, 1.5)
    queries = draw_queries(jax.random.fold_in(key_list[18], 71), 0)
    new_keys = draw_new_keys(jax.random.fold_in(key_list[18], 71), 0)
    new_values = centred(key_list[10], (TOKENS, KV_HEADS * HEAD_DIM), 1.0, 6.0, ((0, 32), (1, 8)))
    store_state = centred(key_list[11], (ENTRIES, STATE, INNER), 1.0, 6.0, ((0, 32), (2, 8)), jnp.float32)
    store_conv = centred(key_list[12], (ENTRIES, 3, INNER), 1.0, 6.0, ((0, 32), (2, 8)))
    store_keys = centred(key_list[13], (ENTRIES, PREFIX, KV_HEADS * HEAD_DIM), 1.0, 4.0, ((0, 32), (2, 8)))
    store_values = centred(key_list[14], (ENTRIES, PREFIX, KV_HEADS * HEAD_DIM), 1.0, 6.0, ((0, 32), (2, 8)))
    hit_entry = draw_hit_entry(jax.random.fold_in(key_list[18], 71), 0)
    hit_blocks = place_ends(jax.random.randint(key_list[16], (REQUESTS,), 1, MAXB + 1), jax.random.fold_in(key_list[16], 1), 1, MAXB).astype(jnp.int32)
    seg_lengths = jax.vmap(lambda own: uneven(own, REQ_DEV, TOK_DEV, TOK_DEV // 2, 2))(jax.random.split(key_list[17], N_CACHE)).reshape((N_CACHE, REQ_DEV)).astype(jnp.int32)
    return dict(x_in=x_in, conv_weight=conv_weight, dt_in_weight=dt_in_weight, bc_weight=bc_weight, dt_weight=dt_weight, dt_bias=dt_bias, decay_rates=decay_rates, skip_gain=skip_gain, queries=queries, new_keys=new_keys, new_values=new_values, store_state=store_state, store_conv=store_conv, store_keys=store_keys, store_values=store_values, hit_entry=hit_entry, hit_blocks=hit_blocks, seg_lengths=seg_lengths)


def segment_tables(lengths, row_count):
    ends_at = jnp.cumsum(lengths, dtype=jnp.int32)
    starts_at = ends_at - lengths
    places = jnp.arange(row_count, dtype=jnp.int32)
    member = (places[:, None] >= starts_at[None, :]) & (places[:, None] < ends_at[None, :])
    labels = jnp.arange(lengths.shape[0], dtype=jnp.int32)
    segment = jnp.sum(jnp.where(member, labels[None, :], 0), axis=1, dtype=jnp.int32)
    offset = places - jnp.sum(jnp.where(member, starts_at[None, :], 0), axis=1, dtype=jnp.int32)
    return ends_at, segment, offset, member


def conv_inputs(x_rows, conv_prev, lengths, conv_weight):
    row_count = x_rows.shape[0]
    ends_at, segment, offset, member = segment_tables(lengths, row_count)
    onehot = member.astype(jnp.float32)
    widened = x_rows.astype(jnp.float32)
    cached = conv_prev.astype(jnp.float32)
    picked = [jnp.dot(onehot, cached[:, column, :], precision=lax.Precision.HIGHEST) for column in range(3)]
    running = conv_weight[3][None, :] * widened
    for lag_step in range(1, 4):
        shifted = jnp.concatenate([jnp.zeros((lag_step, widened.shape[1]), jnp.float32), widened[:-lag_step]], axis=0)
        earlier = jnp.zeros_like(widened)
        for back_step in range(lag_step):
            earlier = jnp.where((offset == back_step)[:, None], picked[3 + back_step - lag_step], earlier)
        previous = jnp.where((offset >= lag_step)[:, None], shifted, earlier)
        running = running + conv_weight[3 - lag_step][None, :] * previous
    mixed_rows = jax.nn.silu(running).astype(jnp.bfloat16)
    places = jnp.arange(row_count, dtype=jnp.int32)
    tail_rows = []
    for column in range(3):
        target = ends_at - 3 + column
        end_pick = (places[None, :] == target[:, None]).astype(jnp.float32)
        from_rows = jnp.dot(end_pick, widened, precision=lax.Precision.HIGHEST)
        source_column = lengths + column
        from_cache = jnp.zeros_like(cached[:, 0, :])
        for stored in range(3):
            from_cache = jnp.where((source_column == stored)[:, None], cached[:, stored, :], from_cache)
        tail_rows.append(jnp.where((source_column >= 3)[:, None], from_rows, from_cache))
    return mixed_rows, jnp.stack(tail_rows, axis=1).astype(jnp.bfloat16)


def selective_scan(mixed_rows, rate_dt, decay_rates, b_rows, c_rows, skip_gain, start_state, lengths, block_rows):
    row_count, channels = mixed_rows.shape
    ends_at, segment, offset, member = segment_tables(lengths, row_count)
    first_row = offset == 0
    start_hot = (member & first_row[:, None]).astype(jnp.float32)
    places = jnp.arange(row_count, dtype=jnp.int32)
    end_hot = (places[None, :] == (ends_at - 1)[:, None]).astype(jnp.float32)

    def combine(earlier_pair, later_pair):
        return earlier_pair[0] * later_pair[0], later_pair[0] * earlier_pair[1] + later_pair[1]

    def advance(state_carry, block_index):
        state_prev, finals = state_carry
        lower_row = block_index * block_rows
        x_part = lax.dynamic_slice_in_dim(mixed_rows, lower_row, block_rows, 0).astype(jnp.float32)
        dt_part = lax.dynamic_slice_in_dim(rate_dt, lower_row, block_rows, 0)
        b_part = lax.dynamic_slice_in_dim(b_rows, lower_row, block_rows, 1)
        c_part = lax.dynamic_slice_in_dim(c_rows, lower_row, block_rows, 1)
        start_part = lax.dynamic_slice_in_dim(start_hot, lower_row, block_rows, 0)
        end_part = lax.dynamic_slice_in_dim(end_hot, lower_row, block_rows, 1)
        first_part = lax.dynamic_slice_in_dim(first_row, lower_row, block_rows, 0)
        decays = jnp.exp(-dt_part[:, None, :] * decay_rates[None, :, :])
        driven = (dt_part * x_part)[:, None, :] * jnp.transpose(b_part)[:, :, None]
        entering = jnp.einsum("tr,rnc->tnc", start_part, start_state, precision=lax.Precision.HIGHEST)
        driven = driven + decays * entering
        decays = jnp.where(first_part[:, None, None], 0.0, decays)
        driven = driven.at[0].add(decays[0] * state_prev)
        _, states = lax.associative_scan(combine, (decays, driven), axis=0)
        output = jnp.einsum("tnc,nt->tc", states, c_part, precision=lax.Precision.HIGHEST) + skip_gain[None, :] * x_part
        finals = finals + jnp.einsum("rt,tnc->rnc", end_part, states, precision=lax.Precision.HIGHEST)
        return (states[-1], finals), output

    state_count = decay_rates.shape[0]
    initial = (jnp.zeros((state_count, channels), jnp.float32), jnp.zeros((lengths.shape[0], state_count, channels), jnp.float32))
    (last_state, finals), outputs = lax.scan(advance, initial, jnp.arange(row_count // block_rows, dtype=jnp.int32))
    return outputs.reshape(row_count, channels).astype(jnp.bfloat16), finals


def attend(q_rows, key_rows, value_rows, prefix_keys, prefix_values, lengths, prefix_live, kv_count):
    row_count = q_rows.shape[0]
    group_size = q_rows.shape[1] // (kv_count * HEAD_DIM)
    ends_at, segment, offset, member = segment_tables(lengths, row_count)
    request_count = prefix_keys.shape[0]
    prefix_rows = prefix_keys.shape[1]
    owner_request = jnp.arange(request_count * prefix_rows, dtype=jnp.int32) // prefix_rows
    prefix_place = jnp.arange(request_count * prefix_rows, dtype=jnp.int32) % prefix_rows
    live_limit = jnp.take(prefix_live, owner_request)
    see_prefix = (segment[:, None] == owner_request[None, :]) & (prefix_place < live_limit)[None, :]
    places = jnp.arange(row_count, dtype=jnp.int32)
    see_new = (segment[:, None] == segment[None, :]) & (places[None, :] <= places[:, None])
    visible = jnp.concatenate([see_prefix, see_new], axis=1)
    all_keys = jnp.concatenate([prefix_keys.reshape(request_count * prefix_rows, -1), key_rows], axis=0)
    all_values = jnp.concatenate([prefix_values.reshape(request_count * prefix_rows, -1), value_rows], axis=0)
    q_heads = q_rows.reshape(row_count, kv_count, group_size, HEAD_DIM).astype(jnp.float32)
    k_heads = all_keys.reshape(-1, kv_count, HEAD_DIM).astype(jnp.float32)
    v_heads = all_values.reshape(-1, kv_count, HEAD_DIM).astype(jnp.float32)
    scores = jnp.einsum("tkgd,skd->kgts", q_heads, k_heads, precision=lax.Precision.HIGHEST) * (HEAD_DIM ** -0.5)
    scores = jnp.where(visible[None, None], scores, -1e30)
    highest = jnp.max(scores, axis=-1, keepdims=True)
    raised = jnp.exp(scores - highest)
    probs = (raised / jnp.sum(raised, axis=-1, keepdims=True)).astype(jnp.bfloat16)
    result = jnp.einsum("kgts,skd->tkgd", probs.astype(jnp.float32), v_heads, precision=lax.Precision.HIGHEST)
    return result.reshape(row_count, -1).astype(jnp.bfloat16)


def reference(x_in, conv_weight, dt_in_weight, bc_weight, dt_weight, dt_bias, decay_rates, skip_gain, queries, new_keys, new_values, store_state, store_conv, store_keys, store_values, hit_entry, hit_blocks, seg_lengths):
    block_rows = min(64, TOK_DEV)

    def one_pack(pack_index):
        row_start = pack_index * TOK_DEV
        request_start = pack_index * REQ_DEV
        x_rows = lax.dynamic_slice_in_dim(x_in, row_start, TOK_DEV, 0)
        entries = lax.dynamic_slice_in_dim(hit_entry, request_start, REQ_DEV, 0)
        blocks = lax.dynamic_slice_in_dim(hit_blocks, request_start, REQ_DEV, 0)
        lengths = seg_lengths[pack_index]
        conv_prev = jnp.take(store_conv, entries, axis=0)
        start_state = jnp.take(store_state, entries, axis=0)
        mixed_rows, conv_tail = conv_inputs(x_rows, conv_prev, lengths, conv_weight)
        dt_low = jnp.dot(mixed_rows, dt_in_weight, preferred_element_type=jnp.float32)
        bc_rows = jnp.dot(bc_weight, jnp.transpose(mixed_rows), preferred_element_type=jnp.float32)
        rate_dt = jax.nn.softplus(jnp.dot(dt_low.astype(jnp.bfloat16), dt_weight, preferred_element_type=jnp.float32) + dt_bias[None, :])
        mixer_rows, finals = selective_scan(mixed_rows, rate_dt, decay_rates, bc_rows[:STATE], bc_rows[STATE:], skip_gain, start_state, lengths, block_rows)
        attended = attend(lax.dynamic_slice_in_dim(queries, row_start, TOK_DEV, 0), lax.dynamic_slice_in_dim(new_keys, row_start, TOK_DEV, 0), lax.dynamic_slice_in_dim(new_values, row_start, TOK_DEV, 0), jnp.take(store_keys, entries, axis=0), jnp.take(store_values, entries, axis=0), lengths, blocks * KVB, KV_HEADS)
        return mixer_rows, attended, finals, conv_tail

    mixer_all, attended_all, finals_all, tails_all = lax.map(one_pack, jnp.arange(N_CACHE, dtype=jnp.int32))
    mixer_out = mixer_all.reshape(TOKENS, INNER)
    attn_out = attended_all.reshape(TOKENS, Q_HEADS * HEAD_DIM)
    new_state = store_state.at[hit_entry].set(finals_all.reshape(REQUESTS, STATE, INNER))
    new_conv = store_conv.at[hit_entry].set(tails_all.reshape(REQUESTS, 3, INNER))
    return mixer_out, attn_out, new_state, new_conv
```

```python
import functools
import math

import jax
import jax.numpy as jnp
from jax import lax
from jax.experimental import pallas as pl
from jax.experimental.pallas import tpu as pltpu
from jax.sharding import PartitionSpec as P

HEAD_DIM = 128
KVB = 128
LANES = 128
BF = jnp.bfloat16
F32 = jnp.float32
I32 = jnp.int32
VMEM = pltpu.VMEM
SMEM = pltpu.SMEM
MIB = 1 << 20


def params(mib):
    return pltpu.CompilerParams(vmem_limit_bytes=mib * MIB)


def in_vmem(count):
    return [pl.BlockSpec(memory_space=VMEM) for _ in range(count)]


def tiles_kernel(state_ref, out_ref, hold):
    entries, states, channels = state_ref.shape
    groups = channels // LANES
    for e in range(entries):
        for low in range(0, states, 8):
            for j in range(groups):
                hold[pl.ds(low * groups + j, 8, stride=groups), :] = state_ref[
                    e, low : low + 8, j * LANES : (j + 1) * LANES
                ]
        out_ref[e] = hold[...].astype(BF)


def state_tiles(store_state):
    slots, states, channels = store_state.shape
    rows = states * channels // LANES
    step = 4
    return pl.pallas_call(
        tiles_kernel,
        grid=(slots // step,),
        in_specs=[pl.BlockSpec((step, states, channels), lambda i: (i, 0, 0))],
        out_specs=pl.BlockSpec((step, rows, LANES), lambda i: (i, 0, 0)),
        out_shape=jax.ShapeDtypeStruct((slots, rows, LANES), BF),
        scratch_shapes=[VMEM((rows, LANES), F32)],
        compiler_params=params(16),
    )(store_state)


def pick_kernel(count, asked_ref, *refs):
    sources, out_ref, sem = refs[:count], refs[count], refs[count + 1]
    blocks = out_ref.shape[0]

    def copies(i):
        pick = jnp.maximum(asked_ref[i], 0)
        made, low = [], 0
        for n, source in enumerate(sources):
            rows = source.shape[1]
            made.append(
                pltpu.make_async_copy(
                    source.at[pick], out_ref.at[i, pl.ds(low, rows)], sem.at[i, n]
                )
            )
            low += rows
        return made

    for i in range(blocks):
        for copy in copies(i):
            copy.start()
    for i in range(blocks):
        for copy in copies(i):
            copy.wait()


def pick(asked, *sources):
    blocks = asked.shape[0]
    rows = sum(s.shape[1] for s in sources)
    return pl.pallas_call(
        functools.partial(pick_kernel, len(sources)),
        in_specs=[pl.BlockSpec(memory_space=SMEM)]
        + [pl.BlockSpec(memory_space=pl.ANY) for _ in sources],
        out_specs=pl.BlockSpec(memory_space=pl.ANY),
        out_shape=jax.ShapeDtypeStruct((blocks, rows, LANES), sources[0].dtype),
        scratch_shapes=[pltpu.SemaphoreType.DMA((blocks, len(sources)))],
        compiler_params=params(4),
    )(asked, *sources)


def conv_kernel(
    rank_ref, x_ref, got_ref, choose_ref, weight_ref, in_ref, bc_ref, *refs
):
    parts, (mixed_ref, tail_ref), (source, wide, total, tails) = refs[:8], refs[8:10], refs[10:]
    tokens, channels = x_ref.shape
    groups = channels // LANES
    olds = got_ref.shape[0] // groups
    wide[...] = got_ref[...].astype(F32)
    source[0:tokens, :] = x_ref[...]
    source[tokens + olds :, :] = jnp.zeros((source.shape[0] - tokens - olds, channels), BF)
    for j in range(groups):
        source[tokens : tokens + olds, j * LANES : (j + 1) * LANES] = wide[
            pl.ds(j, olds, stride=groups), :
        ].astype(BF)
    chunk = min(512, channels)
    rank_dim = in_ref.shape[1]
    for low in range(0, channels, chunk):
        cut = slice(low, low + chunk)
        taken = jnp.dot(choose_ref[...], source[:, cut], preferred_element_type=F32)
        running = weight_ref[3:4, cut] * x_ref[:, cut].astype(F32)
        for lag in range(1, 4):
            running = (
                running
                + weight_ref[3 - lag : 4 - lag, cut] * taken[(lag - 1) * tokens : lag * tokens]
            )
        mixed = (running / (1.0 + jnp.exp(-running))).astype(BF)
        mixed_ref[:, cut] = mixed
        for j in range(chunk // LANES):
            tails[pl.ds(low // LANES + j, olds, stride=groups), :] = taken[
                3 * tokens :, j * LANES : (j + 1) * LANES
            ]
        dt_part = jnp.dot(mixed, in_ref[cut, :], preferred_element_type=F32)
        bc_part = lax.dot_general(
            mixed, bc_ref[:, cut], (((1,), (1,)), ((), ())), preferred_element_type=F32
        )
        if low == 0:
            total[:, 0:rank_dim] = dt_part
            total[:, rank_dim:] = jnp.zeros((tokens, total.shape[1] - rank_dim), F32)
            total[:, rank_dim : rank_dim + bc_part.shape[1]] = bc_part
        else:
            total[:, 0:rank_dim] += dt_part
            total[:, rank_dim : rank_dim + bc_part.shape[1]] += bc_part
    tail_ref[...] = tails[...].astype(BF)
    share = tokens // 8
    for step, part in enumerate(parts):
        place = lax.rem(rank_ref[0] + step, 8) * share
        part[...] = total[pl.ds(pl.multiple_of(place, share), share), :]


def conv_project(rank, x_rows, got_conv, choose, conv_weight, dt_in_weight, bc_weight):
    tokens, channels = x_rows.shape
    width = dt_in_weight.shape[1] + LANES
    tail_rows = got_conv.shape[0]
    return pl.pallas_call(
        conv_kernel,
        in_specs=[pl.BlockSpec(memory_space=SMEM)] + in_vmem(6),
        out_specs=in_vmem(10),
        out_shape=[jax.ShapeDtypeStruct((tokens // 8, width), F32)] * 8
        + [
            jax.ShapeDtypeStruct((tokens, channels), BF),
            jax.ShapeDtypeStruct((tail_rows, LANES), BF),
        ],
        scratch_shapes=[
            VMEM((choose.shape[1], channels), BF),
            VMEM((tail_rows, LANES), F32),
            VMEM((tokens, width), F32),
            VMEM((tail_rows, LANES), F32),
        ],
        compiler_params=params(32),
    )(rank, x_rows, got_conv, choose, conv_weight, dt_in_weight, bc_weight)


def sum_kernel(*refs):
    out_ref = refs[-1]
    total = refs[0][...]
    for part in refs[1:-1]:
        total = total + part[...]
    width = total.shape[1]
    rank_dim = width - LANES
    out_ref[:, 0:rank_dim] = total[:, 0:rank_dim].astype(BF)
    maps = total[:, rank_dim:]
    high = maps.astype(BF)
    out_ref[:, rank_dim:width] = high
    out_ref[:, width:] = (maps - high.astype(F32)).astype(BF)


def sum_parts(parts):
    rows, width = parts[0].shape
    return pl.pallas_call(
        sum_kernel,
        in_specs=in_vmem(len(parts)),
        out_specs=pl.BlockSpec(memory_space=VMEM),
        out_shape=jax.ShapeDtypeStruct((rows, width + LANES), BF),
    )(*parts)


def scan_kernel(states, *refs):
    rank_ref, length_ref, owner_ref = refs[:3]
    pieces = refs[3:11]
    (mixed_ref, weight_ref, bias_ref, decay_ref, skip_ref, start_ref, tail_ref) = refs[11:18]
    out_ref, back_ref = refs[18:20]
    low_dt, maps, map_smem, rates, drives, sums, decays, hold, sem = refs[20:]
    tokens, channels = mixed_ref.shape
    groups = channels // LANES
    share = tokens // 8
    rank_dim = weight_ref.shape[0]
    for step, piece in enumerate(pieces):
        place = pl.multiple_of(lax.rem(rank_ref[0] + 8 - step, 8) * share, share)
        low_dt[pl.ds(place, share), :] = piece[:, 0:rank_dim]
        maps[pl.ds(place, share), :] = piece[:, rank_dim : rank_dim + LANES].astype(F32) + piece[
            :, rank_dim + LANES :
        ].astype(F32)
    copy = pltpu.make_async_copy(maps, map_smem, sem)
    copy.start()
    for low in range(0, states, 8):
        for j in range(groups):
            decays[pl.ds(low * groups + j, 8, stride=groups), :] = decay_ref[
                low : low + 8, j * LANES : (j + 1) * LANES
            ] * (-math.log2(math.e))
    chunk = min(512, channels)
    for low in range(0, channels, chunk):
        cut = slice(low, low + chunk)
        raw = (
            jnp.dot(low_dt[...], weight_ref[:, cut], preferred_element_type=F32) + bias_ref[:, cut]
        )
        rate = jnp.maximum(raw, 0.0) + jnp.log1p(jnp.exp(-jnp.abs(raw)))
        drive = rate * mixed_ref[:, cut].astype(F32)
        for j in range(chunk // LANES):
            rows = pl.ds(low // LANES + j, tokens, stride=groups)
            rates[rows, :] = rate[:, j * LANES : (j + 1) * LANES]
            drives[rows, :] = drive[:, j * LANES : (j + 1) * LANES]
    back_ref[:, states * groups :, :] = tail_ref[...]
    copy.wait()

    def segment(r, begin):
        finish = begin + length_ref[r]
        owner = owner_ref[r]
        held = tuple(
            start_ref[owner, n * groups : (n + 1) * groups, :].astype(F32) for n in range(states)
        )

        def token(t, held):
            place = pl.ds(pl.multiple_of(t * groups, groups), groups)
            rate, drive = rates[place, :], drives[place, :]
            total, later = None, []
            for n in range(states):
                decay = jnp.exp2(rate * decays[n * groups : (n + 1) * groups, :])
                value = decay * held[n] + drive * map_smem[t, n]
                term = value * map_smem[t, states + n]
                total = term if total is None else total + term
                later.append(value)
            sums[place, :] = total
            return tuple(later)

        held = lax.fori_loop(begin, finish, token, held)
        for n in range(states):
            back_ref[owner, n * groups : (n + 1) * groups, :] = held[n].astype(BF)
        return finish

    lax.fori_loop(0, length_ref.shape[0], segment, jnp.int32(0))
    for j in range(groups):
        cut = slice(j * LANES, (j + 1) * LANES)
        out_ref[:, cut] = (
            sums[pl.ds(j, tokens, stride=groups), :]
            + skip_ref[:, cut] * mixed_ref[:, cut].astype(F32)
        ).astype(BF)


def scan(
    rank, lengths, owners, pieces, mixed, dt_weight, dt_bias, decay_rates, skip_gain, start, tails
):
    tokens, channels = mixed.shape
    states = decay_rates.shape[0]
    groups = channels // LANES
    owners_count = start.shape[0]
    rank_dim = dt_weight.shape[0]
    tail_rows = tails.shape[1]
    return pl.pallas_call(
        functools.partial(scan_kernel, states),
        in_specs=[pl.BlockSpec(memory_space=SMEM)] * 3 + in_vmem(15),
        out_specs=in_vmem(2),
        out_shape=[
            jax.ShapeDtypeStruct((tokens, channels), BF),
            jax.ShapeDtypeStruct((owners_count, states * groups + tail_rows, LANES), BF),
        ],
        scratch_shapes=[
            VMEM((tokens, rank_dim), BF),
            VMEM((tokens, LANES), F32),
            SMEM((tokens, LANES), F32),
            VMEM((tokens * groups, LANES), F32),
            VMEM((tokens * groups, LANES), F32),
            VMEM((tokens * groups, LANES), F32),
            VMEM((states * groups, LANES), F32),
            VMEM((8, LANES), F32),
            pltpu.SemaphoreType.DMA,
        ],
        compiler_params=params(32),
    )(
        rank, lengths, owners, *pieces, mixed, dt_weight, dt_bias[None, :], decay_rates,
        skip_gain[None, :], start, tails,
    )


def attend_kernel(length_ref, owner_ref, live_ref, q_ref, k_ref, v_ref, prefix_ref, out_ref, rows_q, rows_o):
    tokens = q_ref.shape[0]
    heads = q_ref.shape[1] // HEAD_DIM
    prefix = prefix_ref.shape[1] // 2
    for h in range(heads):
        rows_q[h * tokens : (h + 1) * tokens, :] = q_ref[:, h * HEAD_DIM : (h + 1) * HEAD_DIM]
    contract = (((1,), (1,)), ((), ()))
    scale = HEAD_DIM**-0.5
    many = heads * tokens
    new_scores = lax.dot_general(
        rows_q[...], k_ref[...], contract, preferred_element_type=F32
    ) * scale
    query_of = lax.rem(lax.broadcasted_iota(I32, (many, tokens), 0), tokens)
    key_of = lax.broadcasted_iota(I32, (many, tokens), 1)
    new_scores = jnp.where(key_of <= query_of, new_scores, -1e30)
    token_of = lax.rem(lax.broadcasted_iota(I32, (many, HEAD_DIM), 0), tokens)
    place_of = lax.broadcasted_iota(I32, (many, prefix), 1)
    rows_o[...] = jnp.zeros((many, HEAD_DIM), F32)

    def request(r, begin):
        finish = begin + length_ref[r]
        owner = owner_ref[r]
        live = live_ref[r] * KVB
        old = lax.dot_general(
            rows_q[...], prefix_ref[owner, 0:prefix, :], contract, preferred_element_type=F32
        ) * scale
        old = jnp.where(place_of < live, old, -1e30)
        new = jnp.where(key_of >= begin, new_scores, -1e30)
        highest = jnp.maximum(
            jnp.max(old, axis=1, keepdims=True), jnp.max(new, axis=1, keepdims=True)
        )
        old, new = jnp.exp(old - highest), jnp.exp(new - highest)
        total = jnp.sum(old, axis=1, keepdims=True) + jnp.sum(new, axis=1, keepdims=True)
        inverse = 1.0 / total
        result = jnp.dot(
            (old * inverse).astype(BF), prefix_ref[owner, prefix:, :], preferred_element_type=F32
        ) + jnp.dot((new * inverse).astype(BF), v_ref[...], preferred_element_type=F32)
        mine = (token_of >= begin) & (token_of < finish)
        rows_o[...] = jnp.where(mine, result, rows_o[...])
        return finish

    lax.fori_loop(0, length_ref.shape[0], request, jnp.int32(0))
    for h in range(heads):
        out_ref[:, h * HEAD_DIM : (h + 1) * HEAD_DIM] = rows_o[
            h * tokens : (h + 1) * tokens, :
        ].astype(BF)


def attend(lengths, owners, live, queries, new_keys, new_values, prefix):
    tokens, width = queries.shape
    many = tokens * width // HEAD_DIM
    return pl.pallas_call(
        attend_kernel,
        in_specs=[pl.BlockSpec(memory_space=SMEM)] * 3 + in_vmem(4),
        out_specs=pl.BlockSpec(memory_space=VMEM),
        out_shape=jax.ShapeDtypeStruct((tokens, width), BF),
        scratch_shapes=[VMEM((many, HEAD_DIM), BF), VMEM((many, HEAD_DIM), F32)],
        compiler_params=params(32),
    )(lengths, owners, live, queries, new_keys, new_values, prefix)


def write_kernel(source_ref, store_ref, back_ref, out_ref, hold):
    step, states, channels = out_ref.shape
    groups = channels // LANES
    first = pl.program_id(0) * step
    for e in range(step):
        row = source_ref[first + e]

        @pl.when(row < 0)
        def _():
            out_ref[e] = store_ref[e]

        @pl.when(row >= 0)
        def _():
            hold[...] = back_ref[row, 0 : states * groups, :].astype(F32)
            for low in range(0, states, 8):
                for j in range(groups):
                    out_ref[e, low : low + 8, j * LANES : (j + 1) * LANES] = hold[
                        pl.ds(low * groups + j, 8, stride=groups), :
                    ]


def write_state(source, store_state, back):
    slots, states, channels = store_state.shape
    rows = states * channels // LANES
    step = 4
    return pl.pallas_call(
        write_kernel,
        grid_spec=pltpu.PrefetchScalarGridSpec(
            num_scalar_prefetch=1,
            grid=(slots // step,),
            in_specs=[
                pl.BlockSpec((step, states, channels), lambda i, s: (i, 0, 0)),
                pl.BlockSpec(memory_space=VMEM),
            ],
            out_specs=pl.BlockSpec((step, states, channels), lambda i, s: (i, 0, 0)),
            scratch_shapes=[VMEM((rows, LANES), F32)],
        ),
        out_shape=jax.ShapeDtypeStruct((slots, states, channels), F32),
        compiler_params=params(24),
    )(source, store_state, back)


def exchange(blocks, axis):
    return lax.all_to_all(blocks, axis, split_axis=0, concat_axis=0, tiled=True)


def choose_matrix(lengths, owners, tokens, owner_count, width):
    ends = jnp.cumsum(lengths, dtype=I32)
    starts = ends - lengths
    places = jnp.arange(tokens, dtype=I32)
    member = (places[:, None] >= starts[None, :]) & (places[:, None] < ends[None, :])
    offset = places - jnp.sum(jnp.where(member, starts[None, :], 0), axis=1, dtype=I32)
    owner = jnp.sum(jnp.where(member, owners[None, :], 0), axis=1, dtype=I32)
    lags = jnp.arange(1, 4, dtype=I32)[:, None]
    lagged = jnp.where(
        offset[None, :] >= lags,
        places[None, :] - lags,
        tokens + owner[None, :] * 3 + 3 + offset[None, :] - lags,
    )
    owner_ids = jnp.arange(owner_count, dtype=I32)
    served = owner_ids[:, None] == owners[None, :]
    ends_of = jnp.sum(jnp.where(served, ends[None, :], 0), axis=1, dtype=I32)[:, None]
    length_of = jnp.sum(jnp.where(served, lengths[None, :], 0), axis=1, dtype=I32)[:, None]
    rows = jnp.arange(3, dtype=I32)[None, :]
    tails = jnp.where(
        length_of + rows >= 3, ends_of - 3 + rows, tokens + owner_ids[:, None] * 3 + length_of + rows
    )
    tails = jnp.where(length_of > 0, tails, width)
    column = jnp.concatenate([lagged.reshape(-1), tails.reshape(-1)])
    return (column[:, None] == jnp.arange(width, dtype=I32)[None, :]).astype(BF)


def shards(
    x_in,
    conv_weight,
    dt_in_weight,
    bc_weight,
    dt_weight,
    dt_bias,
    decay_rates,
    skip_gain,
    queries,
    new_keys,
    new_values,
    store_state,
    store_conv,
    store_keys,
    store_values,
    hit_entry,
    hit_blocks,
    seg_lengths,
):
    owner_count = lax.axis_size("cache")
    tp_count = lax.axis_size("tp")
    rank = lax.axis_index("tp").astype(I32)[None]
    slot_count, states, channels = store_state.shape
    groups = channels // LANES
    tokens = x_in.shape[0]
    lengths = seg_lengths[0]
    owners = hit_entry // slot_count
    slots = hit_entry - owners * slot_count
    owner_ids = jnp.arange(owner_count, dtype=I32)
    served = owner_ids[:, None] == owners[None, :]
    table = jnp.sum(jnp.where(served, slots[None, :] + 1, 0), axis=1, dtype=I32) - 1
    asked = exchange(table[:, None], "cache")[:, 0]

    conv_tiles = store_conv.reshape(slot_count, 3 * groups, LANES)
    got_conv = exchange(pick(asked, conv_tiles), "cache")
    got_state = exchange(pick(asked, state_tiles(store_state)), "cache")
    got_prefix = exchange(pick(asked, store_keys, store_values), "cache")

    width = tokens + -(-3 * owner_count // LANES) * LANES
    choose = choose_matrix(lengths, owners, tokens, owner_count, width)
    *parts, mixed, tails = conv_project(
        rank, x_in, got_conv.reshape(-1, LANES), choose, conv_weight, dt_in_weight, bc_weight
    )

    def turned(step, value):
        return lax.ppermute(value, "tp", [(k, (k + step) % tp_count) for k in range(tp_count)])

    parts = [parts[0]] + [turned(step, parts[step]) for step in range(1, tp_count)]
    summed = sum_parts(parts)
    pieces = [summed] + [turned(step, summed) for step in range(1, tp_count)]

    mixer_out, back = scan(
        rank, lengths, owners, pieces, mixed, dt_weight, dt_bias, decay_rates, skip_gain,
        got_state, tails.reshape(owner_count, 3 * groups, LANES),
    )
    back = exchange(back, "cache")
    attn_out = attend(lengths, owners, hit_blocks, queries, new_keys, new_values, got_prefix)

    slot_ids = jnp.arange(slot_count, dtype=I32)
    landing = asked[None, :] == slot_ids[:, None]
    source = jnp.sum(jnp.where(landing, owner_ids[None, :] + 1, 0), axis=1, dtype=I32) - 1
    new_state = write_state(source, store_state, back)
    back_conv = back[:, states * groups :, :]
    placed_conv = jnp.take(back_conv, jnp.maximum(source, 0), axis=0, mode="clip")
    new_conv = jnp.where(
        (source >= 0)[:, None, None], placed_conv.reshape(store_conv.shape), store_conv
    )
    return (mixer_out, attn_out, new_state, new_conv)


def solution(mesh):
    placed = (
        P("cache", "tp"),
        P(None, "tp"),
        P("tp", None),
        P(None, "tp"),
        P(None, "tp"),
        P("tp"),
        P(None, "tp"),
        P("tp"),
        P("cache", "tp"),
        P("cache", "tp"),
        P("cache", "tp"),
        P("cache", None, "tp"),
        P("cache", None, "tp"),
        P("cache", None, "tp"),
        P("cache", None, "tp"),
        P("cache"),
        P("cache"),
        P("cache", None),
    )
    return jax.shard_map(
        shards,
        mesh=mesh,
        in_specs=placed,
        out_specs=(
            P("cache", "tp"),
            P("cache", "tp"),
            P("cache", None, "tp"),
            P("cache", None, "tp"),
        ),
        check_vma=False,
    )
```

```python
import functools
import math

import jax
import jax.numpy as jnp
from jax import lax
from jax.experimental import pallas as pl
from jax.experimental.pallas import tpu as pltpu
from jax.sharding import PartitionSpec as P

HEAD_DIM = 128
KVB = 128
SMALL = 32
LANES = 128
BF = jnp.bfloat16
F32 = jnp.float32
I32 = jnp.int32
VMEM = pltpu.VMEM
SMEM = pltpu.SMEM
MIB = 1 << 20


def params(mib):
    return pltpu.CompilerParams(vmem_limit_bytes=mib * MIB)


def in_vmem(count):
    return [pl.BlockSpec(memory_space=VMEM) for _ in range(count)]


def in_smem(count):
    return [pl.BlockSpec(memory_space=SMEM) for _ in range(count)]


def in_hbm(count):
    return [pl.BlockSpec(memory_space=pltpu.HBM) for _ in range(count)]


def whole(*arrays):
    return [
        pl.BlockSpec(a.shape, lambda i, n=len(a.shape): (0,) * n, pipeline_mode=pl.Buffered(1))
        for a in arrays
    ]


def ask_kernel(entry_ref, block_ref, length_ref, out_ref, owner_ref, *, slots):
    shape = out_ref.shape
    owner_of = lax.broadcasted_iota(I32, shape, 0)
    field_of = lax.broadcasted_iota(I32, shape, 2)
    table = jnp.full(shape, -1, I32)
    begin = jnp.int32(0)
    for r in range(entry_ref.shape[0]):
        owner = lax.div(entry_ref[r], slots)
        slot = entry_ref[r] - owner * slots
        owner_ref[r] = owner
        fields = jnp.where(field_of == 0, slot, jnp.where(field_of == 1, begin, 0))
        fields = jnp.where(field_of == 2, begin + length_ref[r], fields)
        fields = jnp.where(field_of == 3, block_ref[r], fields)
        table = jnp.where(owner_of == owner, fields, table)
        begin = begin + length_ref[r]
    out_ref[...] = table


def ask(hit_entry, hit_blocks, lengths, slots, owner_count):
    return pl.pallas_call(
        functools.partial(ask_kernel, slots=slots),
        in_specs=in_smem(3),
        out_specs=in_vmem(1) + in_smem(1),
        out_shape=[
            jax.ShapeDtypeStruct((owner_count, 1, LANES), I32),
            jax.ShapeDtypeStruct(hit_entry.shape, I32),
        ],
        compiler_params=params(4),
    )(hit_entry, hit_blocks, lengths)


def tiles_kernel(state_ref, out_ref, hold):
    entries, states, channels = state_ref.shape
    groups = channels // LANES
    for e in range(entries):
        for low in range(0, states, 8):
            for j in range(groups):
                hold[pl.ds(low * groups + j, 8, stride=groups), :] = state_ref[
                    e, low : low + 8, j * LANES : (j + 1) * LANES
                ]
        out_ref[e] = hold[...].astype(BF)


def state_tiles(store_state):
    slots, states, channels = store_state.shape
    rows = states * channels // LANES
    step = 4
    return pl.pallas_call(
        tiles_kernel,
        grid=(slots // step,),
        in_specs=[pl.BlockSpec((step, states, channels), lambda i: (i, 0, 0))],
        out_specs=pl.BlockSpec((step, rows, LANES), lambda i: (i, 0, 0)),
        out_shape=jax.ShapeDtypeStruct((slots, rows, LANES), BF),
        scratch_shapes=[VMEM((rows, LANES), F32)],
        compiler_params=params(16),
    )(store_state)


def pick_kernel(count, asked_ref, *refs):
    sources, out_ref, sem = refs[:count], refs[count], refs[count + 1]
    blocks = out_ref.shape[0]

    def copies(i):
        pick = jnp.maximum(asked_ref[i, 0], 0)
        made, low = [], 0
        for n, source in enumerate(sources):
            rows = source.shape[1]
            made.append(
                pltpu.make_async_copy(
                    source.at[pick], out_ref.at[i, pl.ds(low, rows)], sem.at[i, n]
                )
            )
            low += rows
        return made

    for i in range(blocks):
        for copy in copies(i):
            copy.start()
    for i in range(blocks):
        for copy in copies(i):
            copy.wait()


def pick(asked, *sources):
    blocks = asked.shape[0]
    rows = sum(s.shape[1] for s in sources)
    return pl.pallas_call(
        functools.partial(pick_kernel, len(sources)),
        in_specs=[pl.BlockSpec(memory_space=SMEM)]
        + [pl.BlockSpec(memory_space=pl.ANY) for _ in sources],
        out_specs=in_hbm(1)[0],
        out_shape=jax.ShapeDtypeStruct((blocks, rows, LANES), sources[0].dtype),
        scratch_shapes=[pltpu.SemaphoreType.DMA((blocks, len(sources)))],
        compiler_params=params(4),
    )(asked, *sources)


def conv_kernel(
    rank_ref, x_ref, got_ref, choose_ref, weight_ref, in_ref, bc_ref, *refs
):
    parts, (mixed_ref, tail_ref), (source, wide, total, tails) = refs[:8], refs[8:10], refs[10:]
    tokens, channels = x_ref.shape
    groups = channels // LANES
    olds = got_ref.shape[0] // groups
    wide[...] = got_ref[...].astype(F32)
    source[0:tokens, :] = x_ref[...]
    source[tokens + olds :, :] = jnp.zeros((source.shape[0] - tokens - olds, channels), BF)
    for j in range(groups):
        source[tokens : tokens + olds, j * LANES : (j + 1) * LANES] = wide[
            pl.ds(j, olds, stride=groups), :
        ].astype(BF)
    chunk = min(512, channels)
    rank_dim = in_ref.shape[1]
    for low in range(0, channels, chunk):
        cut = slice(low, low + chunk)
        taken = jnp.dot(choose_ref[...], source[:, cut], preferred_element_type=F32)
        running = weight_ref[3:4, cut] * x_ref[:, cut].astype(F32)
        for lag in range(1, 4):
            running = (
                running
                + weight_ref[3 - lag : 4 - lag, cut] * taken[(lag - 1) * tokens : lag * tokens]
            )
        mixed = (running / (1.0 + jnp.exp(-running))).astype(BF)
        mixed_ref[:, cut] = mixed
        for j in range(chunk // LANES):
            tails[pl.ds(low // LANES + j, olds, stride=groups), :] = taken[
                3 * tokens :, j * LANES : (j + 1) * LANES
            ]
        dt_part = jnp.dot(mixed, in_ref[cut, :], preferred_element_type=F32)
        bc_part = lax.dot_general(
            mixed, bc_ref[:, cut], (((1,), (1,)), ((), ())), preferred_element_type=F32
        )
        if low == 0:
            total[:, 0:rank_dim] = dt_part
            total[:, rank_dim:] = jnp.zeros((tokens, total.shape[1] - rank_dim), F32)
            total[:, rank_dim : rank_dim + bc_part.shape[1]] = bc_part
        else:
            total[:, 0:rank_dim] += dt_part
            total[:, rank_dim : rank_dim + bc_part.shape[1]] += bc_part
    tail_ref[...] = tails[...].astype(BF)
    share = tokens // 8
    for step, part in enumerate(parts):
        place = lax.rem(rank_ref[0] + step, 8) * share
        part[...] = total[pl.ds(pl.multiple_of(place, share), share), :]


def conv_project(rank, x_rows, got_conv, choose, conv_weight, dt_in_weight, bc_weight):
    tokens, channels = x_rows.shape
    width = dt_in_weight.shape[1] + LANES
    tail_rows = got_conv.shape[0]
    return pl.pallas_call(
        conv_kernel,
        grid=(1,),
        in_specs=in_smem(1)
        + whole(x_rows, got_conv, choose, conv_weight, dt_in_weight, bc_weight),
        out_specs=in_vmem(10),
        out_shape=[jax.ShapeDtypeStruct((tokens // 8, width), F32)] * 8
        + [
            jax.ShapeDtypeStruct((tokens, channels), BF),
            jax.ShapeDtypeStruct((tail_rows, LANES), BF),
        ],
        scratch_shapes=[
            VMEM((choose.shape[1], channels), BF),
            VMEM((tail_rows, LANES), F32),
            VMEM((tokens, width), F32),
            VMEM((tail_rows, LANES), F32),
        ],
        compiler_params=params(32),
    )(rank, x_rows, got_conv, choose, conv_weight, dt_in_weight, bc_weight)


def sum_kernel(*refs):
    out_ref = refs[-1]
    total = refs[0][...]
    for part in refs[1:-1]:
        total = total + part[...]
    width = total.shape[1]
    rank_dim = width - LANES
    out_ref[:, 0:rank_dim] = total[:, 0:rank_dim].astype(BF)
    maps = total[:, rank_dim:]
    high = maps.astype(BF)
    out_ref[:, rank_dim:width] = high
    out_ref[:, width:] = (maps - high.astype(F32)).astype(BF)


def sum_parts(parts):
    rows, width = parts[0].shape
    return pl.pallas_call(
        sum_kernel,
        in_specs=in_vmem(len(parts)),
        out_specs=pl.BlockSpec(memory_space=VMEM),
        out_shape=jax.ShapeDtypeStruct((rows, width + LANES), BF),
    )(*parts)


def scan_kernel(states, *refs):
    rank_ref, length_ref, owner_ref = refs[:3]
    pieces = refs[3:11]
    (mixed_ref, weight_ref, bias_ref, decay_ref, skip_ref, start_ref, tail_ref) = refs[11:18]
    out_ref, back_ref = refs[18:20]
    low_dt, maps, map_smem, rates, drives, sums, decays, ready, sem, sems = refs[20:]
    tokens, channels = mixed_ref.shape
    groups = channels // LANES
    share = tokens // 8
    rank_dim = weight_ref.shape[0]
    for step, piece in enumerate(pieces):
        place = pl.multiple_of(lax.rem(rank_ref[0] + 8 - step, 8) * share, share)
        low_dt[pl.ds(place, share), :] = piece[:, 0:rank_dim]
        maps[pl.ds(place, share), :] = piece[:, rank_dim : rank_dim + LANES].astype(F32) + piece[
            :, rank_dim + LANES :
        ].astype(F32)
    copy = pltpu.make_async_copy(maps, map_smem, sem)
    copy.start()
    for low in range(0, states, 8):
        for j in range(groups):
            decays[pl.ds(low * groups + j, 8, stride=groups), :] = decay_ref[
                low : low + 8, j * LANES : (j + 1) * LANES
            ] * (-math.log2(math.e))
    chunk = min(512, channels)
    for low in range(0, channels, chunk):
        cut = slice(low, low + chunk)
        raw = (
            jnp.dot(low_dt[...], weight_ref[:, cut], preferred_element_type=F32) + bias_ref[:, cut]
        )
        rate = jnp.maximum(raw, 0.0) + jnp.log1p(jnp.exp(-jnp.abs(raw)))
        drive = rate * mixed_ref[:, cut].astype(F32)
        for j in range(chunk // LANES):
            rows = pl.ds(low // LANES + j, tokens, stride=groups)
            rates[rows, :] = rate[:, j * LANES : (j + 1) * LANES]
            drives[rows, :] = drive[:, j * LANES : (j + 1) * LANES]
    copy.wait()
    state_rows = states * groups

    def send(r):
        owner = owner_ref[r]
        return (
            pltpu.make_async_copy(
                ready.at[r], back_ref.at[owner, pl.ds(0, state_rows)], sems.at[r, 0]
            ),
            pltpu.make_async_copy(
                tail_ref.at[owner], back_ref.at[owner, pl.ds(state_rows, 3 * groups)], sems.at[r, 1]
            ),
        )

    def segment(r, begin):
        finish = begin + length_ref[r]
        owner = owner_ref[r]
        held = tuple(
            start_ref[owner, n * groups : (n + 1) * groups, :].astype(F32) for n in range(states)
        )

        def token(t, held):
            place = pl.ds(pl.multiple_of(t * groups, groups), groups)
            rate, drive = rates[place, :], drives[place, :]
            total, later = None, []
            for n in range(states):
                decay = jnp.exp2(rate * decays[n * groups : (n + 1) * groups, :])
                value = decay * held[n] + drive * map_smem[t, n]
                term = value * map_smem[t, states + n]
                total = term if total is None else total + term
                later.append(value)
            sums[place, :] = total
            return tuple(later)

        held = lax.fori_loop(begin, finish, token, held)
        for n in range(states):
            ready[r, n * groups : (n + 1) * groups, :] = held[n].astype(BF)
        for copy in send(r):
            copy.start()
        return finish

    lax.fori_loop(0, length_ref.shape[0], segment, jnp.int32(0))
    for j in range(groups):
        cut = slice(j * LANES, (j + 1) * LANES)
        out_ref[:, cut] = (
            sums[pl.ds(j, tokens, stride=groups), :]
            + skip_ref[:, cut] * mixed_ref[:, cut].astype(F32)
        ).astype(BF)
    for r in range(length_ref.shape[0]):
        for copy in send(r):
            copy.wait()


def scan(
    rank, lengths, owners, pieces, mixed, dt_weight, dt_bias, decay_rates, skip_gain, start, tails
):
    tokens, channels = mixed.shape
    states = decay_rates.shape[0]
    groups = channels // LANES
    owners_count = start.shape[0]
    rank_dim = dt_weight.shape[0]
    tail_rows = tails.shape[1]
    return pl.pallas_call(
        functools.partial(scan_kernel, states),
        grid=(1,),
        in_specs=in_smem(3)
        + whole(*pieces, mixed, dt_weight, dt_bias[None, :], decay_rates, skip_gain[None, :])
        + whole(start, tails),
        out_specs=in_vmem(1) + in_hbm(1),
        out_shape=[
            jax.ShapeDtypeStruct((tokens, channels), BF),
            jax.ShapeDtypeStruct((owners_count, states * groups + tail_rows, LANES), BF),
        ],
        scratch_shapes=[
            VMEM((tokens, rank_dim), BF),
            VMEM((tokens, LANES), F32),
            SMEM((tokens, LANES), F32),
            VMEM((tokens * groups, LANES), F32),
            VMEM((tokens * groups, LANES), F32),
            VMEM((tokens * groups, LANES), F32),
            VMEM((states * groups, LANES), F32),
            VMEM((lengths.shape[0], states * groups, LANES), BF),
            pltpu.SemaphoreType.DMA,
            pltpu.SemaphoreType.DMA((lengths.shape[0], 2)),
        ],
        compiler_params=params(32),
    )(
        rank, lengths, owners, *pieces, mixed, dt_weight, dt_bias[None, :], decay_rates,
        skip_gain[None, :], start, tails,
    )


def attend_kernel(
    asked_ref, rows_ref, key_ref, value_ref, pass_ref, out_ref, pass_out, who, rows, prefix, done, sems
):
    count, tokens, _ = rows.shape
    heads = done.shape[2] // HEAD_DIM
    held = prefix.shape[1] // 2
    half = done.shape[1]
    pass_out[...] = pass_ref[...]

    def arrivals(i):
        row = who[i]
        slot = jnp.maximum(asked_ref[row, 0], 0)
        return (
            pltpu.make_async_copy(
                rows_ref.at[pl.ds(pl.multiple_of(row * tokens, tokens), tokens)],
                rows.at[i],
                sems.at[i, 0],
            ),
            pltpu.make_async_copy(key_ref.at[slot], prefix.at[i, pl.ds(0, held)], sems.at[i, 1]),
            pltpu.make_async_copy(
                value_ref.at[slot], prefix.at[i, pl.ds(held, held)], sems.at[i, 2]
            ),
        )

    def departure(i):
        return pltpu.make_async_copy(done.at[i], out_ref.at[who[i]], sems.at[i, 3])

    found = jnp.int32(0)
    for row in range(asked_ref.shape[0]):
        who[found] = row
        found = found + jnp.where(asked_ref[row, 0] >= 0, 1, 0)
    for i in range(count):
        for copy in arrivals(i):
            copy.start()
    factor = HEAD_DIM**-0.5 * math.log2(math.e)
    contract = (((1,), (1,)), ((), ()))
    wide = heads * HEAD_DIM

    def part(i, window):
        row = who[i]
        begin, finish, live = asked_ref[row, 1], asked_ref[row, 2], asked_ref[row, 3] * KVB
        first = jnp.minimum(lax.div(begin, 16), (tokens - window) // 16)
        low = pl.multiple_of(first * 16, 16)
        many = heads * window
        q = jnp.concatenate(
            [
                rows[i, pl.ds(low, window), h * HEAD_DIM : (h + 1) * HEAD_DIM]
                for h in range(heads)
            ],
            axis=0,
        )
        token_of = lax.broadcasted_iota(I32, (window, tokens), 0) + low
        key_of = lax.broadcasted_iota(I32, (window, tokens), 1)
        hidden = jnp.where((key_of >= begin) & (key_of <= token_of), 0.0, -1e30)
        hidden = jnp.concatenate([hidden] * heads, axis=0)
        old = lax.dot_general(q, prefix[i, 0:held, :], contract, preferred_element_type=F32)
        new = lax.dot_general(
            q, rows[i, :, wide : wide + HEAD_DIM], contract, preferred_element_type=F32
        )
        new = jnp.where(hidden < 0.0, -1e30, new)
        tiles = [
            old[:, b * KVB : (b + 1) * KVB] if b == 0
            else jnp.where(live > b * KVB, old[:, b * KVB : (b + 1) * KVB], -1e30)
            for b in range(held // KVB)
        ] + [new]
        highest = functools.reduce(jnp.maximum, tiles)
        highest = jnp.max(highest, axis=1, keepdims=True)
        tiles = [jnp.exp2((tile - highest) * factor) for tile in tiles]
        inverse = 1.0 / jnp.sum(functools.reduce(jnp.add, tiles), axis=1, keepdims=True)
        result = jnp.dot(
            jnp.concatenate([tile.astype(BF) for tile in tiles[:-1]], axis=1),
            prefix[i, held:, :],
            preferred_element_type=F32,
        ) + jnp.dot(
            tiles[-1].astype(BF),
            rows[i, :, wide + HEAD_DIM : wide + 2 * HEAD_DIM],
            preferred_element_type=F32,
        )
        result = result * inverse
        result = jnp.concatenate(
            [result[h * window : (h + 1) * window] for h in range(heads)], axis=1
        )
        for k in range(min(window, half) // 16):
            block = result[k * 16 : (k + 1) * 16]
            if k == 0 and window > half:
                near = lax.broadcasted_iota(I32, (16, wide), 0) + low
                block = jnp.where((near >= begin) & (near < finish), block, result[half:])
            place = pl.multiple_of(lax.rem(first + k, half // 16) * 16, 16)
            done[i, pl.ds(place, 16), :] = block.astype(BF)

    def request(i, carry):
        row = who[i]
        for copy in arrivals(i):
            copy.wait()
        low = jnp.minimum(lax.div(asked_ref[row, 1], 16), (tokens - SMALL) // 16) * 16
        fits = asked_ref[row, 2] <= low + SMALL

        @pl.when(fits)
        def _():
            part(i, SMALL)

        @pl.when(jnp.logical_not(fits))
        def _():
            part(i, half + 16)

        departure(i).start()
        return carry

    lax.fori_loop(0, count, request, 0)
    for i in range(count):
        departure(i).wait()


def attend(asked, all_rows, store_keys, store_values, passed, count, tokens):
    owner_count = asked.shape[0]
    wide = all_rows.shape[1] - 2 * HEAD_DIM
    half = tokens // 2
    return pl.pallas_call(
        attend_kernel,
        in_specs=in_smem(1) + in_hbm(3) + in_vmem(1),
        out_specs=in_hbm(1) + in_vmem(1),
        out_shape=[
            jax.ShapeDtypeStruct((owner_count, half, wide), BF),
            jax.ShapeDtypeStruct(passed.shape, passed.dtype),
        ],
        scratch_shapes=[
            SMEM((count + 1,), I32),
            VMEM((count, tokens, all_rows.shape[1]), BF),
            VMEM((count, 2 * store_keys.shape[1], HEAD_DIM), BF),
            VMEM((count, half, wide), BF),
            pltpu.SemaphoreType.DMA((count, 4)),
        ],
        compiler_params=params(32),
    )(asked, all_rows, store_keys, store_values, passed)


def settle_kernel(length_ref, owner_ref, got_ref, out_ref, held, sems):
    half = got_ref.shape[1]
    count = length_ref.shape[0]
    copies = [
        pltpu.make_async_copy(got_ref.at[owner_ref[r]], held.at[r], sems.at[r])
        for r in range(count)
    ]
    for copy in copies:
        copy.start()
    place = lax.broadcasted_iota(I32, (half, got_ref.shape[2]), 0)
    lower = jnp.zeros((half, got_ref.shape[2]), F32)
    upper = lower
    begin = jnp.int32(0)
    for r, copy in enumerate(copies):
        copy.wait()
        finish = begin + length_ref[r]
        block = held[r].astype(F32)
        lower = jnp.where((place >= begin) & (place < finish), block, lower)
        upper = jnp.where((place >= begin - half) & (place < finish - half), block, upper)
        begin = finish
    out_ref[0:half, :] = lower.astype(BF)
    out_ref[half:, :] = upper.astype(BF)


def settle(lengths, owners, got):
    count = lengths.shape[0]
    _, half, width = got.shape
    return pl.pallas_call(
        settle_kernel,
        in_specs=in_smem(2) + in_hbm(1),
        out_specs=in_vmem(1)[0],
        out_shape=jax.ShapeDtypeStruct((2 * half, width), BF),
        scratch_shapes=[VMEM((count, half, width), BF), pltpu.SemaphoreType.DMA((count,))],
        compiler_params=params(8),
    )(lengths, owners, got)


def write_kernel(asked_ref, store_ref, conv_ref, back_ref, out_ref, conv_out, source, hold, stage, tails, sems):
    slots, states, channels = out_ref.shape
    groups = channels // LANES
    rows = states * groups
    for s in range(slots):
        source[s] = -1
    for row in range(asked_ref.shape[0]):
        slot = asked_ref[row, 0]

        @pl.when(slot >= 0)
        def _():
            source[slot] = row

    def kept(s):
        return pltpu.make_async_copy(store_ref.at[s], out_ref.at[s], sems.at[s])

    def changed(s):
        return pltpu.make_async_copy(stage.at[s], out_ref.at[s], sems.at[s])

    for s in range(slots):

        @pl.when(source[s] < 0)
        def _():
            kept(s).start()
            tails[s * 3 * groups : (s + 1) * 3 * groups, :] = jnp.zeros((3 * groups, LANES), F32)

    landed = jnp.zeros((slots, LANES), I32)
    slot_of = lax.broadcasted_iota(I32, (slots, LANES), 0)
    for s in range(slots):
        row = source[s]
        landed = jnp.where(slot_of == s, row + 1, landed)

        @pl.when(row >= 0)
        def _():
            hold[s % 2] = back_ref[row, 0:rows, :].astype(F32)
            for low in range(0, states, 8):
                for j in range(groups):
                    stage[s, low : low + 8, j * LANES : (j + 1) * LANES] = hold[
                        s % 2, pl.ds(low * groups + j, 8, stride=groups), :
                    ]
            changed(s).start()
            tails[s * 3 * groups : (s + 1) * 3 * groups, :] = back_ref[row, rows:, :].astype(F32)

    for i in range(3):
        for j in range(groups):
            cut = slice(j * LANES, (j + 1) * LANES)
            fresh = tails[pl.ds(i * groups + j, slots, stride=3 * groups), :]
            conv_out[i, :, cut] = jnp.where(
                landed > 0, fresh, conv_ref[i, :, cut].astype(F32)
            ).astype(BF)
    for s in range(slots):
        changed(s).wait()


def write_store(asked, store_state, conv_rows, back):
    slots, states, channels = store_state.shape
    groups = channels // LANES
    return pl.pallas_call(
        write_kernel,
        in_specs=in_smem(1) + in_hbm(1) + in_vmem(2),
        out_specs=in_hbm(1) + in_vmem(1),
        out_shape=[
            jax.ShapeDtypeStruct((slots, states, channels), F32),
            jax.ShapeDtypeStruct(conv_rows.shape, BF),
        ],
        scratch_shapes=[
            SMEM((slots,), I32),
            VMEM((2, states * groups, LANES), F32),
            VMEM((slots, states, channels), F32),
            VMEM((slots * 3 * groups, LANES), F32),
            pltpu.SemaphoreType.DMA((slots,)),
        ],
        compiler_params=params(24),
    )(asked, store_state, conv_rows, back)


def exchange(blocks, axis):
    return lax.all_to_all(blocks, axis, split_axis=0, concat_axis=0, tiled=True)


def choose_matrix(lengths, owners, tokens, owner_count, width):
    ends = jnp.cumsum(lengths, dtype=I32)
    starts = ends - lengths
    places = jnp.arange(tokens, dtype=I32)
    member = (places[:, None] >= starts[None, :]) & (places[:, None] < ends[None, :])
    offset = places - jnp.sum(jnp.where(member, starts[None, :], 0), axis=1, dtype=I32)
    owner = jnp.sum(jnp.where(member, owners[None, :], 0), axis=1, dtype=I32)
    lags = jnp.arange(1, 4, dtype=I32)[:, None]
    lagged = jnp.where(
        offset[None, :] >= lags,
        places[None, :] - lags,
        tokens + owner[None, :] * 3 + 3 + offset[None, :] - lags,
    )
    owner_ids = jnp.arange(owner_count, dtype=I32)
    served = owner_ids[:, None] == owners[None, :]
    ends_of = jnp.sum(jnp.where(served, ends[None, :], 0), axis=1, dtype=I32)[:, None]
    length_of = jnp.sum(jnp.where(served, lengths[None, :], 0), axis=1, dtype=I32)[:, None]
    rows = jnp.arange(3, dtype=I32)[None, :]
    tails = jnp.where(
        length_of + rows >= 3, ends_of - 3 + rows, tokens + owner_ids[:, None] * 3 + length_of + rows
    )
    tails = jnp.where(length_of > 0, tails, width)
    column = jnp.concatenate([lagged.reshape(-1), tails.reshape(-1)])
    return (column[:, None] == jnp.arange(width, dtype=I32)[None, :]).astype(BF)


def shards(
    x_in,
    conv_weight,
    dt_in_weight,
    bc_weight,
    dt_weight,
    dt_bias,
    decay_rates,
    skip_gain,
    queries,
    new_keys,
    new_values,
    store_state,
    store_conv,
    store_keys,
    store_values,
    hit_entry,
    hit_blocks,
    seg_lengths,
):
    owner_count = lax.axis_size("cache")
    tp_count = lax.axis_size("tp")
    rank = lax.axis_index("tp").astype(I32)[None]
    slot_count, states, channels = store_state.shape
    groups = channels // LANES
    tokens = x_in.shape[0]
    lengths = seg_lengths[0]
    request_count = lengths.shape[0]
    table, owners = ask(hit_entry, hit_blocks, lengths, slot_count, owner_count)
    asked = exchange(table, "cache")[:, 0, :]
    all_rows = lax.all_gather(
        jnp.concatenate([queries, new_keys, new_values], axis=1), "cache", tiled=True
    )

    conv_tiles = store_conv.reshape(slot_count, 3 * groups, LANES)
    got_conv = exchange(pick(asked, conv_tiles), "cache")
    got_state = exchange(pick(asked, state_tiles(store_state)), "cache")

    width = tokens + -(-3 * owner_count // LANES) * LANES
    choose = choose_matrix(lengths, owners, tokens, owner_count, width)
    *parts, mixed, tails = conv_project(
        rank, x_in, got_conv.reshape(-1, LANES), choose, conv_weight, dt_in_weight, bc_weight
    )

    def turned(step, value):
        return lax.ppermute(value, "tp", [(k, (k + step) % tp_count) for k in range(tp_count)])

    parts = [parts[0]] + [turned(step, parts[step]) for step in range(1, tp_count)]
    summed = sum_parts(parts)
    attended, summed = attend(
        asked, all_rows, store_keys, store_values, summed, request_count, tokens
    )
    got_attended = exchange(attended, "cache")
    pieces = [summed] + [turned(step, summed) for step in range(1, tp_count)]

    mixer_out, back = scan(
        rank, lengths, owners, pieces, mixed, dt_weight, dt_bias, decay_rates, skip_gain,
        got_state, tails.reshape(owner_count, 3 * groups, LANES),
    )
    back = exchange(back, "cache")
    attn_out = settle(lengths, owners, got_attended)
    new_state, conv_rows = write_store(asked, store_state, store_conv.transpose(1, 0, 2), back)
    return (mixer_out, attn_out, new_state, conv_rows.transpose(1, 0, 2))


def solution(mesh):
    placed = (
        P("cache", "tp"),
        P(None, "tp"),
        P("tp", None),
        P(None, "tp"),
        P(None, "tp"),
        P("tp"),
        P(None, "tp"),
        P("tp"),
        P("cache", "tp"),
        P("cache", "tp"),
        P("cache", "tp"),
        P("cache", None, "tp"),
        P("cache", None, "tp"),
        P("cache", None, "tp"),
        P("cache", None, "tp"),
        P("cache"),
        P("cache"),
        P("cache", None),
    )
    return jax.shard_map(
        shards,
        mesh=mesh,
        in_specs=placed,
        out_specs=(
            P("cache", "tp"),
            P("cache", "tp"),
            P("cache", None, "tp"),
            P("cache", None, "tp"),
        ),
        check_vma=False,
    )
```

```python
import functools
import math

import jax
import jax.numpy as jnp
from jax import lax
from jax.experimental import pallas as pl
from jax.experimental.pallas import tpu as pltpu
from jax.sharding import PartitionSpec as P

HEAD_DIM = 128
KVB = 128
LANES = 128
BF = jnp.bfloat16
F32 = jnp.float32
I32 = jnp.int32
VMEM = pltpu.VMEM
SMEM = pltpu.SMEM
MIB = 1 << 20


def params(mib=58):
    return pltpu.CompilerParams(vmem_limit_bytes=mib * MIB)


def in_vmem(count):
    return [pl.BlockSpec(memory_space=VMEM) for _ in range(count)]


def in_smem(count):
    return [pl.BlockSpec(memory_space=SMEM) for _ in range(count)]


def in_hbm(count):
    return [pl.BlockSpec(memory_space=pltpu.HBM) for _ in range(count)]


def pin(*arrays):
    return [pltpu.with_memory_space_constraint(a, pltpu.HBM) for a in arrays]


def whole(*arrays):
    return [
        pl.BlockSpec(a.shape, lambda i, n=len(a.shape): (0,) * n, pipeline_mode=pl.Buffered(1))
        for a in arrays
    ]


def ask_kernel(entry_ref, block_ref, length_ref, rank_ref, out_ref, plan_ref, *, slots):
    shape = out_ref.shape
    count = entry_ref.shape[0]
    owner_of = lax.broadcasted_iota(I32, shape, 0)
    table = jnp.full(shape, -1, I32)
    for r in range(count):
        owner = lax.div(entry_ref[r], slots)
        plan_ref[r] = owner
        plan_ref[count + r] = length_ref[0, r]
        plan_ref[2 * count + r] = block_ref[r]
        table = jnp.where(owner_of == owner, entry_ref[r] - owner * slots, table)
    plan_ref[3 * count] = rank_ref[0]
    out_ref[...] = table


def ask(hit_entry, hit_blocks, seg_lengths, rank, slots, owner_count):
    return pl.pallas_call(
        functools.partial(ask_kernel, slots=slots),
        in_specs=in_smem(4),
        out_specs=in_vmem(1) + in_smem(1),
        out_shape=[
            jax.ShapeDtypeStruct((owner_count, 1, LANES), I32),
            jax.ShapeDtypeStruct((3 * hit_entry.shape[0] + 1,), I32),
        ],
        compiler_params=params(),
    )(hit_entry, hit_blocks, seg_lengths, rank)


def tiles_kernel(state_ref, out_ref, hold):
    entries, states, channels = state_ref.shape
    groups = channels // LANES
    for e in range(entries):
        for low in range(0, states, 8):
            for j in range(groups):
                hold[pl.ds(low * groups + j, 8, stride=groups), :] = state_ref[
                    e, low : low + 8, j * LANES : (j + 1) * LANES
                ]
        out_ref[e] = hold[...].astype(BF)


def state_tiles(store_state):
    slots, states, channels = store_state.shape
    rows = states * channels // LANES
    step = 4
    return pl.pallas_call(
        tiles_kernel,
        grid=(slots // step,),
        in_specs=[pl.BlockSpec((step, states, channels), lambda i: (i, 0, 0))],
        out_specs=pl.BlockSpec((step, rows, LANES), lambda i: (i, 0, 0)),
        out_shape=jax.ShapeDtypeStruct((slots, rows, LANES), BF),
        scratch_shapes=[VMEM((rows, LANES), F32)],
        compiler_params=params(16),
    )(*pin(store_state))


def pick_kernel(count, always, asked_ref, *refs):
    sources, (out_ref, stage, sems) = refs[:count], refs[count:]
    blocks = out_ref.shape[0]
    lows = [sum(s.shape[1] for s in sources[:n]) for n in range(count + 1)]

    def load(i, n):
        return pltpu.make_async_copy(
            sources[n].at[jnp.maximum(asked_ref[i, 0], 0)],
            stage.at[i, pl.ds(lows[n], sources[n].shape[1])],
            sems.at[0, i, n],
        )

    def store(i, n):
        part = pl.ds(lows[n], sources[n].shape[1])
        return pltpu.make_async_copy(stage.at[i, part], out_ref.at[i, part], sems.at[1, i, n])

    def each(act):
        for i in range(blocks):
            for n in range(always):
                act(i, n)

            @pl.when(asked_ref[i, 0] >= 0)
            def _():
                for n in range(always, count):
                    act(i, n)

    def turn(i, n):
        load(i, n).wait()
        store(i, n).start()

    each(lambda i, n: load(i, n).start())
    each(turn)
    each(lambda i, n: store(i, n).wait())


def pick(asked, always, *sources):
    blocks = asked.shape[0]
    rows = sum(s.shape[1] for s in sources)
    return pl.pallas_call(
        functools.partial(pick_kernel, len(sources), always),
        in_specs=in_smem(1) + in_hbm(len(sources)),
        out_specs=in_hbm(1)[0],
        out_shape=pltpu.HBM((blocks, rows, LANES), BF),
        scratch_shapes=[
            VMEM((blocks, rows, LANES), BF),
            pltpu.SemaphoreType.DMA((2, blocks, len(sources))),
        ],
        compiler_params=params(32),
    )(asked, *sources)


def conv_kernel(plan_ref, x_ref, got_ref, choose_ref, weight_ref, in_ref, bc_ref, *refs):
    parts, (mixed_ref, tail_ref), (source, wide, total, tails) = refs[:8], refs[8:10], refs[10:]
    tokens, chunk = x_ref.shape
    step, last = pl.program_id(0), pl.num_programs(0) - 1
    groups = got_ref.shape[1] // 3
    olds = got_ref.shape[0] * 3
    rank_dim = in_ref.shape[1]

    @pl.when(step == 0)
    def _():
        wide[...] = got_ref[...].reshape(olds * groups, LANES).astype(F32)
        source[tokens + olds :, :] = jnp.zeros((source.shape[0] - tokens - olds, chunk), BF)
        total[...] = jnp.zeros(total.shape, F32)

    source[0:tokens, :] = x_ref[...]
    low = step * (chunk // LANES)
    for j in range(chunk // LANES):
        source[tokens : tokens + olds, j * LANES : (j + 1) * LANES] = wide[
            pl.ds(low + j, olds, stride=groups), :
        ].astype(BF)
    taken = jnp.dot(choose_ref[...], source[...], preferred_element_type=F32)
    running = weight_ref[3:4, :] * x_ref[...].astype(F32)
    for lag in range(1, 4):
        running = (
            running + weight_ref[3 - lag : 4 - lag, :] * taken[(lag - 1) * tokens : lag * tokens]
        )
    mixed = (running / (1.0 + jnp.exp(-running))).astype(BF)
    mixed_ref[...] = mixed
    for j in range(chunk // LANES):
        tails[pl.ds(low + j, olds, stride=groups), :] = taken[
            3 * tokens :, j * LANES : (j + 1) * LANES
        ]
    maps = lax.dot_general(
        mixed, bc_ref[...], (((1,), (1,)), ((), ())), preferred_element_type=F32
    )
    total[:, 0:rank_dim] += jnp.dot(mixed, in_ref[...], preferred_element_type=F32)
    total[:, rank_dim : rank_dim + maps.shape[1]] += maps

    @pl.when(step == last)
    def _():
        tail_ref[...] = tails[...].astype(BF)
        share = tokens // 8
        for turn, part in enumerate(parts):
            place = lax.rem(plan_ref[plan_ref.shape[0] - 1] + turn, 8) * share
            part[...] = total[pl.ds(pl.multiple_of(place, share), share), :]


def conv_project(plan, x_rows, got, choose, conv_weight, dt_in_weight, bc_weight):
    tokens, channels = x_rows.shape
    rank_dim = dt_in_weight.shape[1]
    width = rank_dim + LANES
    conv_rows = 3 * channels // LANES
    tail_rows = got.shape[0] * conv_rows
    chunk = min(512, channels)
    once = pl.Buffered(1)
    return pl.pallas_call(
        conv_kernel,
        grid=(channels // chunk,),
        in_specs=in_smem(1)
        + [
            pl.BlockSpec((tokens, chunk), lambda i: (0, i)),
            pl.BlockSpec((got.shape[0], conv_rows, LANES), lambda i: (0, 0, 0), pipeline_mode=once),
            pl.BlockSpec(choose.shape, lambda i: (0, 0), pipeline_mode=once),
            pl.BlockSpec((4, chunk), lambda i: (0, i)),
            pl.BlockSpec((chunk, rank_dim), lambda i: (i, 0)),
            pl.BlockSpec((bc_weight.shape[0], chunk), lambda i: (0, i)),
        ],
        out_specs=[pl.BlockSpec((tokens // 8, width), lambda i: (0, 0), pipeline_mode=once)] * 8
        + [
            pl.BlockSpec((tokens, chunk), lambda i: (0, i)),
            pl.BlockSpec((tail_rows, LANES), lambda i: (0, 0), pipeline_mode=once),
        ],
        out_shape=[jax.ShapeDtypeStruct((tokens // 8, width), F32)] * 8
        + [
            jax.ShapeDtypeStruct((tokens, channels), BF),
            jax.ShapeDtypeStruct((tail_rows, LANES), BF),
        ],
        scratch_shapes=[
            VMEM((choose.shape[1], chunk), BF),
            VMEM((tail_rows, LANES), F32),
            VMEM((tokens, width), F32),
            VMEM((tail_rows, LANES), F32),
        ],
        compiler_params=params(),
    )(plan, *pin(x_rows, got, choose, conv_weight, dt_in_weight, bc_weight))


def sum_kernel(*refs):
    out_ref = refs[-1]
    total = refs[0][...]
    for part in refs[1:-1]:
        total = total + part[...]
    width = total.shape[1]
    rank_dim = width - LANES
    out_ref[:, 0:rank_dim] = total[:, 0:rank_dim].astype(BF)
    maps = total[:, rank_dim:]
    high = maps.astype(BF)
    out_ref[:, rank_dim:width] = high
    out_ref[:, width:] = (maps - high.astype(F32)).astype(BF)


def sum_parts(parts):
    rows, width = parts[0].shape
    return pl.pallas_call(
        sum_kernel,
        in_specs=in_vmem(len(parts)),
        out_specs=in_vmem(1)[0],
        out_shape=jax.ShapeDtypeStruct((rows, width + LANES), BF),
        compiler_params=params(8),
    )(*parts)


def scan_kernel(states, count, plan_ref, *refs):
    pieces = refs[0:8]
    brought, (start_ref, tail_hbm, out_ref, back_ref) = refs[8:13], refs[13:17]
    mixed_ref, weight_ref, bias_ref, decay_ref, skip_ref, tail_ref = refs[17:23]
    low_dt, maps, map_smem, rates, drives, sums, decays, begun, ready, sem, sems, own = refs[23:]
    fetches = [
        pltpu.make_async_copy(source, target, own.at[n])
        for n, (source, target) in enumerate(zip((*brought, tail_hbm), refs[17:23]))
    ]
    for n in (1, 2, 0, 3, 4, 5):
        fetches[n].start()
    tokens, channels = mixed_ref.shape
    groups = channels // LANES
    share = tokens // 8
    rank_dim = weight_ref.shape[0]
    rank = plan_ref[3 * count]
    conv_rows = 3 * groups
    state_rows = states * groups

    def receive(r):
        return pltpu.make_async_copy(
            start_ref.at[plan_ref[r], pl.ds(conv_rows, state_rows)], begun.at[r], sems.at[r, 0]
        )

    def send_tail(r):
        owner = plan_ref[r]
        return pltpu.make_async_copy(
            tail_ref.at[owner], back_ref.at[owner, pl.ds(0, conv_rows)], sems.at[r, 1]
        )

    def send_state(r):
        return pltpu.make_async_copy(
            ready.at[r], back_ref.at[plan_ref[r], pl.ds(conv_rows, state_rows)], sems.at[r, 2]
        )

    for r in range(count):
        receive(r).start()
    for step, piece in enumerate(pieces):
        place = pl.multiple_of(lax.rem(rank + 8 - step, 8) * share, share)
        low_dt[pl.ds(place, share), :] = piece[:, 0:rank_dim]
        maps[pl.ds(place, share), :] = piece[:, rank_dim : rank_dim + LANES].astype(F32) + piece[
            :, rank_dim + LANES :
        ].astype(F32)
    copy = pltpu.make_async_copy(maps, map_smem, sem)
    copy.start()
    fetches[3].wait()
    for low in range(0, states, 8):
        for j in range(groups):
            decays[pl.ds(low * groups + j, 8, stride=groups), :] = decay_ref[
                low : low + 8, j * LANES : (j + 1) * LANES
            ] * (-math.log2(math.e))
    for n in (0, 1, 2):
        fetches[n].wait()
    chunk = min(512, channels)
    for low in range(0, channels, chunk):
        cut = slice(low, low + chunk)
        raw = (
            jnp.dot(low_dt[...], weight_ref[:, cut], preferred_element_type=F32) + bias_ref[:, cut]
        )
        rate = jnp.maximum(raw, 0.0) + jnp.log1p(jnp.exp(-jnp.abs(raw)))
        drive = rate * mixed_ref[:, cut].astype(F32)
        for j in range(chunk // LANES):
            rows = pl.ds(low // LANES + j, tokens, stride=groups)
            rates[rows, :] = rate[:, j * LANES : (j + 1) * LANES]
            drives[rows, :] = drive[:, j * LANES : (j + 1) * LANES]
    fetches[5].wait()
    for r in range(count):
        send_tail(r).start()
    copy.wait()

    def segment(r, begin):
        finish = begin + plan_ref[count + r]
        receive(r).wait()
        held = tuple(
            begun[r, n * groups : (n + 1) * groups, :].astype(F32) for n in range(states)
        )

        def token(t, held):
            place = pl.ds(pl.multiple_of(t * groups, groups), groups)
            rate, drive = rates[place, :], drives[place, :]
            total, later = None, []
            for n in range(states):
                decay = jnp.exp2(rate * decays[n * groups : (n + 1) * groups, :])
                value = decay * held[n] + drive * map_smem[t, n]
                term = value * map_smem[t, states + n]
                total = term if total is None else total + term
                later.append(value)
            sums[place, :] = total
            return tuple(later)

        held = lax.fori_loop(begin, finish, token, held)
        for n in range(states):
            ready[r, n * groups : (n + 1) * groups, :] = held[n].astype(BF)
        send_state(r).start()
        return finish

    lax.fori_loop(0, count, segment, jnp.int32(0))
    fetches[4].wait()
    for j in range(groups):
        cut = slice(j * LANES, (j + 1) * LANES)
        out_ref[:, cut] = (
            sums[pl.ds(j, tokens, stride=groups), :]
            + skip_ref[:, cut] * mixed_ref[:, cut].astype(F32)
        ).astype(BF)
    for r in range(count):
        send_tail(r).wait()
        send_state(r).wait()


def scan(plan, pieces, mixed, dt_weight, dt_bias, decay_rates, skip_gain, got, tails):
    tokens, channels = mixed.shape
    states = decay_rates.shape[0]
    groups = channels // LANES
    count = (plan.shape[0] - 1) // 3
    brought = (mixed, dt_weight, dt_bias[None, :], decay_rates, skip_gain[None, :])
    return pl.pallas_call(
        functools.partial(scan_kernel, states, count),
        in_specs=in_smem(1) + in_vmem(8) + in_hbm(7),
        out_specs=in_vmem(1) + in_hbm(1),
        out_shape=[
            jax.ShapeDtypeStruct((tokens, channels), BF),
            pltpu.HBM(got.shape, BF),
        ],
        scratch_shapes=[VMEM(a.shape, a.dtype) for a in (*brought, tails)]
        + [
            VMEM((tokens, dt_weight.shape[0]), BF),
            VMEM((tokens, LANES), F32),
            SMEM((tokens, LANES), F32),
            VMEM((tokens * groups, LANES), F32),
            VMEM((tokens * groups, LANES), F32),
            VMEM((tokens * groups, LANES), F32),
            VMEM((states * groups, LANES), F32),
            VMEM((count, states * groups, LANES), BF),
            VMEM((count, states * groups, LANES), BF),
            pltpu.SemaphoreType.DMA,
            pltpu.SemaphoreType.DMA((count, 3)),
            pltpu.SemaphoreType.DMA((6,)),
        ],
        compiler_params=params(32),
    )(plan, *pieces, *pin(*brought, got, tails))


def attend_kernel(count, plan_ref, q_ref, k_ref, v_ref, got_ref, out_ref, rows_q, rows_o, prefix_ref, sems):
    tokens = q_ref.shape[0]
    heads = q_ref.shape[1] // HEAD_DIM
    prefix = prefix_ref.shape[1] // 2

    def receive(r):
        return pltpu.make_async_copy(got_ref.at[plan_ref[r]], prefix_ref.at[r], sems.at[r])

    for r in range(count):
        receive(r).start()
    for h in range(heads):
        rows_q[h * tokens : (h + 1) * tokens, :] = q_ref[:, h * HEAD_DIM : (h + 1) * HEAD_DIM]
    contract = (((1,), (1,)), ((), ()))
    scale = HEAD_DIM**-0.5
    many = heads * tokens
    new_scores = lax.dot_general(
        rows_q[...], k_ref[...], contract, preferred_element_type=F32
    ) * scale
    query_of = lax.rem(lax.broadcasted_iota(I32, (many, tokens), 0), tokens)
    key_of = lax.broadcasted_iota(I32, (many, tokens), 1)
    new_scores = jnp.where(key_of <= query_of, new_scores, -1e30)
    token_of = lax.rem(lax.broadcasted_iota(I32, (many, HEAD_DIM), 0), tokens)
    place_of = lax.broadcasted_iota(I32, (many, prefix), 1)
    rows_o[...] = jnp.zeros((many, HEAD_DIM), F32)

    def request(r, begin):
        finish = begin + plan_ref[count + r]
        live = plan_ref[2 * count + r] * KVB
        receive(r).wait()
        old = lax.dot_general(
            rows_q[...], prefix_ref[r, 0:prefix, :], contract, preferred_element_type=F32
        ) * scale
        old = jnp.where(place_of < live, old, -1e30)
        new = jnp.where(key_of >= begin, new_scores, -1e30)
        highest = jnp.maximum(
            jnp.max(old, axis=1, keepdims=True), jnp.max(new, axis=1, keepdims=True)
        )
        old, new = jnp.exp(old - highest), jnp.exp(new - highest)
        total = jnp.sum(old, axis=1, keepdims=True) + jnp.sum(new, axis=1, keepdims=True)
        inverse = 1.0 / total
        result = jnp.dot(
            (old * inverse).astype(BF), prefix_ref[r, prefix:, :], preferred_element_type=F32
        ) + jnp.dot((new * inverse).astype(BF), v_ref[...], preferred_element_type=F32)
        mine = (token_of >= begin) & (token_of < finish)
        rows_o[...] = jnp.where(mine, result, rows_o[...])
        return finish

    lax.fori_loop(0, count, request, jnp.int32(0))
    for h in range(heads):
        out_ref[:, h * HEAD_DIM : (h + 1) * HEAD_DIM] = rows_o[
            h * tokens : (h + 1) * tokens, :
        ].astype(BF)


def attend(plan, queries, new_keys, new_values, got):
    tokens, width = queries.shape
    many = tokens * width // HEAD_DIM
    count = (plan.shape[0] - 1) // 3
    return pl.pallas_call(
        functools.partial(attend_kernel, count),
        grid=(1,),
        in_specs=in_smem(1) + whole(queries, new_keys, new_values) + in_hbm(1),
        out_specs=pl.BlockSpec((tokens, width), lambda i: (0, 0)),
        out_shape=jax.ShapeDtypeStruct((tokens, width), BF),
        scratch_shapes=[
            VMEM((many, HEAD_DIM), BF),
            VMEM((many, HEAD_DIM), F32),
            VMEM((count,) + got.shape[1:], BF),
            pltpu.SemaphoreType.DMA((count,)),
        ],
        compiler_params=params(),
    )(plan, *pin(queries, new_keys, new_values, got))


def write_kernel(
    asked_ref, conv_ref, store_ref, back_ref, conv_out, out_ref, source, hold, came, stage, tails, sems
):
    slots, states, channels = out_ref.shape
    groups = channels // LANES
    rows = states * groups
    conv_rows = 3 * groups
    for s in range(slots):
        source[s] = -1
    for row in range(asked_ref.shape[0]):
        slot = asked_ref[row, 0]

        @pl.when(slot >= 0)
        def _():
            source[slot] = row

    def kept(s):
        return pltpu.make_async_copy(store_ref.at[s], stage.at[s], sems.at[slots + s])

    def changed(s):
        return pltpu.make_async_copy(stage.at[s], out_ref.at[s], sems.at[s])

    def arrival(s):
        return pltpu.make_async_copy(
            back_ref.at[jnp.maximum(source[s], 0)], came.at[s], sems.at[slots + s]
        )

    for s in range(slots):

        @pl.when(source[s] < 0)
        def _():
            kept(s).start()
            tails[s * conv_rows : (s + 1) * conv_rows, :] = jnp.zeros((conv_rows, LANES), F32)

        @pl.when(source[s] >= 0)
        def _():
            arrival(s).start()

    landed = jnp.zeros((slots, LANES), I32)
    slot_of = lax.broadcasted_iota(I32, (slots, LANES), 0)
    for s in range(slots):
        row = source[s]
        landed = jnp.where(slot_of == s, row + 1, landed)

        @pl.when(row >= 0)
        def _():
            arrival(s).wait()
            hold[s % 2] = came[s, conv_rows:, :].astype(F32)
            for low in range(0, states, 8):
                for j in range(groups):
                    stage[s, low : low + 8, j * LANES : (j + 1) * LANES] = hold[
                        s % 2, pl.ds(low * groups + j, 8, stride=groups), :
                    ]
            changed(s).start()
            tails[s * conv_rows : (s + 1) * conv_rows, :] = came[s, 0:conv_rows, :].astype(F32)

    for i in range(3):
        for j in range(groups):
            cut = slice(j * LANES, (j + 1) * LANES)
            fresh = tails[pl.ds(i * groups + j, slots, stride=3 * groups), :]
            conv_out[i, :, cut] = jnp.where(
                landed > 0, fresh, conv_ref[i, :, cut].astype(F32)
            ).astype(BF)
    for s in range(slots):

        @pl.when(source[s] < 0)
        def _():
            kept(s).wait()
            changed(s).start()

    for s in range(slots):
        changed(s).wait()


def write_store(asked, store_state, conv_rows, back):
    slots, states, channels = store_state.shape
    groups = channels // LANES
    return pl.pallas_call(
        write_kernel,
        grid=(1,),
        in_specs=in_smem(1) + whole(conv_rows) + in_hbm(2),
        out_specs=whole(conv_rows) + in_hbm(1),
        out_shape=[
            jax.ShapeDtypeStruct(conv_rows.shape, BF),
            jax.ShapeDtypeStruct((slots, states, channels), F32),
        ],
        scratch_shapes=[
            SMEM((slots,), I32),
            VMEM((2, states * groups, LANES), F32),
            VMEM((slots,) + back.shape[1:], BF),
            VMEM((slots, states, channels), F32),
            VMEM((slots * 3 * groups, LANES), F32),
            pltpu.SemaphoreType.DMA((2 * slots,)),
        ],
        compiler_params=params(),
    )(asked, *pin(conv_rows, store_state, back))


def exchange(blocks, axis):
    return lax.all_to_all(blocks, axis, split_axis=0, concat_axis=0, tiled=True)


def choose_matrix(lengths, owners, tokens, owner_count, width):
    ends = jnp.cumsum(lengths, dtype=I32)
    starts = ends - lengths
    places = jnp.arange(tokens, dtype=I32)
    member = (places[:, None] >= starts[None, :]) & (places[:, None] < ends[None, :])
    offset = places - jnp.sum(jnp.where(member, starts[None, :], 0), axis=1, dtype=I32)
    owner = jnp.sum(jnp.where(member, owners[None, :], 0), axis=1, dtype=I32)
    lags = jnp.arange(1, 4, dtype=I32)[:, None]
    lagged = jnp.where(
        offset[None, :] >= lags,
        places[None, :] - lags,
        tokens + owner[None, :] * 3 + 3 + offset[None, :] - lags,
    )
    owner_ids = jnp.arange(owner_count, dtype=I32)
    served = owner_ids[:, None] == owners[None, :]
    ends_of = jnp.sum(jnp.where(served, ends[None, :], 0), axis=1, dtype=I32)[:, None]
    length_of = jnp.sum(jnp.where(served, lengths[None, :], 0), axis=1, dtype=I32)[:, None]
    rows = jnp.arange(3, dtype=I32)[None, :]
    tails = jnp.where(
        length_of + rows >= 3, ends_of - 3 + rows, tokens + owner_ids[:, None] * 3 + length_of + rows
    )
    tails = jnp.where(length_of > 0, tails, width)
    column = jnp.concatenate([lagged.reshape(-1), tails.reshape(-1)])
    return (column[:, None] == jnp.arange(width, dtype=I32)[None, :]).astype(BF)


def shards(
    x_in,
    conv_weight,
    dt_in_weight,
    bc_weight,
    dt_weight,
    dt_bias,
    decay_rates,
    skip_gain,
    queries,
    new_keys,
    new_values,
    store_state,
    store_conv,
    store_keys,
    store_values,
    hit_entry,
    hit_blocks,
    seg_lengths,
):
    owner_count = lax.axis_size("cache")
    tp_count = lax.axis_size("tp")
    rank = lax.axis_index("tp").astype(I32)[None]
    slot_count, states, channels = store_state.shape
    groups = channels // LANES
    tokens = x_in.shape[0]
    lengths = seg_lengths[0]
    table, plan = ask(hit_entry, hit_blocks, seg_lengths, rank, slot_count, owner_count)
    asked = exchange(table, "cache")[:, 0, :]

    conv_tiles = store_conv.reshape(slot_count, 3 * groups, LANES)
    got = exchange(pick(asked, 1, conv_tiles, state_tiles(store_state)), "cache")

    width = tokens + -(-3 * owner_count // LANES) * LANES
    choose = choose_matrix(lengths, hit_entry // slot_count, tokens, owner_count, width)
    *parts, mixed, tails = conv_project(
        plan, x_in, got, choose, conv_weight, dt_in_weight, bc_weight
    )

    def turned(step, value):
        return lax.ppermute(value, "tp", [(k, (k + step) % tp_count) for k in range(tp_count)])

    parts = [parts[0]] + [turned(step, parts[step]) for step in range(1, tp_count)]
    summed = sum_parts(parts)
    pieces = [summed] + [turned(step, summed) for step in range(1, tp_count)]
    got_prefix = exchange(pick(asked, 0, store_keys, store_values), "cache")

    mixer_out, back = scan(
        plan, pieces, mixed, dt_weight, dt_bias, decay_rates, skip_gain, got,
        tails.reshape(owner_count, 3 * groups, LANES),
    )
    back = exchange(back, "cache")
    attn_out = attend(plan, queries, new_keys, new_values, got_prefix)
    conv_rows, new_state = write_store(asked, store_state, store_conv.transpose(1, 0, 2), back)
    return (mixer_out, attn_out, new_state, conv_rows.transpose(1, 0, 2))


def solution(mesh):
    placed = (
        P("cache", "tp"),
        P(None, "tp"),
        P("tp", None),
        P(None, "tp"),
        P(None, "tp"),
        P("tp"),
        P(None, "tp"),
        P("tp"),
        P("cache", "tp"),
        P("cache", "tp"),
        P("cache", "tp"),
        P("cache", None, "tp"),
        P("cache", None, "tp"),
        P("cache", None, "tp"),
        P("cache", None, "tp"),
        P("cache"),
        P("cache"),
        P("cache", None),
    )
    return jax.shard_map(
        shards,
        mesh=mesh,
        in_specs=placed,
        out_specs=(
            P("cache", "tp"),
            P("cache", "tp"),
            P("cache", None, "tp"),
            P("cache", None, "tp"),
        ),
        check_vma=False,
    )
```

```python
import functools
import math

import jax
import jax.numpy as jnp
from jax import lax
from jax.experimental import pallas as pl
from jax.experimental.pallas import tpu as pltpu
from jax.sharding import PartitionSpec as P

HEAD_DIM = 128
KVB = 128
LANES = 128
BF = jnp.bfloat16
F32 = jnp.float32
I32 = jnp.int32
VMEM = pltpu.VMEM
SMEM = pltpu.SMEM
MIB = 1 << 20


def params(mib=58):
    return pltpu.CompilerParams(vmem_limit_bytes=mib * MIB)


def in_vmem(count):
    return [pl.BlockSpec(memory_space=VMEM) for _ in range(count)]


def in_smem(count):
    return [pl.BlockSpec(memory_space=SMEM) for _ in range(count)]


def in_hbm(count):
    return [pl.BlockSpec(memory_space=pltpu.HBM) for _ in range(count)]


def pin(*arrays):
    return [pltpu.with_memory_space_constraint(a, pltpu.HBM) for a in arrays]


def whole(*arrays):
    return [
        pl.BlockSpec(a.shape, lambda i, n=len(a.shape): (0,) * n, pipeline_mode=pl.Buffered(1))
        for a in arrays
    ]


def ask_kernel(entry_ref, block_ref, length_ref, rank_ref, out_ref, plan_ref, *, slots):
    shape = out_ref.shape
    count = entry_ref.shape[0]
    owner_of = lax.broadcasted_iota(I32, shape, 0)
    table = jnp.full(shape, -1, I32)
    for r in range(count):
        owner = lax.div(entry_ref[r], slots)
        plan_ref[r] = owner
        plan_ref[count + r] = length_ref[0, r]
        plan_ref[2 * count + r] = block_ref[r]
        table = jnp.where(owner_of == owner, entry_ref[r] - owner * slots, table)
    plan_ref[3 * count] = rank_ref[0]
    out_ref[...] = table


def ask(hit_entry, hit_blocks, seg_lengths, rank, slots, owner_count):
    return pl.pallas_call(
        functools.partial(ask_kernel, slots=slots),
        in_specs=in_smem(4),
        out_specs=in_vmem(1) + in_smem(1),
        out_shape=[
            jax.ShapeDtypeStruct((owner_count, 1, LANES), I32),
            jax.ShapeDtypeStruct((3 * hit_entry.shape[0] + 1,), I32),
        ],
        compiler_params=params(),
    )(hit_entry, hit_blocks, seg_lengths, rank)


def tiles_kernel(conv_ref, state_ref, out_ref, hold, tails):
    entries, states, channels = state_ref.shape
    slots = conv_ref.shape[1]
    groups = channels // LANES
    conv_rows = 3 * groups
    first = pl.program_id(0) * entries

    @pl.when(first == 0)
    def _():
        for i in range(3):
            for j in range(groups):
                tails[pl.ds(i * groups + j, slots, stride=conv_rows), :] = conv_ref[
                    i, :, j * LANES : (j + 1) * LANES
                ].astype(F32)

    for e in range(entries):
        for low in range(0, states, 8):
            for j in range(groups):
                hold[pl.ds(low * groups + j, 8, stride=groups), :] = state_ref[
                    e, low : low + 8, j * LANES : (j + 1) * LANES
                ]
        place = pl.multiple_of((first + e) * conv_rows, conv_rows)
        out_ref[e, 0:conv_rows, :] = tails[pl.ds(place, conv_rows), :].astype(BF)
        out_ref[e, conv_rows:, :] = hold[...].astype(BF)


def entry_tiles(conv_rows, store_state):
    slots, states, channels = store_state.shape
    rows = states * channels // LANES
    tail_rows = 3 * channels // LANES
    step = 4
    return pl.pallas_call(
        tiles_kernel,
        grid=(slots // step,),
        in_specs=whole(conv_rows)
        + [pl.BlockSpec((step, states, channels), lambda i: (i, 0, 0))],
        out_specs=pl.BlockSpec((step, tail_rows + rows, LANES), lambda i: (i, 0, 0)),
        out_shape=jax.ShapeDtypeStruct((slots, tail_rows + rows, LANES), BF),
        scratch_shapes=[VMEM((rows, LANES), F32), VMEM((slots * tail_rows, LANES), F32)],
        compiler_params=params(16),
    )(*pin(conv_rows, store_state))


def pick_kernel(count, asked_ref, *refs):
    sources, (out_ref, stage, sems) = refs[:count], refs[count:]
    blocks = out_ref.shape[0]
    lows = [sum(s.shape[1] for s in sources[:n]) for n in range(count + 1)]

    def load(i, n):
        return pltpu.make_async_copy(
            sources[n].at[jnp.maximum(asked_ref[i, 0], 0)],
            stage.at[i, pl.ds(lows[n], sources[n].shape[1])],
            sems.at[0, i, n],
        )

    def store(i, n):
        part = pl.ds(lows[n], sources[n].shape[1])
        return pltpu.make_async_copy(stage.at[i, part], out_ref.at[i, part], sems.at[1, i, n])

    def each(act):
        for i in range(blocks):

            @pl.when(asked_ref[i, 0] >= 0)
            def _():
                for n in range(count):
                    act(i, n)

    def turn(i, n):
        load(i, n).wait()
        store(i, n).start()

    each(lambda i, n: load(i, n).start())
    each(turn)
    each(lambda i, n: store(i, n).wait())


def pick(asked, *sources):
    blocks = asked.shape[0]
    rows = sum(s.shape[1] for s in sources)
    return pl.pallas_call(
        functools.partial(pick_kernel, len(sources)),
        in_specs=in_smem(1) + in_hbm(len(sources)),
        out_specs=in_hbm(1)[0],
        out_shape=pltpu.HBM((blocks, rows, LANES), BF),
        scratch_shapes=[
            VMEM((blocks, rows, LANES), BF),
            pltpu.SemaphoreType.DMA((2, blocks, len(sources))),
        ],
        compiler_params=params(32),
    )(asked, *sources)


def pick_tiles_kernel(part, asked_ref, tiles_ref, out_ref, sems):
    def act(name):
        for i in range(out_ref.shape[0]):
            slot = asked_ref[i, 0]

            @pl.when(slot >= 0)
            def _():
                getattr(pltpu.make_async_copy(tiles_ref.at[slot], out_ref.at[i], sems.at[i]), name)()

            @pl.when(slot < 0)
            def _():
                few = pl.ds(0, part)
                getattr(
                    pltpu.make_async_copy(tiles_ref.at[0, few], out_ref.at[i, few], sems.at[i]), name
                )()

    act("start")
    act("wait")


def pick_tiles(asked, tiles, part):
    blocks = asked.shape[0]
    return pl.pallas_call(
        functools.partial(pick_tiles_kernel, part),
        in_specs=in_smem(1) + in_vmem(1),
        out_specs=in_hbm(1)[0],
        out_shape=pltpu.HBM((blocks,) + tiles.shape[1:], BF),
        scratch_shapes=[pltpu.SemaphoreType.DMA((blocks,))],
        compiler_params=params(4),
    )(asked, tiles)


def conv_kernel(plan_ref, x_ref, got_ref, choose_ref, weight_ref, in_ref, bc_ref, *refs):
    parts, (mixed_ref, tail_ref), (source, wide, total, tails) = refs[:8], refs[8:10], refs[10:]
    tokens, chunk = x_ref.shape
    step, last = pl.program_id(0), pl.num_programs(0) - 1
    groups = got_ref.shape[1] // 3
    olds = got_ref.shape[0] * 3
    rank_dim = in_ref.shape[1]

    @pl.when(step == 0)
    def _():
        wide[...] = got_ref[...].reshape(olds * groups, LANES).astype(F32)
        source[tokens + olds :, :] = jnp.zeros((source.shape[0] - tokens - olds, chunk), BF)
        total[...] = jnp.zeros(total.shape, F32)

    source[0:tokens, :] = x_ref[...]
    low = step * (chunk // LANES)
    for j in range(chunk // LANES):
        source[tokens : tokens + olds, j * LANES : (j + 1) * LANES] = wide[
            pl.ds(low + j, olds, stride=groups), :
        ].astype(BF)
    taken = jnp.dot(choose_ref[...], source[...], preferred_element_type=F32)
    running = weight_ref[3:4, :] * x_ref[...].astype(F32)
    for lag in range(1, 4):
        running = (
            running + weight_ref[3 - lag : 4 - lag, :] * taken[(lag - 1) * tokens : lag * tokens]
        )
    mixed = (running / (1.0 + jnp.exp(-running))).astype(BF)
    mixed_ref[...] = mixed
    for j in range(chunk // LANES):
        tails[pl.ds(low + j, olds, stride=groups), :] = taken[
            3 * tokens :, j * LANES : (j + 1) * LANES
        ]
    maps = lax.dot_general(
        mixed, bc_ref[...], (((1,), (1,)), ((), ())), preferred_element_type=F32
    )
    total[:, 0:rank_dim] += jnp.dot(mixed, in_ref[...], preferred_element_type=F32)
    total[:, rank_dim : rank_dim + maps.shape[1]] += maps

    @pl.when(step == last)
    def _():
        tail_ref[...] = tails[...].astype(BF)
        share, width = tokens // 8, total.shape[1]
        for turn, part in enumerate(parts):
            place = lax.rem(plan_ref[plan_ref.shape[0] - 1] + turn, 8) * share
            rows = total[pl.ds(pl.multiple_of(place, share), share), :]
            high = rows.astype(BF)
            part[:, 0:width] = high
            part[:, width:] = (rows[:, rank_dim:] - high[:, rank_dim:].astype(F32)).astype(BF)


def conv_project(plan, x_rows, got, choose, conv_weight, dt_in_weight, bc_weight):
    tokens, channels = x_rows.shape
    rank_dim = dt_in_weight.shape[1]
    width = rank_dim + LANES
    conv_rows = 3 * channels // LANES
    tail_rows = got.shape[0] * conv_rows
    chunk = min(512, channels)
    once = pl.Buffered(1)
    return pl.pallas_call(
        conv_kernel,
        grid=(channels // chunk,),
        in_specs=in_smem(1)
        + [
            pl.BlockSpec((tokens, chunk), lambda i: (0, i)),
            pl.BlockSpec((got.shape[0], conv_rows, LANES), lambda i: (0, 0, 0), pipeline_mode=once),
            pl.BlockSpec(choose.shape, lambda i: (0, 0), pipeline_mode=once),
            pl.BlockSpec((4, chunk), lambda i: (0, i)),
            pl.BlockSpec((chunk, rank_dim), lambda i: (i, 0)),
            pl.BlockSpec((bc_weight.shape[0], chunk), lambda i: (0, i)),
        ],
        out_specs=in_vmem(8)
        + [
            pl.BlockSpec((tokens, chunk), lambda i: (0, i)),
            pl.BlockSpec((tail_rows, LANES), lambda i: (0, 0), pipeline_mode=once),
        ],
        out_shape=[jax.ShapeDtypeStruct((tokens // 8, width + LANES), BF)] * 8
        + [
            jax.ShapeDtypeStruct((tokens, channels), BF),
            jax.ShapeDtypeStruct((tail_rows, LANES), BF),
        ],
        scratch_shapes=[
            VMEM((choose.shape[1], chunk), BF),
            VMEM((tail_rows, LANES), F32),
            VMEM((tokens, width), F32),
            VMEM((tail_rows, LANES), F32),
        ],
        compiler_params=params(24),
    )(plan, *pin(x_rows, got, choose, conv_weight, dt_in_weight, bc_weight))


def sum_kernel(*refs):
    out_ref = refs[-1]
    total, rest = (
        functools.reduce(jnp.add, [part[:, cut].astype(F32) for part in refs[:-1]])
        for cut in (slice(0, -LANES), slice(-LANES, None))
    )
    rank_dim = total.shape[1] - LANES
    maps = total[:, rank_dim:] + rest
    high = maps.astype(BF)
    out_ref[:, 0:rank_dim] = total[:, 0:rank_dim].astype(BF)
    out_ref[:, rank_dim : rank_dim + LANES] = high
    out_ref[:, rank_dim + LANES :] = (maps - high.astype(F32)).astype(BF)


def sum_parts(parts):
    rows, width = parts[0].shape
    return pl.pallas_call(
        sum_kernel,
        in_specs=in_vmem(len(parts)),
        out_specs=in_vmem(1)[0],
        out_shape=jax.ShapeDtypeStruct((rows, width), BF),
        compiler_params=params(8),
    )(*parts)


def scan_kernel(states, count, plan_ref, *refs):
    pieces = refs[0:8]
    brought, (start_ref, tail_hbm, out_ref, back_ref) = refs[8:13], refs[13:17]
    mixed_ref, weight_ref, bias_ref, decay_ref, skip_ref, tail_ref = refs[17:23]
    low_dt, maps, map_smem, rates, drives, sums, decays, begun, ready, sem, sems, own = refs[23:]
    fetches = [
        pltpu.make_async_copy(source, target, own.at[n])
        for n, (source, target) in enumerate(zip((*brought, tail_hbm), refs[17:23]))
    ]
    for n in (1, 2, 0, 3, 4, 5):
        fetches[n].start()
    tokens, channels = mixed_ref.shape
    groups = channels // LANES
    share = tokens // 8
    rank_dim = weight_ref.shape[0]
    rank = plan_ref[3 * count]
    conv_rows = 3 * groups
    state_rows = states * groups

    def receive(r):
        return pltpu.make_async_copy(
            start_ref.at[plan_ref[r], pl.ds(conv_rows, state_rows)], begun.at[r], sems.at[r, 0]
        )

    def send_tail(r):
        owner = plan_ref[r]
        return pltpu.make_async_copy(
            tail_ref.at[owner], back_ref.at[owner, pl.ds(0, conv_rows)], sems.at[r, 1]
        )

    def send_state(r):
        return pltpu.make_async_copy(
            ready.at[r], back_ref.at[plan_ref[r], pl.ds(conv_rows, state_rows)], sems.at[r, 2]
        )

    for r in range(count):
        receive(r).start()
    for step, piece in enumerate(pieces):
        place = pl.multiple_of(lax.rem(rank + 8 - step, 8) * share, share)
        low_dt[pl.ds(place, share), :] = piece[:, 0:rank_dim]
        maps[pl.ds(place, share), :] = piece[:, rank_dim : rank_dim + LANES].astype(F32) + piece[
            :, rank_dim + LANES :
        ].astype(F32)
    copy = pltpu.make_async_copy(maps, map_smem, sem)
    copy.start()
    fetches[3].wait()
    for low in range(0, states, 8):
        for j in range(groups):
            decays[pl.ds(low * groups + j, 8, stride=groups), :] = decay_ref[
                low : low + 8, j * LANES : (j + 1) * LANES
            ] * (-math.log2(math.e))
    for n in (0, 1, 2):
        fetches[n].wait()
    chunk = min(512, channels)
    for low in range(0, channels, chunk):
        cut = slice(low, low + chunk)
        raw = (
            jnp.dot(low_dt[...], weight_ref[:, cut], preferred_element_type=F32) + bias_ref[:, cut]
        )
        rate = jnp.maximum(raw, 0.0) + jnp.log1p(jnp.exp(-jnp.abs(raw)))
        drive = rate * mixed_ref[:, cut].astype(F32)
        for j in range(chunk // LANES):
            rows = pl.ds(low // LANES + j, tokens, stride=groups)
            rates[rows, :] = rate[:, j * LANES : (j + 1) * LANES]
            drives[rows, :] = drive[:, j * LANES : (j + 1) * LANES]
    fetches[5].wait()
    for r in range(count):
        send_tail(r).start()
    copy.wait()

    def segment(r, begin):
        finish = begin + plan_ref[count + r]
        receive(r).wait()
        held = tuple(
            begun[r, n * groups : (n + 1) * groups, :].astype(F32) for n in range(states)
        )

        def token(t, held):
            place = pl.ds(pl.multiple_of(t * groups, groups), groups)
            rate, drive = rates[place, :], drives[place, :]
            total, later = None, []
            for n in range(states):
                decay = jnp.exp2(rate * decays[n * groups : (n + 1) * groups, :])
                value = decay * held[n] + drive * map_smem[t, n]
                term = value * map_smem[t, states + n]
                total = term if total is None else total + term
                later.append(value)
            sums[place, :] = total
            return tuple(later)

        held = lax.fori_loop(begin, finish, token, held)
        for n in range(states):
            ready[r, n * groups : (n + 1) * groups, :] = held[n].astype(BF)
        send_state(r).start()
        return finish

    lax.fori_loop(0, count, segment, jnp.int32(0))
    fetches[4].wait()
    for j in range(groups):
        cut = slice(j * LANES, (j + 1) * LANES)
        out_ref[:, cut] = (
            sums[pl.ds(j, tokens, stride=groups), :]
            + skip_ref[:, cut] * mixed_ref[:, cut].astype(F32)
        ).astype(BF)
    for r in range(count):
        send_tail(r).wait()
        send_state(r).wait()


def scan(plan, pieces, mixed, dt_weight, dt_bias, decay_rates, skip_gain, got, tails):
    tokens, channels = mixed.shape
    states = decay_rates.shape[0]
    groups = channels // LANES
    count = (plan.shape[0] - 1) // 3
    brought = (mixed, dt_weight, dt_bias[None, :], decay_rates, skip_gain[None, :])
    return pl.pallas_call(
        functools.partial(scan_kernel, states, count),
        in_specs=in_smem(1) + in_vmem(8) + in_hbm(7),
        out_specs=in_vmem(1) + in_hbm(1),
        out_shape=[
            jax.ShapeDtypeStruct((tokens, channels), BF),
            pltpu.HBM(got.shape, BF),
        ],
        scratch_shapes=[VMEM(a.shape, a.dtype) for a in (*brought, tails)]
        + [
            VMEM((tokens, dt_weight.shape[0]), BF),
            VMEM((tokens, LANES), F32),
            SMEM((tokens, LANES), F32),
            VMEM((tokens * groups, LANES), F32),
            VMEM((tokens * groups, LANES), F32),
            VMEM((tokens * groups, LANES), F32),
            VMEM((states * groups, LANES), F32),
            VMEM((count, states * groups, LANES), BF),
            VMEM((count, states * groups, LANES), BF),
            pltpu.SemaphoreType.DMA,
            pltpu.SemaphoreType.DMA((count, 3)),
            pltpu.SemaphoreType.DMA((6,)),
        ],
        compiler_params=params(32),
    )(plan, *pieces, *pin(*brought, got, tails))


def attend_kernel(count, plan_ref, q_ref, k_ref, v_ref, got_ref, out_ref, rows_q, rows_o, prefix_ref, sems):
    tokens = q_ref.shape[0]
    heads = q_ref.shape[1] // HEAD_DIM
    prefix = prefix_ref.shape[1] // 2

    def receive(r):
        return pltpu.make_async_copy(got_ref.at[plan_ref[r]], prefix_ref.at[r], sems.at[r])

    for r in range(count):
        receive(r).start()
    for h in range(heads):
        rows_q[h * tokens : (h + 1) * tokens, :] = q_ref[:, h * HEAD_DIM : (h + 1) * HEAD_DIM]
    contract = (((1,), (1,)), ((), ()))
    scale = HEAD_DIM**-0.5
    many = heads * tokens
    new_scores = lax.dot_general(
        rows_q[...], k_ref[...], contract, preferred_element_type=F32
    ) * scale
    query_of = lax.rem(lax.broadcasted_iota(I32, (many, tokens), 0), tokens)
    key_of = lax.broadcasted_iota(I32, (many, tokens), 1)
    new_scores = jnp.where(key_of <= query_of, new_scores, -1e30)
    token_of = lax.rem(lax.broadcasted_iota(I32, (many, HEAD_DIM), 0), tokens)
    place_of = lax.broadcasted_iota(I32, (many, prefix), 1)
    rows_o[...] = jnp.zeros((many, HEAD_DIM), F32)

    def request(r, begin):
        finish = begin + plan_ref[count + r]
        live = plan_ref[2 * count + r] * KVB
        receive(r).wait()
        old = lax.dot_general(
            rows_q[...], prefix_ref[r, 0:prefix, :], contract, preferred_element_type=F32
        ) * scale
        old = jnp.where(place_of < live, old, -1e30)
        new = jnp.where(key_of >= begin, new_scores, -1e30)
        highest = jnp.maximum(
            jnp.max(old, axis=1, keepdims=True), jnp.max(new, axis=1, keepdims=True)
        )
        old, new = jnp.exp(old - highest), jnp.exp(new - highest)
        total = jnp.sum(old, axis=1, keepdims=True) + jnp.sum(new, axis=1, keepdims=True)
        inverse = 1.0 / total
        result = jnp.dot(
            (old * inverse).astype(BF), prefix_ref[r, prefix:, :], preferred_element_type=F32
        ) + jnp.dot((new * inverse).astype(BF), v_ref[...], preferred_element_type=F32)
        mine = (token_of >= begin) & (token_of < finish)
        rows_o[...] = jnp.where(mine, result, rows_o[...])
        return finish

    lax.fori_loop(0, count, request, jnp.int32(0))
    for h in range(heads):
        out_ref[:, h * HEAD_DIM : (h + 1) * HEAD_DIM] = rows_o[
            h * tokens : (h + 1) * tokens, :
        ].astype(BF)


def attend(plan, queries, new_keys, new_values, got):
    tokens, width = queries.shape
    many = tokens * width // HEAD_DIM
    count = (plan.shape[0] - 1) // 3
    return pl.pallas_call(
        functools.partial(attend_kernel, count),
        grid=(1,),
        in_specs=in_smem(1) + whole(queries, new_keys, new_values) + in_hbm(1),
        out_specs=pl.BlockSpec((tokens, width), lambda i: (0, 0)),
        out_shape=jax.ShapeDtypeStruct((tokens, width), BF),
        scratch_shapes=[
            VMEM((many, HEAD_DIM), BF),
            VMEM((many, HEAD_DIM), F32),
            VMEM((count,) + got.shape[1:], BF),
            pltpu.SemaphoreType.DMA((count,)),
        ],
        compiler_params=params(),
    )(plan, *pin(queries, new_keys, new_values, got))


def write_kernel(
    asked_ref, conv_ref, store_ref, back_ref, conv_out, out_ref, source, hold, stage, tails, sems
):
    slots, states, channels = out_ref.shape
    groups = channels // LANES
    rows = states * groups
    conv_rows = 3 * groups
    for s in range(slots):
        source[s] = -1
    for row in range(asked_ref.shape[0]):
        slot = asked_ref[row, 0]

        @pl.when(slot >= 0)
        def _():
            source[slot] = row

    def kept(s):
        return pltpu.make_async_copy(store_ref.at[s], stage.at[s], sems.at[slots + s])

    def changed(s):
        return pltpu.make_async_copy(stage.at[s], out_ref.at[s], sems.at[s])

    for s in range(slots):

        @pl.when(source[s] < 0)
        def _():
            kept(s).start()
            tails[s * conv_rows : (s + 1) * conv_rows, :] = jnp.zeros((conv_rows, LANES), F32)
    landed = jnp.zeros((slots, LANES), I32)
    slot_of = lax.broadcasted_iota(I32, (slots, LANES), 0)
    for s in range(slots):
        row = source[s]
        landed = jnp.where(slot_of == s, row + 1, landed)

        @pl.when(row >= 0)
        def _():
            hold[s % 2] = back_ref[row, conv_rows:, :].astype(F32)
            for low in range(0, states, 8):
                for j in range(groups):
                    stage[s, low : low + 8, j * LANES : (j + 1) * LANES] = hold[
                        s % 2, pl.ds(low * groups + j, 8, stride=groups), :
                    ]
            changed(s).start()
            tails[s * conv_rows : (s + 1) * conv_rows, :] = back_ref[row, 0:conv_rows, :].astype(F32)

    for i in range(3):
        for j in range(groups):
            cut = slice(j * LANES, (j + 1) * LANES)
            fresh = tails[pl.ds(i * groups + j, slots, stride=3 * groups), :]
            conv_out[i, :, cut] = jnp.where(
                landed > 0, fresh, conv_ref[i, :, cut].astype(F32)
            ).astype(BF)
    for s in range(slots):

        @pl.when(source[s] < 0)
        def _():
            kept(s).wait()
            changed(s).start()

    for s in range(slots):
        changed(s).wait()


def write_store(asked, store_state, conv_rows, back):
    slots, states, channels = store_state.shape
    groups = channels // LANES
    return pl.pallas_call(
        write_kernel,
        grid=(1,),
        in_specs=in_smem(1) + whole(conv_rows) + in_hbm(1) + in_vmem(1),
        out_specs=whole(conv_rows) + in_hbm(1),
        out_shape=[
            jax.ShapeDtypeStruct(conv_rows.shape, BF),
            jax.ShapeDtypeStruct((slots, states, channels), F32),
        ],
        scratch_shapes=[
            SMEM((slots,), I32),
            VMEM((2, states * groups, LANES), F32),
            VMEM((slots, states, channels), F32),
            VMEM((slots * 3 * groups, LANES), F32),
            pltpu.SemaphoreType.DMA((2 * slots,)),
        ],
        compiler_params=params(24),
    )(asked, *pin(conv_rows, store_state), back)


def exchange(blocks, axis):
    return lax.all_to_all(blocks, axis, split_axis=0, concat_axis=0, tiled=True)


def choose_matrix(lengths, owners, tokens, owner_count, width):
    ends = jnp.cumsum(lengths, dtype=I32)
    starts = ends - lengths
    places = jnp.arange(tokens, dtype=I32)
    member = (places[:, None] >= starts[None, :]) & (places[:, None] < ends[None, :])
    offset = places - jnp.sum(jnp.where(member, starts[None, :], 0), axis=1, dtype=I32)
    owner = jnp.sum(jnp.where(member, owners[None, :], 0), axis=1, dtype=I32)
    lags = jnp.arange(1, 4, dtype=I32)[:, None]
    lagged = jnp.where(
        offset[None, :] >= lags,
        places[None, :] - lags,
        tokens + owner[None, :] * 3 + 3 + offset[None, :] - lags,
    )
    owner_ids = jnp.arange(owner_count, dtype=I32)
    served = owner_ids[:, None] == owners[None, :]
    ends_of = jnp.sum(jnp.where(served, ends[None, :], 0), axis=1, dtype=I32)[:, None]
    length_of = jnp.sum(jnp.where(served, lengths[None, :], 0), axis=1, dtype=I32)[:, None]
    rows = jnp.arange(3, dtype=I32)[None, :]
    tails = jnp.where(
        length_of + rows >= 3, ends_of - 3 + rows, tokens + owner_ids[:, None] * 3 + length_of + rows
    )
    tails = jnp.where(length_of > 0, tails, width)
    column = jnp.concatenate([lagged.reshape(-1), tails.reshape(-1)])
    return (column[:, None] == jnp.arange(width, dtype=I32)[None, :]).astype(BF)


def shards(
    x_in,
    conv_weight,
    dt_in_weight,
    bc_weight,
    dt_weight,
    dt_bias,
    decay_rates,
    skip_gain,
    queries,
    new_keys,
    new_values,
    store_state,
    store_conv,
    store_keys,
    store_values,
    hit_entry,
    hit_blocks,
    seg_lengths,
):
    owner_count = lax.axis_size("cache")
    tp_count = lax.axis_size("tp")
    rank = lax.axis_index("tp").astype(I32)[None]
    slot_count, states, channels = store_state.shape
    groups = channels // LANES
    tokens = x_in.shape[0]
    lengths = seg_lengths[0]
    table, plan = ask(hit_entry, hit_blocks, seg_lengths, rank, slot_count, owner_count)
    asked = exchange(table, "cache")[:, 0, :]

    conv_store = store_conv.transpose(1, 0, 2)
    tiles = entry_tiles(conv_store, store_state)
    got = exchange(pick_tiles(asked, tiles, 3 * groups), "cache")

    width = tokens + -(-3 * owner_count // LANES) * LANES
    choose = choose_matrix(lengths, hit_entry // slot_count, tokens, owner_count, width)
    *parts, mixed, tails = conv_project(
        plan, x_in, got, choose, conv_weight, dt_in_weight, bc_weight
    )

    def turned(step, value):
        return lax.ppermute(value, "tp", [(k, (k + step) % tp_count) for k in range(tp_count)])

    parts = [parts[0]] + [turned(step, parts[step]) for step in range(1, tp_count)]
    summed = sum_parts(parts)
    pieces = [summed] + [turned(step, summed) for step in range(1, tp_count)]
    got_prefix = exchange(pick(asked, *pin(store_keys, store_values)), "cache")

    mixer_out, back = scan(
        plan, pieces, mixed, dt_weight, dt_bias, decay_rates, skip_gain, got,
        tails.reshape(owner_count, 3 * groups, LANES),
    )
    back = exchange(back, "cache")
    attn_out = attend(plan, queries, new_keys, new_values, got_prefix)
    conv_rows, new_state = write_store(asked, store_state, conv_store, back)
    return (mixer_out, attn_out, new_state, conv_rows.transpose(1, 0, 2))


def solution(mesh):
    placed = (
        P("cache", "tp"),
        P(None, "tp"),
        P("tp", None),
        P(None, "tp"),
        P(None, "tp"),
        P("tp"),
        P(None, "tp"),
        P("tp"),
        P("cache", "tp"),
        P("cache", "tp"),
        P("cache", "tp"),
        P("cache", None, "tp"),
        P("cache", None, "tp"),
        P("cache", None, "tp"),
        P("cache", None, "tp"),
        P("cache"),
        P("cache"),
        P("cache", None),
    )
    return jax.shard_map(
        shards,
        mesh=mesh,
        in_specs=placed,
        out_specs=(
            P("cache", "tp"),
            P("cache", "tp"),
            P("cache", None, "tp"),
            P("cache", None, "tp"),
        ),
        check_vma=False,
    )
```

```python
import functools
import math

import jax
import jax.numpy as jnp
from jax import lax
from jax.experimental import pallas as pl
from jax.experimental.pallas import tpu as pltpu
from jax.sharding import PartitionSpec as P

HEAD_DIM = 128
KVB = 128
LANES = 128
BF = jnp.bfloat16
F32 = jnp.float32
I32 = jnp.int32
VMEM = pltpu.VMEM
SMEM = pltpu.SMEM
MIB = 1 << 20


def params(mib=58):
    return pltpu.CompilerParams(vmem_limit_bytes=mib * MIB)


def in_vmem(count):
    return [pl.BlockSpec(memory_space=VMEM) for _ in range(count)]


def in_smem(count):
    return [pl.BlockSpec(memory_space=SMEM) for _ in range(count)]


def in_hbm(count):
    return [pl.BlockSpec(memory_space=pltpu.HBM) for _ in range(count)]


def pin(*arrays):
    return [pltpu.with_memory_space_constraint(a, pltpu.HBM) for a in arrays]


def whole(*arrays):
    return [
        pl.BlockSpec(a.shape, lambda i, n=len(a.shape): (0,) * n, pipeline_mode=pl.Buffered(1))
        for a in arrays
    ]


def ask_kernel(entry_ref, block_ref, length_ref, rank_ref, out_ref, plan_ref, *, slots):
    shape = out_ref.shape
    count = entry_ref.shape[0]
    owner_of = lax.broadcasted_iota(I32, shape, 0)
    table = jnp.full(shape, -1, I32)
    for r in range(count):
        owner = lax.div(entry_ref[r], slots)
        plan_ref[r] = owner
        plan_ref[count + r] = length_ref[0, r]
        plan_ref[2 * count + r] = block_ref[r]
        table = jnp.where(owner_of == owner, entry_ref[r] - owner * slots, table)
    plan_ref[3 * count] = rank_ref[0]
    out_ref[...] = table


def ask(hit_entry, hit_blocks, seg_lengths, rank, slots, owner_count):
    return pl.pallas_call(
        functools.partial(ask_kernel, slots=slots),
        in_specs=in_smem(4),
        out_specs=in_vmem(1) + in_smem(1),
        out_shape=[
            jax.ShapeDtypeStruct((owner_count, 1, LANES), I32),
            jax.ShapeDtypeStruct((3 * hit_entry.shape[0] + 1,), I32),
        ],
        compiler_params=params(),
    )(hit_entry, hit_blocks, seg_lengths, rank)


def tiles_kernel(conv_ref, state_ref, out_ref, hold, tails):
    entries, states, channels = state_ref.shape
    slots = conv_ref.shape[1]
    groups = channels // LANES
    conv_rows = 3 * groups
    first = pl.program_id(0) * entries

    @pl.when(first == 0)
    def _():
        for i in range(3):
            for j in range(groups):
                tails[pl.ds(i * groups + j, slots, stride=conv_rows), :] = conv_ref[
                    i, :, j * LANES : (j + 1) * LANES
                ].astype(F32)

    for e in range(entries):
        for low in range(0, states, 8):
            for j in range(groups):
                hold[pl.ds(low * groups + j, 8, stride=groups), :] = state_ref[
                    e, low : low + 8, j * LANES : (j + 1) * LANES
                ]
        place = pl.multiple_of((first + e) * conv_rows, conv_rows)
        out_ref[e, 0:conv_rows, :] = tails[pl.ds(place, conv_rows), :].astype(BF)
        out_ref[e, conv_rows:, :] = hold[...].astype(BF)


def entry_tiles(conv_rows, store_state):
    slots, states, channels = store_state.shape
    rows = states * channels // LANES
    tail_rows = 3 * channels // LANES
    step = 4
    return pl.pallas_call(
        tiles_kernel,
        grid=(slots // step,),
        in_specs=whole(conv_rows)
        + [pl.BlockSpec((step, states, channels), lambda i: (i, 0, 0))],
        out_specs=pl.BlockSpec((step, tail_rows + rows, LANES), lambda i: (i, 0, 0)),
        out_shape=jax.ShapeDtypeStruct((slots, tail_rows + rows, LANES), BF),
        scratch_shapes=[VMEM((rows, LANES), F32), VMEM((slots * tail_rows, LANES), F32)],
        compiler_params=params(16),
    )(*pin(conv_rows, store_state))


def pick_kernel(count, asked_ref, *refs):
    sources, (out_ref, stage, sems) = refs[:count], refs[count:]
    blocks = out_ref.shape[0]
    lows = [sum(s.shape[1] for s in sources[:n]) for n in range(count + 1)]

    def load(i, n):
        return pltpu.make_async_copy(
            sources[n].at[jnp.maximum(asked_ref[i, 0], 0)],
            stage.at[i, pl.ds(lows[n], sources[n].shape[1])],
            sems.at[0, i, n],
        )

    def store(i, n):
        part = pl.ds(lows[n], sources[n].shape[1])
        return pltpu.make_async_copy(stage.at[i, part], out_ref.at[i, part], sems.at[1, i, n])

    def each(act):
        for i in range(blocks):

            @pl.when(asked_ref[i, 0] >= 0)
            def _():
                for n in range(count):
                    act(i, n)

    def turn(i, n):
        load(i, n).wait()
        store(i, n).start()

    each(lambda i, n: load(i, n).start())
    each(turn)
    each(lambda i, n: store(i, n).wait())


def pick(asked, *sources):
    blocks = asked.shape[0]
    rows = sum(s.shape[1] for s in sources)
    return pl.pallas_call(
        functools.partial(pick_kernel, len(sources)),
        in_specs=in_smem(1) + in_hbm(len(sources)),
        out_specs=in_hbm(1)[0],
        out_shape=pltpu.HBM((blocks, rows, LANES), BF),
        scratch_shapes=[
            VMEM((blocks, rows, LANES), BF),
            pltpu.SemaphoreType.DMA((2, blocks, len(sources))),
        ],
        compiler_params=params(32),
    )(asked, *sources)


def pick_tiles_kernel(part, asked_ref, tiles_ref, out_ref, sems):
    def act(name):
        for i in range(out_ref.shape[0]):
            slot = asked_ref[i, 0]

            @pl.when(slot >= 0)
            def _():
                getattr(pltpu.make_async_copy(tiles_ref.at[slot], out_ref.at[i], sems.at[i]), name)()

            @pl.when(slot < 0)
            def _():
                few = pl.ds(0, part)
                getattr(
                    pltpu.make_async_copy(tiles_ref.at[0, few], out_ref.at[i, few], sems.at[i]), name
                )()

    act("start")
    act("wait")


def pick_tiles(asked, tiles, part):
    blocks = asked.shape[0]
    return pl.pallas_call(
        functools.partial(pick_tiles_kernel, part),
        in_specs=in_smem(1) + in_vmem(1),
        out_specs=in_hbm(1)[0],
        out_shape=pltpu.HBM((blocks,) + tiles.shape[1:], BF),
        scratch_shapes=[pltpu.SemaphoreType.DMA((blocks,))],
        compiler_params=params(4),
    )(asked, tiles)


def bring_kernel(count, after_ref, *refs):
    sources, targets = refs[:count], refs[count + 1 : 2 * count + 1]
    decay_ref, tile_ref, sems = refs[count], refs[2 * count + 1], refs[2 * count + 2]
    copies = [
        pltpu.make_async_copy(source, target, sems.at[n])
        for n, (source, target) in enumerate(zip(sources, targets))
    ]
    for copy in copies:
        copy.start()
    states, channels = decay_ref.shape
    groups = channels // LANES
    for low in range(0, states, 8):
        for j in range(groups):
            tile_ref[pl.ds(low * groups + j, 8, stride=groups), :] = decay_ref[
                low : low + 8, j * LANES : (j + 1) * LANES
            ] * (-math.log2(math.e))
    for copy in copies:
        copy.wait()


def bring(after, decay_rates, *arrays):
    states, channels = decay_rates.shape
    return pl.pallas_call(
        functools.partial(bring_kernel, len(arrays)),
        in_specs=in_hbm(1 + len(arrays)) + in_vmem(1),
        out_specs=in_vmem(len(arrays) + 1),
        out_shape=[jax.ShapeDtypeStruct(a.shape, a.dtype) for a in arrays]
        + [jax.ShapeDtypeStruct((states * channels // LANES, LANES), F32)],
        scratch_shapes=[pltpu.SemaphoreType.DMA((len(arrays),))],
        compiler_params=params(4),
    )(*pin(after, *arrays), decay_rates)


def conv_kernel(plan_ref, x_ref, choose_ref, weight_ref, in_ref, bc_ref, got_ref, *refs):
    parts, (mixed_ref, tail_ref), (source, wide, total, tails, came, sem) = (
        refs[:8], refs[8:10], refs[10:]
    )
    tokens, channels = x_ref.shape
    groups = channels // LANES
    olds = got_ref.shape[0] * 3
    rank_dim = in_ref.shape[1]
    chunk = source.shape[1]
    copy = pltpu.make_async_copy(got_ref.at[:, pl.ds(0, 3 * groups)], came, sem)
    copy.start()
    source[tokens + olds :, :] = jnp.zeros((source.shape[0] - tokens - olds, chunk), BF)
    total[...] = jnp.zeros(total.shape, F32)
    copy.wait()
    wide[...] = came[...].reshape(olds * groups, LANES).astype(F32)
    for low in range(0, channels, chunk):
        cut = slice(low, low + chunk)
        source[0:tokens, :] = x_ref[:, cut]
        for j in range(chunk // LANES):
            source[tokens : tokens + olds, j * LANES : (j + 1) * LANES] = wide[
                pl.ds(low // LANES + j, olds, stride=groups), :
            ].astype(BF)
        taken = jnp.dot(choose_ref[...], source[...], preferred_element_type=F32)
        running = weight_ref[3:4, cut] * x_ref[:, cut].astype(F32)
        for lag in range(1, 4):
            running = (
                running
                + weight_ref[3 - lag : 4 - lag, cut] * taken[(lag - 1) * tokens : lag * tokens]
            )
        mixed = (running / (1.0 + jnp.exp(-running))).astype(BF)
        mixed_ref[:, cut] = mixed
        for j in range(chunk // LANES):
            tails[pl.ds(low // LANES + j, olds, stride=groups), :] = taken[
                3 * tokens :, j * LANES : (j + 1) * LANES
            ]
        maps = lax.dot_general(
            mixed, bc_ref[:, cut], (((1,), (1,)), ((), ())), preferred_element_type=F32
        )
        total[:, 0:rank_dim] += jnp.dot(mixed, in_ref[cut, :], preferred_element_type=F32)
        total[:, rank_dim : rank_dim + maps.shape[1]] += maps
    tail_ref[...] = tails[...].reshape(tail_ref.shape).astype(BF)
    share, width = tokens // 8, total.shape[1]
    for turn, part in enumerate(parts):
        place = lax.rem(plan_ref[plan_ref.shape[0] - 1] + turn, 8) * share
        rows = total[pl.ds(pl.multiple_of(place, share), share), :]
        high = rows.astype(BF)
        part[:, 0:width] = high
        part[:, width:] = (rows[:, rank_dim:] - high[:, rank_dim:].astype(F32)).astype(BF)


def conv_project(plan, x_rows, choose, conv_weight, dt_in_weight, bc_weight, got):
    tokens, channels = x_rows.shape
    width = dt_in_weight.shape[1] + LANES
    conv_rows = 3 * channels // LANES
    tail_rows = got.shape[0] * conv_rows
    return pl.pallas_call(
        conv_kernel,
        in_specs=in_smem(1) + in_vmem(5) + [pl.BlockSpec(memory_space=pl.ANY)],
        out_specs=in_vmem(10),
        out_shape=[jax.ShapeDtypeStruct((tokens // 8, width + LANES), BF)] * 8
        + [
            jax.ShapeDtypeStruct((tokens, channels), BF),
            jax.ShapeDtypeStruct((got.shape[0], conv_rows, LANES), BF),
        ],
        scratch_shapes=[
            VMEM((choose.shape[1], min(512, channels)), BF),
            VMEM((tail_rows, LANES), F32),
            VMEM((tokens, width), F32),
            VMEM((tail_rows, LANES), F32),
            VMEM((got.shape[0], conv_rows, LANES), BF),
            pltpu.SemaphoreType.DMA,
        ],
        compiler_params=params(24),
    )(plan, x_rows, choose, conv_weight, dt_in_weight, bc_weight, got)


def sum_kernel(*refs):
    out_ref = refs[-1]
    total, rest = (
        functools.reduce(jnp.add, [part[:, cut].astype(F32) for part in refs[:-1]])
        for cut in (slice(0, -LANES), slice(-LANES, None))
    )
    rank_dim = total.shape[1] - LANES
    maps = total[:, rank_dim:] + rest
    high = maps.astype(BF)
    out_ref[:, 0:rank_dim] = total[:, 0:rank_dim].astype(BF)
    out_ref[:, rank_dim : rank_dim + LANES] = high
    out_ref[:, rank_dim + LANES :] = (maps - high.astype(F32)).astype(BF)


def sum_parts(parts):
    rows, width = parts[0].shape
    return pl.pallas_call(
        sum_kernel,
        in_specs=in_vmem(len(parts)),
        out_specs=in_vmem(1)[0],
        out_shape=jax.ShapeDtypeStruct((rows, width), BF),
        compiler_params=params(8),
    )(*parts)


def scan_kernel(states, count, plan_ref, *refs):
    pieces = refs[0:8]
    mixed_ref, weight_ref, bias_ref, skip_ref, tail_ref, decays, start_ref = refs[8:15]
    out_ref, back_ref = refs[15:17]
    low_dt, maps, map_smem, rates, drives, sums, begun, ready, sem, sems = refs[17:]
    tokens, channels = mixed_ref.shape
    groups = channels // LANES
    share = tokens // 8
    rank_dim = weight_ref.shape[0]
    rank = plan_ref[3 * count]
    conv_rows = 3 * groups
    state_rows = states * groups

    def receive(r):
        return pltpu.make_async_copy(
            start_ref.at[plan_ref[r], pl.ds(conv_rows, state_rows)], begun.at[r], sems.at[r, 0]
        )

    def send_tail(r):
        owner = plan_ref[r]
        return pltpu.make_async_copy(
            tail_ref.at[owner], back_ref.at[owner, pl.ds(0, conv_rows)], sems.at[r, 1]
        )

    def send_state(r):
        return pltpu.make_async_copy(
            ready.at[r], back_ref.at[plan_ref[r], pl.ds(conv_rows, state_rows)], sems.at[r, 2]
        )

    for r in range(count):
        receive(r).start()
        send_tail(r).start()
    for step, piece in enumerate(pieces):
        place = pl.multiple_of(lax.rem(rank + 8 - step, 8) * share, share)
        low_dt[pl.ds(place, share), :] = piece[:, 0:rank_dim]
        maps[pl.ds(place, share), :] = piece[:, rank_dim : rank_dim + LANES].astype(F32) + piece[
            :, rank_dim + LANES :
        ].astype(F32)
    copy = pltpu.make_async_copy(maps, map_smem, sem)
    copy.start()
    chunk = min(512, channels)
    for low in range(0, channels, chunk):
        cut = slice(low, low + chunk)
        raw = (
            jnp.dot(low_dt[...], weight_ref[:, cut], preferred_element_type=F32) + bias_ref[:, cut]
        )
        rate = jnp.maximum(raw, 0.0) + jnp.log1p(jnp.exp(-jnp.abs(raw)))
        drive = rate * mixed_ref[:, cut].astype(F32)
        for j in range(chunk // LANES):
            rows = pl.ds(low // LANES + j, tokens, stride=groups)
            rates[rows, :] = rate[:, j * LANES : (j + 1) * LANES]
            drives[rows, :] = drive[:, j * LANES : (j + 1) * LANES]
    copy.wait()

    def segment(r, begin):
        finish = begin + plan_ref[count + r]
        receive(r).wait()
        held = tuple(
            begun[r, n * groups : (n + 1) * groups, :].astype(F32) for n in range(states)
        )

        def token(t, held):
            place = pl.ds(pl.multiple_of(t * groups, groups), groups)
            rate, drive = rates[place, :], drives[place, :]
            total, later = None, []
            for n in range(states):
                decay = jnp.exp2(rate * decays[n * groups : (n + 1) * groups, :])
                value = decay * held[n] + drive * map_smem[t, n]
                term = value * map_smem[t, states + n]
                total = term if total is None else total + term
                later.append(value)
            sums[place, :] = total
            return tuple(later)

        held = lax.fori_loop(begin, finish, token, held)
        for n in range(states):
            ready[r, n * groups : (n + 1) * groups, :] = held[n].astype(BF)
        send_state(r).start()
        return finish

    lax.fori_loop(0, count, segment, jnp.int32(0))
    for j in range(groups):
        cut = slice(j * LANES, (j + 1) * LANES)
        out_ref[:, cut] = (
            sums[pl.ds(j, tokens, stride=groups), :]
            + skip_ref[:, cut] * mixed_ref[:, cut].astype(F32)
        ).astype(BF)
    for r in range(count):
        send_tail(r).wait()
        send_state(r).wait()


def scan(plan, pieces, mixed, dt_weight, dt_bias, skip_gain, tails, decays, got):
    tokens, channels = mixed.shape
    groups = channels // LANES
    state_rows = decays.shape[0]
    count = (plan.shape[0] - 1) // 3
    return pl.pallas_call(
        functools.partial(scan_kernel, state_rows // groups, count),
        in_specs=in_smem(1) + in_vmem(14) + [pl.BlockSpec(memory_space=pl.ANY)],
        out_specs=in_vmem(1) + in_hbm(1),
        out_shape=[
            jax.ShapeDtypeStruct((tokens, channels), BF),
            pltpu.HBM(got.shape, BF),
        ],
        scratch_shapes=[
            VMEM((tokens, dt_weight.shape[0]), BF),
            VMEM((tokens, LANES), F32),
            SMEM((tokens, LANES), F32),
            VMEM((tokens * groups, LANES), F32),
            VMEM((tokens * groups, LANES), F32),
            VMEM((tokens * groups, LANES), F32),
            VMEM((count, state_rows, LANES), BF),
            VMEM((count, state_rows, LANES), BF),
            pltpu.SemaphoreType.DMA,
            pltpu.SemaphoreType.DMA((count, 3)),
        ],
        compiler_params=params(24),
    )(plan, *pieces, mixed, dt_weight, dt_bias, skip_gain, tails, decays, got)


def attend_kernel(count, plan_ref, q_ref, k_ref, v_ref, got_ref, out_ref, rows_q, rows_o, prefix_ref, sems):
    tokens = q_ref.shape[0]
    heads = q_ref.shape[1] // HEAD_DIM
    prefix = prefix_ref.shape[1] // 2

    def receive(r):
        return pltpu.make_async_copy(got_ref.at[plan_ref[r]], prefix_ref.at[r], sems.at[r])

    for r in range(count):
        receive(r).start()
    for h in range(heads):
        rows_q[h * tokens : (h + 1) * tokens, :] = q_ref[:, h * HEAD_DIM : (h + 1) * HEAD_DIM]
    contract = (((1,), (1,)), ((), ()))
    scale = HEAD_DIM**-0.5
    many = heads * tokens
    new_scores = lax.dot_general(
        rows_q[...], k_ref[...], contract, preferred_element_type=F32
    ) * scale
    query_of = lax.rem(lax.broadcasted_iota(I32, (many, tokens), 0), tokens)
    key_of = lax.broadcasted_iota(I32, (many, tokens), 1)
    new_scores = jnp.where(key_of <= query_of, new_scores, -1e30)
    token_of = lax.rem(lax.broadcasted_iota(I32, (many, HEAD_DIM), 0), tokens)
    place_of = lax.broadcasted_iota(I32, (many, prefix), 1)
    rows_o[...] = jnp.zeros((many, HEAD_DIM), F32)

    def request(r, begin):
        finish = begin + plan_ref[count + r]
        live = plan_ref[2 * count + r] * KVB
        receive(r).wait()
        old = lax.dot_general(
            rows_q[...], prefix_ref[r, 0:prefix, :], contract, preferred_element_type=F32
        ) * scale
        old = jnp.where(place_of < live, old, -1e30)
        new = jnp.where(key_of >= begin, new_scores, -1e30)
        highest = jnp.maximum(
            jnp.max(old, axis=1, keepdims=True), jnp.max(new, axis=1, keepdims=True)
        )
        old, new = jnp.exp(old - highest), jnp.exp(new - highest)
        total = jnp.sum(old, axis=1, keepdims=True) + jnp.sum(new, axis=1, keepdims=True)
        inverse = 1.0 / total
        result = jnp.dot(
            (old * inverse).astype(BF), prefix_ref[r, prefix:, :], preferred_element_type=F32
        ) + jnp.dot((new * inverse).astype(BF), v_ref[...], preferred_element_type=F32)
        mine = (token_of >= begin) & (token_of < finish)
        rows_o[...] = jnp.where(mine, result, rows_o[...])
        return finish

    lax.fori_loop(0, count, request, jnp.int32(0))
    for h in range(heads):
        out_ref[:, h * HEAD_DIM : (h + 1) * HEAD_DIM] = rows_o[
            h * tokens : (h + 1) * tokens, :
        ].astype(BF)


def attend(plan, queries, new_keys, new_values, got):
    tokens, width = queries.shape
    many = tokens * width // HEAD_DIM
    count = (plan.shape[0] - 1) // 3
    return pl.pallas_call(
        functools.partial(attend_kernel, count),
        grid=(1,),
        in_specs=in_smem(1) + whole(queries, new_keys, new_values) + in_hbm(1),
        out_specs=pl.BlockSpec((tokens, width), lambda i: (0, 0)),
        out_shape=jax.ShapeDtypeStruct((tokens, width), BF),
        scratch_shapes=[
            VMEM((many, HEAD_DIM), BF),
            VMEM((many, HEAD_DIM), F32),
            VMEM((count,) + got.shape[1:], BF),
            pltpu.SemaphoreType.DMA((count,)),
        ],
        compiler_params=params(),
    )(plan, *pin(queries, new_keys, new_values, got))


def write_kernel(
    asked_ref, conv_ref, store_ref, back_ref, conv_out, out_ref, source, hold, stage, tails, sems
):
    slots, states, channels = out_ref.shape
    groups = channels // LANES
    rows = states * groups
    conv_rows = 3 * groups
    for s in range(slots):
        source[s] = -1
    for row in range(asked_ref.shape[0]):
        slot = asked_ref[row, 0]

        @pl.when(slot >= 0)
        def _():
            source[slot] = row

    def kept(s):
        return pltpu.make_async_copy(store_ref.at[s], stage.at[s], sems.at[slots + s])

    def changed(s):
        return pltpu.make_async_copy(stage.at[s], out_ref.at[s], sems.at[s])

    for s in range(slots):

        @pl.when(source[s] < 0)
        def _():
            kept(s).start()
            tails[s * conv_rows : (s + 1) * conv_rows, :] = jnp.zeros((conv_rows, LANES), F32)
    landed = jnp.zeros((slots, LANES), I32)
    slot_of = lax.broadcasted_iota(I32, (slots, LANES), 0)
    for s in range(slots):
        row = source[s]
        landed = jnp.where(slot_of == s, row + 1, landed)

        @pl.when(row >= 0)
        def _():
            hold[s % 2] = back_ref[row, conv_rows:, :].astype(F32)
            for low in range(0, states, 8):
                for j in range(groups):
                    stage[s, low : low + 8, j * LANES : (j + 1) * LANES] = hold[
                        s % 2, pl.ds(low * groups + j, 8, stride=groups), :
                    ]
            changed(s).start()
            tails[s * conv_rows : (s + 1) * conv_rows, :] = back_ref[row, 0:conv_rows, :].astype(F32)

    for i in range(3):
        for j in range(groups):
            cut = slice(j * LANES, (j + 1) * LANES)
            fresh = tails[pl.ds(i * groups + j, slots, stride=3 * groups), :]
            conv_out[i, :, cut] = jnp.where(
                landed > 0, fresh, conv_ref[i, :, cut].astype(F32)
            ).astype(BF)
    for s in range(slots):

        @pl.when(source[s] < 0)
        def _():
            kept(s).wait()
            changed(s).start()

    for s in range(slots):
        changed(s).wait()


def write_store(asked, store_state, conv_rows, back):
    slots, states, channels = store_state.shape
    groups = channels // LANES
    return pl.pallas_call(
        write_kernel,
        grid=(1,),
        in_specs=in_smem(1) + whole(conv_rows) + in_hbm(1) + in_vmem(1),
        out_specs=whole(conv_rows) + in_hbm(1),
        out_shape=[
            jax.ShapeDtypeStruct(conv_rows.shape, BF),
            jax.ShapeDtypeStruct((slots, states, channels), F32),
        ],
        scratch_shapes=[
            SMEM((slots,), I32),
            VMEM((2, states * groups, LANES), F32),
            VMEM((slots, states, channels), F32),
            VMEM((slots * 3 * groups, LANES), F32),
            pltpu.SemaphoreType.DMA((2 * slots,)),
        ],
        compiler_params=params(24),
    )(asked, *pin(conv_rows, store_state), back)


def exchange(blocks, axis):
    return lax.all_to_all(blocks, axis, split_axis=0, concat_axis=0, tiled=True)


def choose_matrix(lengths, owners, tokens, owner_count, width):
    ends = jnp.cumsum(lengths, dtype=I32)
    starts = ends - lengths
    places = jnp.arange(tokens, dtype=I32)
    member = (places[:, None] >= starts[None, :]) & (places[:, None] < ends[None, :])
    offset = places - jnp.sum(jnp.where(member, starts[None, :], 0), axis=1, dtype=I32)
    owner = jnp.sum(jnp.where(member, owners[None, :], 0), axis=1, dtype=I32)
    lags = jnp.arange(1, 4, dtype=I32)[:, None]
    lagged = jnp.where(
        offset[None, :] >= lags,
        places[None, :] - lags,
        tokens + owner[None, :] * 3 + 3 + offset[None, :] - lags,
    )
    owner_ids = jnp.arange(owner_count, dtype=I32)
    served = owner_ids[:, None] == owners[None, :]
    ends_of = jnp.sum(jnp.where(served, ends[None, :], 0), axis=1, dtype=I32)[:, None]
    length_of = jnp.sum(jnp.where(served, lengths[None, :], 0), axis=1, dtype=I32)[:, None]
    rows = jnp.arange(3, dtype=I32)[None, :]
    tails = jnp.where(
        length_of + rows >= 3, ends_of - 3 + rows, tokens + owner_ids[:, None] * 3 + length_of + rows
    )
    tails = jnp.where(length_of > 0, tails, width)
    column = jnp.concatenate([lagged.reshape(-1), tails.reshape(-1)])
    return (column[:, None] == jnp.arange(width, dtype=I32)[None, :]).astype(BF)


def shards(
    x_in,
    conv_weight,
    dt_in_weight,
    bc_weight,
    dt_weight,
    dt_bias,
    decay_rates,
    skip_gain,
    queries,
    new_keys,
    new_values,
    store_state,
    store_conv,
    store_keys,
    store_values,
    hit_entry,
    hit_blocks,
    seg_lengths,
):
    owner_count = lax.axis_size("cache")
    tp_count = lax.axis_size("tp")
    rank = lax.axis_index("tp").astype(I32)[None]
    slot_count, states, channels = store_state.shape
    groups = channels // LANES
    tokens = x_in.shape[0]
    lengths = seg_lengths[0]
    table, plan = ask(hit_entry, hit_blocks, seg_lengths, rank, slot_count, owner_count)
    asked = exchange(table, "cache")[:, 0, :]

    conv_store = store_conv.transpose(1, 0, 2)
    tiles = entry_tiles(conv_store, store_state)
    sent = pick_tiles(asked, tiles, 3 * groups)
    width = tokens + -(-3 * owner_count // LANES) * LANES
    choose = choose_matrix(lengths, hit_entry // slot_count, tokens, owner_count, width)
    x_rows, choose, taps, dt_in, bc_in, dt_out, bias, skip, decays = bring(
        sent, decay_rates, x_in, choose, conv_weight, dt_in_weight, bc_weight, dt_weight,
        dt_bias[None, :], skip_gain[None, :],
    )
    got = exchange(sent, "cache")
    *parts, mixed, tails = conv_project(plan, x_rows, choose, taps, dt_in, bc_in, got)

    def turned(step, value):
        return lax.ppermute(value, "tp", [(k, (k + step) % tp_count) for k in range(tp_count)])

    parts = [parts[0]] + [turned(step, parts[step]) for step in range(1, tp_count)]
    summed = sum_parts(parts)
    pieces = [summed] + [turned(step, summed) for step in range(1, tp_count)]
    got_prefix = exchange(pick(asked, *pin(store_keys, store_values)), "cache")

    mixer_out, back = scan(plan, pieces, mixed, dt_out, bias, skip, tails, decays, got)
    back = exchange(back, "cache")
    attn_out = attend(plan, queries, new_keys, new_values, got_prefix)
    conv_rows, new_state = write_store(asked, store_state, conv_store, back)
    return (mixer_out, attn_out, new_state, conv_rows.transpose(1, 0, 2))


def solution(mesh):
    placed = (
        P("cache", "tp"),
        P(None, "tp"),
        P("tp", None),
        P(None, "tp"),
        P(None, "tp"),
        P("tp"),
        P(None, "tp"),
        P("tp"),
        P("cache", "tp"),
        P("cache", "tp"),
        P("cache", "tp"),
        P("cache", None, "tp"),
        P("cache", None, "tp"),
        P("cache", None, "tp"),
        P("cache", None, "tp"),
        P("cache"),
        P("cache"),
        P("cache", None),
    )
    return jax.shard_map(
        shards,
        mesh=mesh,
        in_specs=placed,
        out_specs=(
            P("cache", "tp"),
            P("cache", "tp"),
            P("cache", None, "tp"),
            P("cache", None, "tp"),
        ),
        check_vma=False,
    )
```

```python
import functools
import math

import jax
import jax.numpy as jnp
from jax import lax
from jax.experimental import pallas as pl
from jax.experimental.pallas import tpu as pltpu
from jax.sharding import PartitionSpec as P

HEAD_DIM = 128
KVB = 128
LANES = 128
BF = jnp.bfloat16
F32 = jnp.float32
I32 = jnp.int32
VMEM = pltpu.VMEM
SMEM = pltpu.SMEM
MIB = 1 << 20


def params(mib=58):
    return pltpu.CompilerParams(vmem_limit_bytes=mib * MIB)


def in_vmem(count):
    return [pl.BlockSpec(memory_space=VMEM) for _ in range(count)]


def in_smem(count):
    return [pl.BlockSpec(memory_space=SMEM) for _ in range(count)]


def in_hbm(count):
    return [pl.BlockSpec(memory_space=pltpu.HBM) for _ in range(count)]


def pin(*arrays):
    return [pltpu.with_memory_space_constraint(a, pltpu.HBM) for a in arrays]


def whole(*arrays):
    return [
        pl.BlockSpec(a.shape, lambda i, n=len(a.shape): (0,) * n, pipeline_mode=pl.Buffered(1))
        for a in arrays
    ]


def ask_kernel(entry_ref, block_ref, length_ref, rank_ref, out_ref, plan_ref, *, slots):
    shape = out_ref.shape
    count = entry_ref.shape[0]
    owner_of = lax.broadcasted_iota(I32, shape, 0)
    table = jnp.full(shape, -1, I32)
    for r in range(count):
        owner = lax.div(entry_ref[r], slots)
        plan_ref[r] = owner
        plan_ref[count + r] = length_ref[0, r]
        plan_ref[2 * count + r] = block_ref[r]
        table = jnp.where(owner_of == owner, entry_ref[r] - owner * slots, table)
    plan_ref[3 * count] = rank_ref[0]
    out_ref[...] = table


def ask(hit_entry, hit_blocks, seg_lengths, rank, slots, owner_count):
    return pl.pallas_call(
        functools.partial(ask_kernel, slots=slots),
        in_specs=in_smem(4),
        out_specs=in_vmem(1) + in_smem(1),
        out_shape=[
            jax.ShapeDtypeStruct((owner_count, 1, LANES), I32),
            jax.ShapeDtypeStruct((3 * hit_entry.shape[0] + 1,), I32),
        ],
        compiler_params=params(),
    )(hit_entry, hit_blocks, seg_lengths, rank)


def tiles_kernel(conv_ref, state_ref, out_ref, hold, tails):
    entries, states, channels = state_ref.shape
    slots = conv_ref.shape[1]
    groups = channels // LANES
    conv_rows = 3 * groups
    first = pl.program_id(0) * entries

    @pl.when(first == 0)
    def _():
        for i in range(3):
            for j in range(groups):
                tails[pl.ds(i * groups + j, slots, stride=conv_rows), :] = conv_ref[
                    i, :, j * LANES : (j + 1) * LANES
                ].astype(F32)

    for e in range(entries):
        for low in range(0, states, 8):
            for j in range(groups):
                hold[pl.ds(low * groups + j, 8, stride=groups), :] = state_ref[
                    e, low : low + 8, j * LANES : (j + 1) * LANES
                ]
        place = pl.multiple_of((first + e) * conv_rows, conv_rows)
        out_ref[e, 0:conv_rows, :] = tails[pl.ds(place, conv_rows), :].astype(BF)
        out_ref[e, conv_rows:, :] = hold[...].astype(BF)


def entry_tiles(conv_rows, store_state):
    slots, states, channels = store_state.shape
    rows = states * channels // LANES
    tail_rows = 3 * channels // LANES
    step = 4
    return pl.pallas_call(
        tiles_kernel,
        grid=(slots // step,),
        in_specs=whole(conv_rows)
        + [pl.BlockSpec((step, states, channels), lambda i: (i, 0, 0))],
        out_specs=pl.BlockSpec((step, tail_rows + rows, LANES), lambda i: (i, 0, 0)),
        out_shape=jax.ShapeDtypeStruct((slots, tail_rows + rows, LANES), BF),
        scratch_shapes=[VMEM((rows, LANES), F32), VMEM((slots * tail_rows, LANES), F32)],
        compiler_params=params(16),
    )(*pin(conv_rows, store_state))


def pick_kernel(count, asked_ref, *refs):
    sources, (_, out_ref, stage, sems) = refs[:count], refs[count:]
    blocks = out_ref.shape[0]
    lows = [sum(s.shape[1] for s in sources[:n]) for n in range(count + 1)]

    def load(i, n):
        return pltpu.make_async_copy(
            sources[n].at[jnp.maximum(asked_ref[i, 0], 0)],
            stage.at[i, pl.ds(lows[n], sources[n].shape[1])],
            sems.at[0, i, n],
        )

    def store(i, n):
        part = pl.ds(lows[n], sources[n].shape[1])
        return pltpu.make_async_copy(stage.at[i, part], out_ref.at[i, part], sems.at[1, i, n])

    def each(act):
        for i in range(blocks):

            @pl.when(asked_ref[i, 0] >= 0)
            def _():
                for n in range(count):
                    act(i, n)

    def turn(i, n):
        load(i, n).wait()
        store(i, n).start()

    each(lambda i, n: load(i, n).start())
    each(turn)
    each(lambda i, n: store(i, n).wait())


def pick(asked, after, *sources):
    blocks = asked.shape[0]
    rows = sum(s.shape[1] for s in sources)
    return pl.pallas_call(
        functools.partial(pick_kernel, len(sources)),
        in_specs=in_smem(1) + in_hbm(len(sources)) + [pl.BlockSpec(memory_space=pl.ANY)],
        out_specs=in_hbm(1)[0],
        out_shape=pltpu.HBM((blocks, rows, LANES), BF),
        scratch_shapes=[
            VMEM((blocks, rows, LANES), BF),
            pltpu.SemaphoreType.DMA((2, blocks, len(sources))),
        ],
        compiler_params=params(32),
    )(asked, *sources, after)


def pick_tiles_kernel(part, asked_ref, tiles_ref, out_ref, sems):
    def act(name):
        for i in range(out_ref.shape[0]):
            slot = asked_ref[i, 0]

            @pl.when(slot >= 0)
            def _():
                getattr(pltpu.make_async_copy(tiles_ref.at[slot], out_ref.at[i], sems.at[i]), name)()

            @pl.when(slot < 0)
            def _():
                few = pl.ds(0, part)
                getattr(
                    pltpu.make_async_copy(tiles_ref.at[0, few], out_ref.at[i, few], sems.at[i]), name
                )()

    act("start")
    act("wait")


def pick_tiles(asked, tiles, part):
    blocks = asked.shape[0]
    return pl.pallas_call(
        functools.partial(pick_tiles_kernel, part),
        in_specs=in_smem(1) + in_vmem(1),
        out_specs=in_hbm(1)[0],
        out_shape=pltpu.HBM((blocks,) + tiles.shape[1:], BF),
        scratch_shapes=[pltpu.SemaphoreType.DMA((blocks,))],
        compiler_params=params(4),
    )(asked, tiles)


def bring_kernel(count, after_ref, *refs):
    sources, targets = refs[:count], refs[count + 1 : 2 * count + 1]
    decay_ref, tile_ref, sems = refs[count], refs[2 * count + 1], refs[2 * count + 2]
    copies = [
        pltpu.make_async_copy(source, target, sems.at[n])
        for n, (source, target) in enumerate(zip(sources, targets))
    ]
    for copy in copies:
        copy.start()
    states, channels = decay_ref.shape
    groups = channels // LANES
    for low in range(0, states, 8):
        for j in range(groups):
            tile_ref[pl.ds(low * groups + j, 8, stride=groups), :] = decay_ref[
                low : low + 8, j * LANES : (j + 1) * LANES
            ] * (-math.log2(math.e))
    for copy in copies:
        copy.wait()


def bring(after, decay_rates, *arrays):
    states, channels = decay_rates.shape
    return pl.pallas_call(
        functools.partial(bring_kernel, len(arrays)),
        in_specs=in_hbm(1 + len(arrays)) + in_vmem(1),
        out_specs=in_vmem(len(arrays) + 1),
        out_shape=[jax.ShapeDtypeStruct(a.shape, a.dtype) for a in arrays]
        + [jax.ShapeDtypeStruct((states * channels // LANES, LANES), F32)],
        scratch_shapes=[pltpu.SemaphoreType.DMA((len(arrays),))],
        compiler_params=params(4),
    )(*pin(after, *arrays), decay_rates)


def conv_kernel(plan_ref, x_ref, choose_ref, weight_ref, in_ref, bc_ref, got_ref, *refs):
    parts, (mixed_ref, tail_ref), (source, wide, total, tails, came, sem) = (
        refs[:8], refs[8:10], refs[10:]
    )
    tokens, channels = x_ref.shape
    groups = channels // LANES
    olds = got_ref.shape[0] * 3
    rank_dim = in_ref.shape[1]
    chunk = source.shape[1]
    copy = pltpu.make_async_copy(got_ref.at[:, pl.ds(0, 3 * groups)], came, sem)
    copy.start()
    source[tokens + olds :, :] = jnp.zeros((source.shape[0] - tokens - olds, chunk), BF)
    total[...] = jnp.zeros(total.shape, F32)
    copy.wait()
    wide[...] = came[...].reshape(olds * groups, LANES).astype(F32)
    for low in range(0, channels, chunk):
        cut = slice(low, low + chunk)
        source[0:tokens, :] = x_ref[:, cut]
        for j in range(chunk // LANES):
            source[tokens : tokens + olds, j * LANES : (j + 1) * LANES] = wide[
                pl.ds(low // LANES + j, olds, stride=groups), :
            ].astype(BF)
        taken = jnp.dot(choose_ref[...], source[...], preferred_element_type=F32)
        running = weight_ref[3:4, cut] * x_ref[:, cut].astype(F32)
        for lag in range(1, 4):
            running = (
                running
                + weight_ref[3 - lag : 4 - lag, cut] * taken[(lag - 1) * tokens : lag * tokens]
            )
        mixed = (running / (1.0 + jnp.exp(-running))).astype(BF)
        mixed_ref[:, cut] = mixed
        for j in range(chunk // LANES):
            tails[pl.ds(low // LANES + j, olds, stride=groups), :] = taken[
                3 * tokens :, j * LANES : (j + 1) * LANES
            ]
        maps = lax.dot_general(
            mixed, bc_ref[:, cut], (((1,), (1,)), ((), ())), preferred_element_type=F32
        )
        total[:, 0:rank_dim] += jnp.dot(mixed, in_ref[cut, :], preferred_element_type=F32)
        total[:, rank_dim : rank_dim + maps.shape[1]] += maps
    tail_ref[...] = tails[...].reshape(tail_ref.shape).astype(BF)
    share, width = tokens // 8, total.shape[1]
    for turn, part in enumerate(parts):
        place = lax.rem(plan_ref[plan_ref.shape[0] - 1] + turn, 8) * share
        rows = total[pl.ds(pl.multiple_of(place, share), share), :]
        high = rows.astype(BF)
        part[:, 0:width] = high
        part[:, width:] = (rows[:, rank_dim:] - high[:, rank_dim:].astype(F32)).astype(BF)


def conv_project(plan, x_rows, choose, conv_weight, dt_in_weight, bc_weight, got):
    tokens, channels = x_rows.shape
    width = dt_in_weight.shape[1] + LANES
    conv_rows = 3 * channels // LANES
    tail_rows = got.shape[0] * conv_rows
    return pl.pallas_call(
        conv_kernel,
        in_specs=in_smem(1) + in_vmem(5) + [pl.BlockSpec(memory_space=pl.ANY)],
        out_specs=in_vmem(10),
        out_shape=[jax.ShapeDtypeStruct((tokens // 8, width + LANES), BF)] * 8
        + [
            jax.ShapeDtypeStruct((tokens, channels), BF),
            jax.ShapeDtypeStruct((got.shape[0], conv_rows, LANES), BF),
        ],
        scratch_shapes=[
            VMEM((choose.shape[1], min(512, channels)), BF),
            VMEM((tail_rows, LANES), F32),
            VMEM((tokens, width), F32),
            VMEM((tail_rows, LANES), F32),
            VMEM((got.shape[0], conv_rows, LANES), BF),
            pltpu.SemaphoreType.DMA,
        ],
        compiler_params=params(24),
    )(plan, x_rows, choose, conv_weight, dt_in_weight, bc_weight, got)


def sum_kernel(*refs):
    out_ref = refs[-1]
    total, rest = (
        functools.reduce(jnp.add, [part[:, cut].astype(F32) for part in refs[:-1]])
        for cut in (slice(0, -LANES), slice(-LANES, None))
    )
    rank_dim = total.shape[1] - LANES
    maps = total[:, rank_dim:] + rest
    high = maps.astype(BF)
    out_ref[:, 0:rank_dim] = total[:, 0:rank_dim].astype(BF)
    out_ref[:, rank_dim : rank_dim + LANES] = high
    out_ref[:, rank_dim + LANES :] = (maps - high.astype(F32)).astype(BF)


def sum_parts(parts):
    rows, width = parts[0].shape
    return pl.pallas_call(
        sum_kernel,
        in_specs=in_vmem(len(parts)),
        out_specs=in_vmem(1)[0],
        out_shape=jax.ShapeDtypeStruct((rows, width), BF),
        compiler_params=params(8),
    )(*parts)


def scan_kernel(states, count, plan_ref, *refs):
    pieces = refs[0:8]
    mixed_ref, weight_ref, bias_ref, skip_ref, tail_ref, decays, start_ref = refs[8:15]
    out_ref, back_ref = refs[15:17]
    low_dt, maps, turned, map_smem, rates, drives, sums, begun, ready, sem, sems = refs[17:]
    tokens, channels = mixed_ref.shape
    groups = channels // LANES
    share = tokens // 8
    rank_dim = weight_ref.shape[0]
    rank = plan_ref[3 * count]
    conv_rows = 3 * groups
    state_rows = states * groups

    def receive(r):
        return pltpu.make_async_copy(
            start_ref.at[plan_ref[r], pl.ds(conv_rows, state_rows)], begun.at[r], sems.at[r, 0]
        )

    def send_tail(r):
        owner = plan_ref[r]
        return pltpu.make_async_copy(
            tail_ref.at[owner], back_ref.at[owner, pl.ds(0, conv_rows)], sems.at[r, 1]
        )

    def send_state(r):
        return pltpu.make_async_copy(
            ready.at[r], back_ref.at[plan_ref[r], pl.ds(conv_rows, state_rows)], sems.at[r, 2]
        )

    for step, piece in enumerate(pieces):
        place = pl.multiple_of(lax.rem(rank + 8 - step, 8) * share, share)
        low_dt[pl.ds(place, share), :] = piece[:, 0:rank_dim]
        maps[pl.ds(place, share), :] = piece[:, rank_dim : rank_dim + LANES].astype(F32) + piece[
            :, rank_dim + LANES :
        ].astype(F32)
    turned[...] = jnp.transpose(maps[...])[0 : 2 * states, :]
    copy = pltpu.make_async_copy(turned, map_smem, sem)
    copy.start()
    for r in range(count):
        receive(r).start()
    chunk = min(512, channels)
    for low in range(0, channels, chunk):
        cut = slice(low, low + chunk)
        raw = (
            jnp.dot(low_dt[...], weight_ref[:, cut], preferred_element_type=F32) + bias_ref[:, cut]
        )
        rate = jnp.maximum(raw, 0.0) + jnp.log1p(jnp.exp(-jnp.abs(raw)))
        drive = rate * mixed_ref[:, cut].astype(F32)
        for j in range(chunk // LANES):
            rows = pl.ds(low // LANES + j, tokens, stride=groups)
            rates[rows, :] = rate[:, j * LANES : (j + 1) * LANES]
            drives[rows, :] = drive[:, j * LANES : (j + 1) * LANES]
    copy.wait()

    def segment(r, begin):
        finish = begin + plan_ref[count + r]
        receive(r).wait()
        held = tuple(
            begun[r, n * groups : (n + 1) * groups, :].astype(F32) for n in range(states)
        )

        def token(t, held):
            place = pl.ds(pl.multiple_of(t * groups, groups), groups)
            rate, drive = rates[place, :], drives[place, :]
            total, later = None, []
            for n in range(states):
                decay = jnp.exp2(rate * decays[n * groups : (n + 1) * groups, :])
                value = decay * held[n] + drive * map_smem[n, t]
                term = value * map_smem[states + n, t]
                total = term if total is None else total + term
                later.append(value)
            sums[place, :] = total
            return tuple(later)

        held = lax.fori_loop(begin, finish, token, held)
        for n in range(states):
            ready[r, n * groups : (n + 1) * groups, :] = held[n].astype(BF)
        send_state(r).start()
        send_tail(r).start()
        return finish

    lax.fori_loop(0, count, segment, jnp.int32(0))
    for j in range(groups):
        cut = slice(j * LANES, (j + 1) * LANES)
        out_ref[:, cut] = (
            sums[pl.ds(j, tokens, stride=groups), :]
            + skip_ref[:, cut] * mixed_ref[:, cut].astype(F32)
        ).astype(BF)
    for r in range(count):
        send_tail(r).wait()
        send_state(r).wait()


def scan(plan, pieces, mixed, dt_weight, dt_bias, skip_gain, tails, decays, got):
    tokens, channels = mixed.shape
    groups = channels // LANES
    state_rows = decays.shape[0]
    count = (plan.shape[0] - 1) // 3
    return pl.pallas_call(
        functools.partial(scan_kernel, state_rows // groups, count),
        in_specs=in_smem(1) + in_vmem(14) + [pl.BlockSpec(memory_space=pl.ANY)],
        out_specs=in_vmem(1) + in_hbm(1),
        out_shape=[
            jax.ShapeDtypeStruct((tokens, channels), BF),
            pltpu.HBM(got.shape, BF),
        ],
        scratch_shapes=[
            VMEM((tokens, dt_weight.shape[0]), BF),
            VMEM((tokens, LANES), F32),
            VMEM((2 * state_rows // groups, tokens), F32),
            SMEM((2 * state_rows // groups, tokens), F32),
            VMEM((tokens * groups, LANES), F32),
            VMEM((tokens * groups, LANES), F32),
            VMEM((tokens * groups, LANES), F32),
            VMEM((count, state_rows, LANES), BF),
            VMEM((count, state_rows, LANES), BF),
            pltpu.SemaphoreType.DMA,
            pltpu.SemaphoreType.DMA((count, 3)),
        ],
        compiler_params=params(24),
    )(plan, *pieces, mixed, dt_weight, dt_bias, skip_gain, tails, decays, got)


def attend_kernel(count, plan_ref, q_ref, k_ref, v_ref, got_ref, out_ref, rows_q, rows_o, prefix_ref, sems):
    tokens = q_ref.shape[0]
    heads = q_ref.shape[1] // HEAD_DIM
    prefix = prefix_ref.shape[1] // 2

    def receive(r):
        return pltpu.make_async_copy(got_ref.at[plan_ref[r]], prefix_ref.at[r], sems.at[r])

    for r in range(count):
        receive(r).start()
    for h in range(heads):
        rows_q[h * tokens : (h + 1) * tokens, :] = q_ref[:, h * HEAD_DIM : (h + 1) * HEAD_DIM]
    contract = (((1,), (1,)), ((), ()))
    scale = HEAD_DIM**-0.5
    many = heads * tokens
    new_scores = lax.dot_general(
        rows_q[...], k_ref[...], contract, preferred_element_type=F32
    ) * scale
    query_of = lax.rem(lax.broadcasted_iota(I32, (many, tokens), 0), tokens)
    key_of = lax.broadcasted_iota(I32, (many, tokens), 1)
    new_scores = jnp.where(key_of <= query_of, new_scores, -1e30)
    token_of = lax.rem(lax.broadcasted_iota(I32, (many, HEAD_DIM), 0), tokens)
    place_of = lax.broadcasted_iota(I32, (many, prefix), 1)
    rows_o[...] = jnp.zeros((many, HEAD_DIM), F32)

    def request(r, begin):
        finish = begin + plan_ref[count + r]
        live = plan_ref[2 * count + r] * KVB
        receive(r).wait()
        old = lax.dot_general(
            rows_q[...], prefix_ref[r, 0:prefix, :], contract, preferred_element_type=F32
        ) * scale
        old = jnp.where(place_of < live, old, -1e30)
        new = jnp.where(key_of >= begin, new_scores, -1e30)
        highest = jnp.maximum(
            jnp.max(old, axis=1, keepdims=True), jnp.max(new, axis=1, keepdims=True)
        )
        old, new = jnp.exp(old - highest), jnp.exp(new - highest)
        total = jnp.sum(old, axis=1, keepdims=True) + jnp.sum(new, axis=1, keepdims=True)
        inverse = 1.0 / total
        result = jnp.dot(
            (old * inverse).astype(BF), prefix_ref[r, prefix:, :], preferred_element_type=F32
        ) + jnp.dot((new * inverse).astype(BF), v_ref[...], preferred_element_type=F32)
        mine = (token_of >= begin) & (token_of < finish)
        rows_o[...] = jnp.where(mine, result, rows_o[...])
        return finish

    lax.fori_loop(0, count, request, jnp.int32(0))
    for h in range(heads):
        out_ref[:, h * HEAD_DIM : (h + 1) * HEAD_DIM] = rows_o[
            h * tokens : (h + 1) * tokens, :
        ].astype(BF)


def attend(plan, queries, new_keys, new_values, got):
    tokens, width = queries.shape
    many = tokens * width // HEAD_DIM
    count = (plan.shape[0] - 1) // 3
    return pl.pallas_call(
        functools.partial(attend_kernel, count),
        grid=(1,),
        in_specs=in_smem(1) + whole(queries, new_keys, new_values) + in_hbm(1),
        out_specs=pl.BlockSpec((tokens, width), lambda i: (0, 0)),
        out_shape=jax.ShapeDtypeStruct((tokens, width), BF),
        scratch_shapes=[
            VMEM((many, HEAD_DIM), BF),
            VMEM((many, HEAD_DIM), F32),
            VMEM((count,) + got.shape[1:], BF),
            pltpu.SemaphoreType.DMA((count,)),
        ],
        compiler_params=params(),
    )(plan, *pin(queries, new_keys, new_values, got))


def write_kernel(
    asked_ref, conv_ref, store_ref, back_ref, conv_out, out_ref, source, hold, stage, tails, sems
):
    slots, states, channels = out_ref.shape
    groups = channels // LANES
    rows = states * groups
    conv_rows = 3 * groups
    for s in range(slots):
        source[s] = -1
    for row in range(asked_ref.shape[0]):
        slot = asked_ref[row, 0]

        @pl.when(slot >= 0)
        def _():
            source[slot] = row

    def kept(s):
        return pltpu.make_async_copy(store_ref.at[s], stage.at[s], sems.at[slots + s])

    def changed(s):
        return pltpu.make_async_copy(stage.at[s], out_ref.at[s], sems.at[s])

    for s in range(slots):

        @pl.when(source[s] < 0)
        def _():
            kept(s).start()
            tails[s * conv_rows : (s + 1) * conv_rows, :] = jnp.zeros((conv_rows, LANES), F32)
    landed = jnp.zeros((slots, LANES), I32)
    slot_of = lax.broadcasted_iota(I32, (slots, LANES), 0)
    for s in range(slots):
        row = source[s]
        landed = jnp.where(slot_of == s, row + 1, landed)

        @pl.when(row >= 0)
        def _():
            hold[s % 2] = back_ref[row, conv_rows:, :].astype(F32)
            for low in range(0, states, 8):
                for j in range(groups):
                    stage[s, low : low + 8, j * LANES : (j + 1) * LANES] = hold[
                        s % 2, pl.ds(low * groups + j, 8, stride=groups), :
                    ]
            changed(s).start()
            tails[s * conv_rows : (s + 1) * conv_rows, :] = back_ref[row, 0:conv_rows, :].astype(F32)

    for i in range(3):
        for j in range(groups):
            cut = slice(j * LANES, (j + 1) * LANES)
            fresh = tails[pl.ds(i * groups + j, slots, stride=3 * groups), :]
            conv_out[i, :, cut] = jnp.where(
                landed > 0, fresh, conv_ref[i, :, cut].astype(F32)
            ).astype(BF)
    for s in range(slots):

        @pl.when(source[s] < 0)
        def _():
            kept(s).wait()
            changed(s).start()

    for s in range(slots):
        changed(s).wait()


def write_store(asked, store_state, conv_rows, back):
    slots, states, channels = store_state.shape
    groups = channels // LANES
    return pl.pallas_call(
        write_kernel,
        grid=(1,),
        in_specs=in_smem(1) + whole(conv_rows) + in_hbm(1) + in_vmem(1),
        out_specs=whole(conv_rows) + in_hbm(1),
        out_shape=[
            jax.ShapeDtypeStruct(conv_rows.shape, BF),
            jax.ShapeDtypeStruct((slots, states, channels), F32),
        ],
        scratch_shapes=[
            SMEM((slots,), I32),
            VMEM((2, states * groups, LANES), F32),
            VMEM((slots, states, channels), F32),
            VMEM((slots * 3 * groups, LANES), F32),
            pltpu.SemaphoreType.DMA((2 * slots,)),
        ],
        compiler_params=params(24),
    )(asked, *pin(conv_rows, store_state), back)


def exchange(blocks, axis):
    return lax.all_to_all(blocks, axis, split_axis=0, concat_axis=0, tiled=True)


def choose_matrix(lengths, owners, tokens, owner_count, width):
    ends = jnp.cumsum(lengths, dtype=I32)
    starts = ends - lengths
    places = jnp.arange(tokens, dtype=I32)
    member = (places[:, None] >= starts[None, :]) & (places[:, None] < ends[None, :])
    offset = places - jnp.sum(jnp.where(member, starts[None, :], 0), axis=1, dtype=I32)
    owner = jnp.sum(jnp.where(member, owners[None, :], 0), axis=1, dtype=I32)
    lags = jnp.arange(1, 4, dtype=I32)[:, None]
    lagged = jnp.where(
        offset[None, :] >= lags,
        places[None, :] - lags,
        tokens + owner[None, :] * 3 + 3 + offset[None, :] - lags,
    )
    owner_ids = jnp.arange(owner_count, dtype=I32)
    served = owner_ids[:, None] == owners[None, :]
    ends_of = jnp.sum(jnp.where(served, ends[None, :], 0), axis=1, dtype=I32)[:, None]
    length_of = jnp.sum(jnp.where(served, lengths[None, :], 0), axis=1, dtype=I32)[:, None]
    rows = jnp.arange(3, dtype=I32)[None, :]
    tails = jnp.where(
        length_of + rows >= 3, ends_of - 3 + rows, tokens + owner_ids[:, None] * 3 + length_of + rows
    )
    tails = jnp.where(length_of > 0, tails, width)
    column = jnp.concatenate([lagged.reshape(-1), tails.reshape(-1)])
    return (column[:, None] == jnp.arange(width, dtype=I32)[None, :]).astype(BF)


def shards(
    x_in,
    conv_weight,
    dt_in_weight,
    bc_weight,
    dt_weight,
    dt_bias,
    decay_rates,
    skip_gain,
    queries,
    new_keys,
    new_values,
    store_state,
    store_conv,
    store_keys,
    store_values,
    hit_entry,
    hit_blocks,
    seg_lengths,
):
    owner_count = lax.axis_size("cache")
    tp_count = lax.axis_size("tp")
    rank = lax.axis_index("tp").astype(I32)[None]
    slot_count, states, channels = store_state.shape
    groups = channels // LANES
    tokens = x_in.shape[0]
    lengths = seg_lengths[0]
    table, plan = ask(hit_entry, hit_blocks, seg_lengths, rank, slot_count, owner_count)
    asked = exchange(table, "cache")[:, 0, :]

    conv_store = store_conv.transpose(1, 0, 2)
    tiles = entry_tiles(conv_store, store_state)
    sent = pick_tiles(asked, tiles, 3 * groups)
    width = tokens + -(-3 * owner_count // LANES) * LANES
    choose = choose_matrix(lengths, hit_entry // slot_count, tokens, owner_count, width)
    x_rows, choose, taps, dt_in, bc_in, dt_out, bias, skip, decays = bring(
        sent, decay_rates, x_in, choose, conv_weight, dt_in_weight, bc_weight, dt_weight,
        dt_bias[None, :], skip_gain[None, :],
    )
    got = exchange(sent, "cache")
    *parts, mixed, tails = conv_project(plan, x_rows, choose, taps, dt_in, bc_in, got)

    def turned(step, value):
        return lax.ppermute(value, "tp", [(k, (k + step) % tp_count) for k in range(tp_count)])

    parts = [parts[0]] + [turned(step, parts[step]) for step in range(1, tp_count)]
    summed = sum_parts(parts)
    pieces = [summed] + [turned(step, summed) for step in range(1, tp_count)]
    got_prefix = exchange(pick(asked, bias, *pin(store_keys, store_values)), "cache")

    mixer_out, back = scan(plan, pieces, mixed, dt_out, bias, skip, tails, decays, got)
    back = exchange(back, "cache")
    attn_out = attend(plan, queries, new_keys, new_values, got_prefix)
    conv_rows, new_state = write_store(asked, store_state, conv_store, back)
    return (mixer_out, attn_out, new_state, conv_rows.transpose(1, 0, 2))


def solution(mesh):
    placed = (
        P("cache", "tp"),
        P(None, "tp"),
        P("tp", None),
        P(None, "tp"),
        P(None, "tp"),
        P("tp"),
        P(None, "tp"),
        P("tp"),
        P("cache", "tp"),
        P("cache", "tp"),
        P("cache", "tp"),
        P("cache", None, "tp"),
        P("cache", None, "tp"),
        P("cache", None, "tp"),
        P("cache", None, "tp"),
        P("cache"),
        P("cache"),
        P("cache", None),
    )
    return jax.shard_map(
        shards,
        mesh=mesh,
        in_specs=placed,
        out_specs=(
            P("cache", "tp"),
            P("cache", "tp"),
            P("cache", None, "tp"),
            P("cache", None, "tp"),
        ),
        check_vma=False,
    )
```

```python
import functools
import math

import jax
import jax.numpy as jnp
from jax import lax
from jax.experimental import pallas as pl
from jax.experimental.pallas import tpu as pltpu
from jax.sharding import PartitionSpec as P

HEAD_DIM = 128
KVB = 128
LANES = 128
BF = jnp.bfloat16
F32 = jnp.float32
I32 = jnp.int32
VMEM = pltpu.VMEM
SMEM = pltpu.SMEM
MIB = 1 << 20


def params(mib=58):
    return pltpu.CompilerParams(vmem_limit_bytes=mib * MIB)


def in_vmem(count):
    return [pl.BlockSpec(memory_space=VMEM) for _ in range(count)]


def in_smem(count):
    return [pl.BlockSpec(memory_space=SMEM) for _ in range(count)]


def in_hbm(count):
    return [pl.BlockSpec(memory_space=pltpu.HBM) for _ in range(count)]


def pin(*arrays):
    return [pltpu.with_memory_space_constraint(a, pltpu.HBM) for a in arrays]


def whole(*arrays):
    return [
        pl.BlockSpec(a.shape, lambda i, n=len(a.shape): (0,) * n, pipeline_mode=pl.Buffered(1))
        for a in arrays
    ]


def ask_kernel(entry_ref, block_ref, length_ref, rank_ref, out_ref, plan_ref, *, slots):
    shape = out_ref.shape
    count = entry_ref.shape[0]
    owner_of = lax.broadcasted_iota(I32, shape, 0)
    table = jnp.full(shape, -1, I32)
    for r in range(count):
        owner = lax.div(entry_ref[r], slots)
        plan_ref[r] = owner
        plan_ref[count + r] = length_ref[0, r]
        plan_ref[2 * count + r] = block_ref[r]
        table = jnp.where(owner_of == owner, entry_ref[r] - owner * slots, table)
    plan_ref[3 * count] = rank_ref[0]
    out_ref[...] = table


def ask(hit_entry, hit_blocks, seg_lengths, rank, slots, owner_count):
    return pl.pallas_call(
        functools.partial(ask_kernel, slots=slots),
        in_specs=in_smem(4),
        out_specs=in_vmem(1) + in_smem(1),
        out_shape=[
            jax.ShapeDtypeStruct((owner_count, 1, LANES), I32),
            jax.ShapeDtypeStruct((3 * hit_entry.shape[0] + 1,), I32),
        ],
        compiler_params=params(),
    )(hit_entry, hit_blocks, seg_lengths, rank)


def tiles_kernel(conv_ref, state_ref, out_ref, hold, tails):
    entries, states, channels = state_ref.shape
    slots = conv_ref.shape[1]
    groups = channels // LANES
    conv_rows = 3 * groups
    first = pl.program_id(0) * entries

    @pl.when(first == 0)
    def _():
        for i in range(3):
            for j in range(groups):
                tails[pl.ds(i * groups + j, slots, stride=conv_rows), :] = conv_ref[
                    i, :, j * LANES : (j + 1) * LANES
                ].astype(F32)

    for e in range(entries):
        for low in range(0, states, 8):
            for j in range(groups):
                hold[pl.ds(low * groups + j, 8, stride=groups), :] = state_ref[
                    e, low : low + 8, j * LANES : (j + 1) * LANES
                ]
        place = pl.multiple_of((first + e) * conv_rows, conv_rows)
        out_ref[e, 0:conv_rows, :] = tails[pl.ds(place, conv_rows), :].astype(BF)
        out_ref[e, conv_rows:, :] = hold[...].astype(BF)


def entry_tiles(conv_rows, store_state):
    slots, states, channels = store_state.shape
    rows = states * channels // LANES
    tail_rows = 3 * channels // LANES
    step = 4
    return pl.pallas_call(
        tiles_kernel,
        grid=(slots // step,),
        in_specs=whole(conv_rows)
        + [pl.BlockSpec((step, states, channels), lambda i: (i, 0, 0))],
        out_specs=pl.BlockSpec((step, tail_rows + rows, LANES), lambda i: (i, 0, 0)),
        out_shape=jax.ShapeDtypeStruct((slots, tail_rows + rows, LANES), BF),
        scratch_shapes=[VMEM((rows, LANES), F32), VMEM((slots * tail_rows, LANES), F32)],
        compiler_params=params(8),
    )(*pin(conv_rows, store_state))


def pick_kernel(count, asked_ref, *refs):
    sources, (_, out_ref, stage, sems) = refs[:count], refs[count:]
    blocks = out_ref.shape[0]
    lows = [sum(s.shape[1] for s in sources[:n]) for n in range(count + 1)]

    def load(i, n):
        return pltpu.make_async_copy(
            sources[n].at[jnp.maximum(asked_ref[i, 0], 0)],
            stage.at[i, pl.ds(lows[n], sources[n].shape[1])],
            sems.at[0, i, n],
        )

    def store(i, n):
        part = pl.ds(lows[n], sources[n].shape[1])
        return pltpu.make_async_copy(stage.at[i, part], out_ref.at[i, part], sems.at[1, i, n])

    def each(act):
        for i in range(blocks):

            @pl.when(asked_ref[i, 0] >= 0)
            def _():
                for n in range(count):
                    act(i, n)

    def turn(i, n):
        load(i, n).wait()
        store(i, n).start()

    each(lambda i, n: load(i, n).start())
    each(turn)
    each(lambda i, n: store(i, n).wait())


def pick(asked, after, *sources):
    blocks = asked.shape[0]
    rows = sum(s.shape[1] for s in sources)
    return pl.pallas_call(
        functools.partial(pick_kernel, len(sources)),
        in_specs=in_smem(1) + in_hbm(len(sources)) + [pl.BlockSpec(memory_space=pl.ANY)],
        out_specs=in_hbm(1)[0],
        out_shape=pltpu.HBM((blocks, rows, LANES), BF),
        scratch_shapes=[
            VMEM((blocks, rows, LANES), BF),
            pltpu.SemaphoreType.DMA((2, blocks, len(sources))),
        ],
        compiler_params=params(6),
    )(asked, *sources, after)


def pick_tiles_kernel(part, asked_ref, tiles_ref, out_ref, sems):
    def act(name):
        for i in range(out_ref.shape[0]):
            slot = asked_ref[i, 0]

            @pl.when(slot >= 0)
            def _():
                getattr(pltpu.make_async_copy(tiles_ref.at[slot], out_ref.at[i], sems.at[i]), name)()

            @pl.when(slot < 0)
            def _():
                few = pl.ds(0, part)
                getattr(
                    pltpu.make_async_copy(tiles_ref.at[0, few], out_ref.at[i, few], sems.at[i]), name
                )()

    act("start")
    act("wait")


def pick_tiles(asked, tiles, part):
    blocks = asked.shape[0]
    return pl.pallas_call(
        functools.partial(pick_tiles_kernel, part),
        in_specs=in_smem(1) + in_vmem(1),
        out_specs=in_hbm(1)[0],
        out_shape=pltpu.HBM((blocks,) + tiles.shape[1:], BF),
        scratch_shapes=[pltpu.SemaphoreType.DMA((blocks,))],
        compiler_params=params(4),
    )(asked, tiles)


def bring_kernel(count, after_ref, *refs):
    sources, targets = refs[:count], refs[count + 1 : 2 * count + 1]
    decay_ref, tile_ref, sems = refs[count], refs[2 * count + 1], refs[2 * count + 2]
    copies = [
        pltpu.make_async_copy(source, target, sems.at[n])
        for n, (source, target) in enumerate(zip(sources, targets))
    ]
    for copy in copies:
        copy.start()
    states, channels = decay_ref.shape
    groups = channels // LANES
    for low in range(0, states, 8):
        for j in range(groups):
            tile_ref[pl.ds(low * groups + j, 8, stride=groups), :] = decay_ref[
                low : low + 8, j * LANES : (j + 1) * LANES
            ] * (-math.log2(math.e))
    for copy in copies:
        copy.wait()


def bring(after, decay_rates, *arrays):
    states, channels = decay_rates.shape
    return pl.pallas_call(
        functools.partial(bring_kernel, len(arrays)),
        in_specs=in_hbm(1 + len(arrays)) + in_vmem(1),
        out_specs=in_vmem(len(arrays) + 1),
        out_shape=[jax.ShapeDtypeStruct(a.shape, a.dtype) for a in arrays]
        + [jax.ShapeDtypeStruct((states * channels // LANES, LANES), F32)],
        scratch_shapes=[pltpu.SemaphoreType.DMA((len(arrays),))],
        compiler_params=params(4),
    )(*pin(after, *arrays), decay_rates)


def conv_kernel(plan_ref, x_ref, choose_ref, weight_ref, in_ref, bc_ref, got_ref, *refs):
    parts, (mixed_ref, tail_ref), (source, wide, total, tails, came, sem) = (
        refs[:8], refs[8:10], refs[10:]
    )
    tokens, channels = x_ref.shape
    groups = channels // LANES
    olds = got_ref.shape[0] * 3
    rank_dim = in_ref.shape[1]
    chunk = source.shape[1]
    copy = pltpu.make_async_copy(got_ref.at[:, pl.ds(0, 3 * groups)], came, sem)
    copy.start()
    source[tokens + olds :, :] = jnp.zeros((source.shape[0] - tokens - olds, chunk), BF)
    total[...] = jnp.zeros(total.shape, F32)
    copy.wait()
    wide[...] = came[...].reshape(olds * groups, LANES).astype(F32)
    for low in range(0, channels, chunk):
        cut = slice(low, low + chunk)
        source[0:tokens, :] = x_ref[:, cut]
        for j in range(chunk // LANES):
            source[tokens : tokens + olds, j * LANES : (j + 1) * LANES] = wide[
                pl.ds(low // LANES + j, olds, stride=groups), :
            ].astype(BF)
        taken = jnp.dot(choose_ref[...], source[...], preferred_element_type=F32)
        running = weight_ref[3:4, cut] * x_ref[:, cut].astype(F32)
        for lag in range(1, 4):
            running = (
                running
                + weight_ref[3 - lag : 4 - lag, cut] * taken[(lag - 1) * tokens : lag * tokens]
            )
        mixed = (running / (1.0 + jnp.exp(-running))).astype(BF)
        mixed_ref[:, cut] = mixed
        for j in range(chunk // LANES):
            tails[pl.ds(low // LANES + j, olds, stride=groups), :] = taken[
                3 * tokens :, j * LANES : (j + 1) * LANES
            ]
        maps = lax.dot_general(
            mixed, bc_ref[:, cut], (((1,), (1,)), ((), ())), preferred_element_type=F32
        )
        total[:, 0:rank_dim] += jnp.dot(mixed, in_ref[cut, :], preferred_element_type=F32)
        total[:, rank_dim : rank_dim + maps.shape[1]] += maps
    tail_ref[...] = tails[...].reshape(tail_ref.shape).astype(BF)
    share, width = tokens // 8, total.shape[1]
    for turn, part in enumerate(parts):
        place = lax.rem(plan_ref[plan_ref.shape[0] - 1] + turn, 8) * share
        rows = total[pl.ds(pl.multiple_of(place, share), share), :]
        high = rows.astype(BF)
        part[:, 0:width] = high
        part[:, width:] = (rows[:, rank_dim:] - high[:, rank_dim:].astype(F32)).astype(BF)


def conv_project(plan, x_rows, choose, conv_weight, dt_in_weight, bc_weight, got):
    tokens, channels = x_rows.shape
    width = dt_in_weight.shape[1] + LANES
    conv_rows = 3 * channels // LANES
    tail_rows = got.shape[0] * conv_rows
    return pl.pallas_call(
        conv_kernel,
        in_specs=in_smem(1) + in_vmem(5) + [pl.BlockSpec(memory_space=pl.ANY)],
        out_specs=in_vmem(10),
        out_shape=[jax.ShapeDtypeStruct((tokens // 8, width + LANES), BF)] * 8
        + [
            jax.ShapeDtypeStruct((tokens, channels), BF),
            jax.ShapeDtypeStruct((got.shape[0], conv_rows, LANES), BF),
        ],
        scratch_shapes=[
            VMEM((choose.shape[1], min(512, channels)), BF),
            VMEM((tail_rows, LANES), F32),
            VMEM((tokens, width), F32),
            VMEM((tail_rows, LANES), F32),
            VMEM((got.shape[0], conv_rows, LANES), BF),
            pltpu.SemaphoreType.DMA,
        ],
        compiler_params=params(24),
    )(plan, x_rows, choose, conv_weight, dt_in_weight, bc_weight, got)


def sum_kernel(*refs):
    out_ref = refs[-1]
    total, rest = (
        functools.reduce(jnp.add, [part[:, cut].astype(F32) for part in refs[:-1]])
        for cut in (slice(0, -LANES), slice(-LANES, None))
    )
    rank_dim = total.shape[1] - LANES
    maps = total[:, rank_dim:] + rest
    high = maps.astype(BF)
    out_ref[:, 0:rank_dim] = total[:, 0:rank_dim].astype(BF)
    out_ref[:, rank_dim : rank_dim + LANES] = high
    out_ref[:, rank_dim + LANES :] = (maps - high.astype(F32)).astype(BF)


def sum_parts(parts):
    rows, width = parts[0].shape
    return pl.pallas_call(
        sum_kernel,
        in_specs=in_vmem(len(parts)),
        out_specs=in_vmem(1)[0],
        out_shape=jax.ShapeDtypeStruct((rows, width), BF),
        compiler_params=params(8),
    )(*parts)


def scan_kernel(states, count, plan_ref, *refs):
    pieces = refs[0:8]
    mixed_ref, weight_ref, bias_ref, skip_ref, tail_ref, decays, start_ref = refs[8:15]
    out_ref, back_ref = refs[15:17]
    low_dt, maps, turned, map_smem, rates, drives, sums, begun, ready, sem, sems = refs[17:]
    tokens, channels = mixed_ref.shape
    groups = channels // LANES
    share = tokens // 8
    rank_dim = weight_ref.shape[0]
    rank = plan_ref[3 * count]
    conv_rows = 3 * groups
    state_rows = states * groups

    def receive(r):
        return pltpu.make_async_copy(
            start_ref.at[plan_ref[r], pl.ds(conv_rows, state_rows)], begun.at[r], sems.at[r, 0]
        )

    def send_tail(r):
        owner = plan_ref[r]
        return pltpu.make_async_copy(
            tail_ref.at[owner], back_ref.at[owner, pl.ds(0, conv_rows)], sems.at[r, 1]
        )

    def send_state(r):
        return pltpu.make_async_copy(
            ready.at[r], back_ref.at[plan_ref[r], pl.ds(conv_rows, state_rows)], sems.at[r, 2]
        )

    for step, piece in enumerate(pieces):
        place = pl.multiple_of(lax.rem(rank + 8 - step, 8) * share, share)
        low_dt[pl.ds(place, share), :] = piece[:, 0:rank_dim]
        maps[pl.ds(place, share), :] = piece[:, rank_dim : rank_dim + LANES].astype(F32) + piece[
            :, rank_dim + LANES :
        ].astype(F32)
    turned[...] = jnp.transpose(maps[...])[0 : 2 * states, :]
    copy = pltpu.make_async_copy(turned, map_smem, sem)
    copy.start()
    for r in range(count):
        receive(r).start()
    chunk = min(512, channels)
    for low in range(0, channels, chunk):
        cut = slice(low, low + chunk)
        raw = (
            jnp.dot(low_dt[...], weight_ref[:, cut], preferred_element_type=F32) + bias_ref[:, cut]
        )
        rate = jnp.maximum(raw, 0.0) + jnp.log1p(jnp.exp(-jnp.abs(raw)))
        drive = rate * mixed_ref[:, cut].astype(F32)
        for j in range(chunk // LANES):
            rows = pl.ds(low // LANES + j, tokens, stride=groups)
            rates[rows, :] = rate[:, j * LANES : (j + 1) * LANES]
            drives[rows, :] = drive[:, j * LANES : (j + 1) * LANES]
    copy.wait()

    def segment(r, begin):
        finish = begin + plan_ref[count + r]
        receive(r).wait()
        held = tuple(
            begun[r, n * groups : (n + 1) * groups, :].astype(F32) for n in range(states)
        )

        def token(t, held):
            place = pl.ds(pl.multiple_of(t * groups, groups), groups)
            rate, drive = rates[place, :], drives[place, :]
            total, later = None, []
            for n in range(states):
                decay = jnp.exp2(rate * decays[n * groups : (n + 1) * groups, :])
                value = decay * held[n] + drive * map_smem[n, t]
                term = value * map_smem[states + n, t]
                total = term if total is None else total + term
                later.append(value)
            sums[place, :] = total
            return tuple(later)

        held = lax.fori_loop(begin, finish, token, held)
        for n in range(states):
            ready[r, n * groups : (n + 1) * groups, :] = held[n].astype(BF)
        send_state(r).start()
        send_tail(r).start()
        return finish

    lax.fori_loop(0, count, segment, jnp.int32(0))
    for j in range(groups):
        cut = slice(j * LANES, (j + 1) * LANES)
        out_ref[:, cut] = (
            sums[pl.ds(j, tokens, stride=groups), :]
            + skip_ref[:, cut] * mixed_ref[:, cut].astype(F32)
        ).astype(BF)
    for r in range(count):
        send_tail(r).wait()
        send_state(r).wait()


def scan(plan, pieces, mixed, dt_weight, dt_bias, skip_gain, tails, decays, got):
    tokens, channels = mixed.shape
    groups = channels // LANES
    state_rows = decays.shape[0]
    count = (plan.shape[0] - 1) // 3
    return pl.pallas_call(
        functools.partial(scan_kernel, state_rows // groups, count),
        in_specs=in_smem(1) + in_vmem(14) + [pl.BlockSpec(memory_space=pl.ANY)],
        out_specs=in_vmem(1) + in_hbm(1),
        out_shape=[
            jax.ShapeDtypeStruct((tokens, channels), BF),
            pltpu.HBM(got.shape, BF),
        ],
        scratch_shapes=[
            VMEM((tokens, dt_weight.shape[0]), BF),
            VMEM((tokens, LANES), F32),
            VMEM((2 * state_rows // groups, tokens), F32),
            SMEM((2 * state_rows // groups, tokens), F32),
            VMEM((tokens * groups, LANES), F32),
            VMEM((tokens * groups, LANES), F32),
            VMEM((tokens * groups, LANES), F32),
            VMEM((count, state_rows, LANES), BF),
            VMEM((count, state_rows, LANES), BF),
            pltpu.SemaphoreType.DMA,
            pltpu.SemaphoreType.DMA((count, 3)),
        ],
        compiler_params=params(24),
    )(plan, *pieces, mixed, dt_weight, dt_bias, skip_gain, tails, decays, got)


def attend_kernel(count, plan_ref, q_ref, k_ref, v_ref, got_ref, out_ref, rows_q, rows_o, prefix_ref, sems):
    tokens = q_ref.shape[0]
    heads = q_ref.shape[1] // HEAD_DIM
    prefix = prefix_ref.shape[1] // 2

    def receive(r):
        return pltpu.make_async_copy(got_ref.at[plan_ref[r]], prefix_ref.at[r], sems.at[r])

    for r in range(count):
        receive(r).start()
    for h in range(heads):
        rows_q[h * tokens : (h + 1) * tokens, :] = q_ref[:, h * HEAD_DIM : (h + 1) * HEAD_DIM]
    contract = (((1,), (1,)), ((), ()))
    scale = HEAD_DIM**-0.5
    many = heads * tokens
    new_scores = lax.dot_general(
        rows_q[...], k_ref[...], contract, preferred_element_type=F32
    ) * scale
    query_of = lax.rem(lax.broadcasted_iota(I32, (many, tokens), 0), tokens)
    key_of = lax.broadcasted_iota(I32, (many, tokens), 1)
    new_scores = jnp.where(key_of <= query_of, new_scores, -1e30)
    token_of = lax.rem(lax.broadcasted_iota(I32, (many, HEAD_DIM), 0), tokens)
    place_of = lax.broadcasted_iota(I32, (many, prefix), 1)
    rows_o[...] = jnp.zeros((many, HEAD_DIM), F32)

    def request(r, begin):
        finish = begin + plan_ref[count + r]
        live = plan_ref[2 * count + r] * KVB
        receive(r).wait()
        old = lax.dot_general(
            rows_q[...], prefix_ref[r, 0:prefix, :], contract, preferred_element_type=F32
        ) * scale
        old = jnp.where(place_of < live, old, -1e30)
        new = jnp.where(key_of >= begin, new_scores, -1e30)
        highest = jnp.maximum(
            jnp.max(old, axis=1, keepdims=True), jnp.max(new, axis=1, keepdims=True)
        )
        old, new = jnp.exp(old - highest), jnp.exp(new - highest)
        total = jnp.sum(old, axis=1, keepdims=True) + jnp.sum(new, axis=1, keepdims=True)
        inverse = 1.0 / total
        result = jnp.dot(
            (old * inverse).astype(BF), prefix_ref[r, prefix:, :], preferred_element_type=F32
        ) + jnp.dot((new * inverse).astype(BF), v_ref[...], preferred_element_type=F32)
        mine = (token_of >= begin) & (token_of < finish)
        rows_o[...] = jnp.where(mine, result, rows_o[...])
        return finish

    lax.fori_loop(0, count, request, jnp.int32(0))
    for h in range(heads):
        out_ref[:, h * HEAD_DIM : (h + 1) * HEAD_DIM] = rows_o[
            h * tokens : (h + 1) * tokens, :
        ].astype(BF)


def attend(plan, queries, new_keys, new_values, got):
    tokens, width = queries.shape
    many = tokens * width // HEAD_DIM
    count = (plan.shape[0] - 1) // 3
    return pl.pallas_call(
        functools.partial(attend_kernel, count),
        grid=(1,),
        in_specs=in_smem(1) + whole(queries, new_keys, new_values) + in_hbm(1),
        out_specs=pl.BlockSpec((tokens, width), lambda i: (0, 0)),
        out_shape=jax.ShapeDtypeStruct((tokens, width), BF),
        scratch_shapes=[
            VMEM((many, HEAD_DIM), BF),
            VMEM((many, HEAD_DIM), F32),
            VMEM((count,) + got.shape[1:], BF),
            pltpu.SemaphoreType.DMA((count,)),
        ],
        compiler_params=params(),
    )(plan, *pin(queries, new_keys, new_values, got))


def write_kernel(
    asked_ref, conv_ref, store_ref, back_ref, conv_out, out_ref, source, hold, stage, tails, sems
):
    slots, states, channels = out_ref.shape
    groups = channels // LANES
    rows = states * groups
    conv_rows = 3 * groups
    for s in range(slots):
        source[s] = -1
    for row in range(asked_ref.shape[0]):
        slot = asked_ref[row, 0]

        @pl.when(slot >= 0)
        def _():
            source[slot] = row

    def kept(s):
        return pltpu.make_async_copy(store_ref.at[s], stage.at[s], sems.at[slots + s])

    def changed(s):
        return pltpu.make_async_copy(stage.at[s], out_ref.at[s], sems.at[s])

    for s in range(slots):

        @pl.when(source[s] < 0)
        def _():
            kept(s).start()
            tails[s * conv_rows : (s + 1) * conv_rows, :] = jnp.zeros((conv_rows, LANES), F32)
    landed = jnp.zeros((slots, LANES), I32)
    slot_of = lax.broadcasted_iota(I32, (slots, LANES), 0)
    for s in range(slots):
        row = source[s]
        landed = jnp.where(slot_of == s, row + 1, landed)

        @pl.when(row >= 0)
        def _():
            hold[s % 2] = back_ref[row, conv_rows:, :].astype(F32)
            for low in range(0, states, 8):
                for j in range(groups):
                    stage[s, low : low + 8, j * LANES : (j + 1) * LANES] = hold[
                        s % 2, pl.ds(low * groups + j, 8, stride=groups), :
                    ]
            changed(s).start()
            tails[s * conv_rows : (s + 1) * conv_rows, :] = back_ref[row, 0:conv_rows, :].astype(F32)

    for i in range(3):
        for j in range(groups):
            cut = slice(j * LANES, (j + 1) * LANES)
            fresh = tails[pl.ds(i * groups + j, slots, stride=3 * groups), :]
            conv_out[i, :, cut] = jnp.where(
                landed > 0, fresh, conv_ref[i, :, cut].astype(F32)
            ).astype(BF)
    for s in range(slots):

        @pl.when(source[s] < 0)
        def _():
            kept(s).wait()
            changed(s).start()

    for s in range(slots):
        changed(s).wait()


def write_store(asked, store_state, conv_rows, back):
    slots, states, channels = store_state.shape
    groups = channels // LANES
    return pl.pallas_call(
        write_kernel,
        grid=(1,),
        in_specs=in_smem(1) + whole(conv_rows) + in_hbm(1) + in_vmem(1),
        out_specs=whole(conv_rows) + in_hbm(1),
        out_shape=[
            jax.ShapeDtypeStruct(conv_rows.shape, BF),
            jax.ShapeDtypeStruct((slots, states, channels), F32),
        ],
        scratch_shapes=[
            SMEM((slots,), I32),
            VMEM((2, states * groups, LANES), F32),
            VMEM((slots, states, channels), F32),
            VMEM((slots * 3 * groups, LANES), F32),
            pltpu.SemaphoreType.DMA((2 * slots,)),
        ],
        compiler_params=params(24),
    )(asked, *pin(conv_rows, store_state), back)


def exchange(blocks, axis):
    return lax.all_to_all(blocks, axis, split_axis=0, concat_axis=0, tiled=True)


def choose_matrix(lengths, owners, tokens, owner_count, width):
    ends = jnp.cumsum(lengths, dtype=I32)
    starts = ends - lengths
    places = jnp.arange(tokens, dtype=I32)
    member = (places[:, None] >= starts[None, :]) & (places[:, None] < ends[None, :])
    offset = places - jnp.sum(jnp.where(member, starts[None, :], 0), axis=1, dtype=I32)
    owner = jnp.sum(jnp.where(member, owners[None, :], 0), axis=1, dtype=I32)
    lags = jnp.arange(1, 4, dtype=I32)[:, None]
    lagged = jnp.where(
        offset[None, :] >= lags,
        places[None, :] - lags,
        tokens + owner[None, :] * 3 + 3 + offset[None, :] - lags,
    )
    owner_ids = jnp.arange(owner_count, dtype=I32)
    served = owner_ids[:, None] == owners[None, :]
    ends_of = jnp.sum(jnp.where(served, ends[None, :], 0), axis=1, dtype=I32)[:, None]
    length_of = jnp.sum(jnp.where(served, lengths[None, :], 0), axis=1, dtype=I32)[:, None]
    rows = jnp.arange(3, dtype=I32)[None, :]
    tails = jnp.where(
        length_of + rows >= 3, ends_of - 3 + rows, tokens + owner_ids[:, None] * 3 + length_of + rows
    )
    tails = jnp.where(length_of > 0, tails, width)
    column = jnp.concatenate([lagged.reshape(-1), tails.reshape(-1)])
    return (column[:, None] == jnp.arange(width, dtype=I32)[None, :]).astype(BF)


def shards(
    x_in,
    conv_weight,
    dt_in_weight,
    bc_weight,
    dt_weight,
    dt_bias,
    decay_rates,
    skip_gain,
    queries,
    new_keys,
    new_values,
    store_state,
    store_conv,
    store_keys,
    store_values,
    hit_entry,
    hit_blocks,
    seg_lengths,
):
    owner_count = lax.axis_size("cache")
    tp_count = lax.axis_size("tp")
    rank = lax.axis_index("tp").astype(I32)[None]
    slot_count, states, channels = store_state.shape
    groups = channels // LANES
    tokens = x_in.shape[0]
    lengths = seg_lengths[0]
    table, plan = ask(hit_entry, hit_blocks, seg_lengths, rank, slot_count, owner_count)
    asked = exchange(table, "cache")[:, 0, :]

    conv_store = store_conv.transpose(1, 0, 2)
    tiles = entry_tiles(conv_store, store_state)
    sent = pick_tiles(asked, tiles, 3 * groups)
    width = tokens + -(-3 * owner_count // LANES) * LANES
    choose = choose_matrix(lengths, hit_entry // slot_count, tokens, owner_count, width)
    x_rows, choose, taps, dt_in, bc_in, dt_out, bias, skip, decays = bring(
        sent, decay_rates, x_in, choose, conv_weight, dt_in_weight, bc_weight, dt_weight,
        dt_bias[None, :], skip_gain[None, :],
    )
    got = exchange(sent, "cache")
    *parts, mixed, tails = conv_project(plan, x_rows, choose, taps, dt_in, bc_in, got)

    def turned(step, value):
        return lax.ppermute(value, "tp", [(k, (k + step) % tp_count) for k in range(tp_count)])

    parts = [parts[0]] + [turned(step, parts[step]) for step in range(1, tp_count)]
    summed = sum_parts(parts)
    pieces = [summed] + [turned(step, summed) for step in range(1, tp_count)]
    got_prefix = exchange(pick(asked, bias, *pin(store_keys, store_values)), "cache")

    mixer_out, back = scan(plan, pieces, mixed, dt_out, bias, skip, tails, decays, got)
    back = exchange(back, "cache")
    attn_out = attend(plan, queries, new_keys, new_values, got_prefix)
    conv_rows, new_state = write_store(asked, store_state, conv_store, back)
    return (mixer_out, attn_out, new_state, conv_rows.transpose(1, 0, 2))


def solution(mesh):
    placed = (
        P("cache", "tp"),
        P(None, "tp"),
        P("tp", None),
        P(None, "tp"),
        P(None, "tp"),
        P("tp"),
        P(None, "tp"),
        P("tp"),
        P("cache", "tp"),
        P("cache", "tp"),
        P("cache", "tp"),
        P("cache", None, "tp"),
        P("cache", None, "tp"),
        P("cache", None, "tp"),
        P("cache", None, "tp"),
        P("cache"),
        P("cache"),
        P("cache", None),
    )
    return jax.shard_map(
        shards,
        mesh=mesh,
        in_specs=placed,
        out_specs=(
            P("cache", "tp"),
            P("cache", "tp"),
            P("cache", None, "tp"),
            P("cache", None, "tp"),
        ),
        check_vma=False,
    )
```
